32 devices in a mesh: wide: 16 (over z, y, core), narrow: 2 (over x).
Axes of the slice: x: 2, y: 2, z: 4, core: 2. Of those that a mesh axis runs over, the one named last changes fastest.
Arguments:
- target: bfloat16 [65536, 512], P(('wide', 'narrow')), may hold values from -6 to 6
- memory: bfloat16 [65536, 512], P(('wide', 'narrow')), may hold values from -6 to 6
- out_grad: bfloat16 [65536, 512], P(('wide', 'narrow')), may hold values from -6 to 6
- target_segments: int32 [64, 1024], P(('wide', 'narrow')), may hold values from 0 to 24, as said below
- source_segments: int32 [64, 1024], P(('wide', 'narrow')), may hold values from 0 to 24, as said below
- target_positions: int32 [64, 1024], P(('wide', 'narrow')), may hold values from 0 to 999, as said below
- self_qkv: bfloat16 [512, 1536], P(('wide', 'narrow')), may hold values from -0.25 to 0.25
- self_out: bfloat16 [512, 512], P(('wide', 'narrow')), may hold values from -1 to 1
- cross_query: bfloat16 [512, 512], P(('wide', 'narrow')), may hold values from -0.25 to 0.25
- cross_kv: bfloat16 [512, 1024], P(('wide', 'narrow')), may hold values from -0.25 to 0.25
- cross_out: bfloat16 [512, 512], P(('wide', 'narrow')), may hold values from -1 to 1
- ffn_in: bfloat16 [512, 2048], P(('wide', 'narrow')), may hold values from -0.25 to 0.25
- ffn_out: bfloat16 [2048, 512], P(('wide', 'narrow')), may hold values from -0.125 to 0.125
- self_bias: bfloat16 [1536], P(('wide', 'narrow')), may hold values from -3 to 3
- self_gain: bfloat16 [512], P(('wide', 'narrow')), may hold values from 0.5 to 1.5
- self_shift: bfloat16 [512], P(('wide', 'narrow')), may hold values from -2 to 2
- cross_bias: bfloat16 [1536], P(('wide', 'narrow')), may hold values from -3 to 3
- cross_gain: bfloat16 [512], P(('wide', 'narrow')), may hold values from 0.5 to 1.5
- cross_shift: bfloat16 [512], P(('wide', 'narrow')), may hold values from -2 to 2
- ffn_in_bias: bfloat16 [2048], P(('wide', 'narrow')), may hold values from -3 to 3
- ffn_out_bias: bfloat16 [512], P(('wide', 'narrow')), may hold values from -2 to 2
- ffn_gain: bfloat16 [512], P(('wide', 'narrow')), may hold values from 0.5 to 1.5
- ffn_shift: bfloat16 [512], P(('wide', 'narrow')), may hold values from -2 to 2
Outputs:
- output: bfloat16 [65536, 512], P(('wide', 'narrow'))
- target_grad: bfloat16 [65536, 512], P(('wide', 'narrow'))
- memory_grad: bfloat16 [65536, 512], P(('wide', 'narrow'))
- self_qkv_grad: float32 [512, 1536], P(('wide', 'narrow'))
- self_out_grad: float32 [512, 512], P(('wide', 'narrow'))
- cross_query_grad: float32 [512, 512], P(('wide', 'narrow'))
- cross_kv_grad: float32 [512, 1024], P(('wide', 'narrow'))
- cross_out_grad: float32 [512, 512], P(('wide', 'narrow'))
- ffn_in_grad: float32 [512, 2048], P(('wide', 'narrow'))
- ffn_out_grad: float32 [2048, 512], P(('wide', 'narrow'))
- self_bias_grad: float32 [1536], P(('wide', 'narrow'))
- self_gain_grad: float32 [512], P(('wide', 'narrow'))
- self_shift_grad: float32 [512], P(('wide', 'narrow'))
- cross_bias_grad: float32 [1536], P(('wide', 'narrow'))
- cross_gain_grad: float32 [512], P(('wide', 'narrow'))
- cross_shift_grad: float32 [512], P(('wide', 'narrow'))
- ffn_in_bias_grad: float32 [2048], P(('wide', 'narrow'))
- ffn_out_bias_grad: float32 [512], P(('wide', 'narrow'))
- ffn_gain_grad: float32 [512], P(('wide', 'narrow'))
- ffn_shift_grad: float32 [512], P(('wide', 'narrow'))
The draws below stay inside these ranges and needn't reach their ends.
Inputs may be any that keep to these rules, and one draw needn't show every extreme that they name: `target_segments`: each row holds 24 target sentences numbered 1 to 24 in order, each a run of consecutive tokens, then padding numbered 0 of 1 to 64 tokens at its end. In one row, drawn from the seed, sentences 1 to 23 have one token each and the padding is one token. `source_segments`: each row holds 24 source sentences numbered 1 to 24 in order, each a run of consecutive tokens, then padding numbered 0 of 1 to 64 tokens at its end. `target_positions`: A token's offset from the first token of its sentence (of its padding for padding tokens).
All inputs are finite; a program needn't handle non-finite values.
Results may differ from the reference program's by a relative error of at most 0.028.
Values may be sent and summed in bfloat16 or wider, within the bound.
No kernel may reach another device: no remote copies, remote signals or barrier semaphores. Data moves between devices by JAX's collectives and lax.ppermute only.
A program may use at most 256 MiB of HBM per device.

```python
import math
import jax
import jax.numpy as jnp
from jax import lax

D = 512
HEADS = 8
FF = 2048
SEQ = 1024
PAIRS = 24
ROWS = 64
TOKENS = 65536


def row_layout(key, special):
    spare = SEQ // 16
    cut_key, pad_key = jax.random.split(key)
    order = jax.random.permutation(cut_key, SEQ - spare - 1) + 1
    random_cuts = order[:PAIRS - 1].astype(jnp.int32)
    tight_cuts = jnp.arange(1, PAIRS, dtype=jnp.int32)
    cuts = jnp.where(special, tight_cuts, random_cuts).astype(jnp.int32)
    used = jnp.where(special, SEQ - 1, SEQ - jax.random.randint(pad_key, (), 1, spare + 1)).astype(jnp.int32)
    place = jnp.arange(SEQ, dtype=jnp.int32)
    after = place[:, None] >= cuts[None, :]
    segment = 1 + jnp.sum(after.astype(jnp.int32), axis=1)
    start = jnp.max(jnp.where(after, cuts[None, :], 0), axis=1)
    padded = place >= used
    segment = jnp.where(padded, 0, segment).astype(jnp.int32)
    position = jnp.where(padded, place - used, place - start).astype(jnp.int32)
    return (segment, position)


def target_layout(key):
    key = jax.random.fold_in(key, 11)
    pick_key, rows_key = jax.random.split(key)
    chosen = jax.random.randint(pick_key, (), 0, ROWS)
    special = jnp.arange(ROWS, dtype=jnp.int32) == chosen
    row_keys = jax.random.split(rows_key, ROWS)
    return jax.vmap(row_layout)(row_keys, special)


def draw_target_segments(key, part):
    segment, position = target_layout(key)
    return segment


def draw_target_positions(key, part):
    segment, position = target_layout(key)
    return position


def draw_source_segments(key, part):
    key = jax.random.fold_in(key, 29)
    row_keys = jax.random.split(key, ROWS)
    special = jnp.zeros((ROWS,), dtype=bool)
    segment, position = jax.vmap(row_layout)(row_keys, special)
    return segment


def spiked(entries, key, source, target, shards_of, factor):
    def block_of(axis_at):
        return (jnp.arange(entries.shape[axis_at]) // (entries.shape[axis_at] // shards_of)).reshape((-1,) + (1,) * (entries.ndim - 1 - axis_at))

    near = jax.random.permutation(key, shards_of)[block_of(target)]
    other_side = (block_of(target) + shards_of // 2) % shards_of
    return jnp.where((block_of(source) == near) | (block_of(source) == other_side), factor * entries, entries)


def shard_levels(key, extent, cuts, smallest, top_value):
    factor_of = 1.0
    for dim, shards_of in cuts:
        draws = jax.random.uniform(jax.random.fold_in(jax.random.fold_in(key, 6), dim), (shards_of,), jnp.float32, smallest / len(cuts), top_value / len(cuts))
        factor_of = factor_of * jnp.repeat(jnp.exp(draws), extent[dim] // shards_of).reshape((-1,) + (1,) * (len(extent) - 1 - dim))
    return factor_of


def scatter_about(rng, dims, width, bound, cuts=(), kind=jnp.bfloat16):
    factor_of = shard_levels(rng, dims, cuts, -0.22, 0.18) if cuts else 1.0
    array = jax.random.normal(rng, dims, jnp.float32) * width * factor_of
    return jnp.minimum(jnp.maximum(array, -bound), bound).astype(kind)


def gaussian_with(stream_key, shape, scale, reach, shards, heavy, kind=jnp.bfloat16):
    array = scale * jax.random.normal(stream_key, shape, jnp.float32)
    if shards:
        array = array * shard_levels(stream_key, shape, shards, -0.22, 0.18)
    return jnp.clip(spiked(array, jax.random.fold_in(stream_key, 3), *heavy), -reach, reach).astype(kind)


def setup_inputs(seed: int = 0) -> dict:
    streams_of = jax.random.split(jax.random.key(seed), 24)
    return {
        "target": scatter_about(streams_of[0], (TOKENS, D), 1.0, 6.0, ((0, 32),)),
        "memory": scatter_about(streams_of[1], (TOKENS, D), 1.0, 6.0, ((0, 32),)),
        "out_grad": gaussian_with(streams_of[2], (TOKENS, D), 1.0, 6.0, ((0, 32),), (0, 1, 32, 2.75)),
        "target_segments": draw_target_segments(jax.random.fold_in(streams_of[23], 71), 0),
        "source_segments": draw_source_segments(jax.random.fold_in(streams_of[23], 71), 0),
        "target_positions": draw_target_positions(jax.random.fold_in(streams_of[23], 71), 0),
        "self_qkv": scatter_about(streams_of[6], (D, 3 * D), D ** -0.5, 0.25, ((0, 32),)),
        "self_out": scatter_about(streams_of[7], (D, D), (D // 16) ** -0.5, 1.0, ((0, 32),)),
        "cross_query": scatter_about(streams_of[8], (D, D), D ** -0.5, 0.25, ((0, 32),)),
        "cross_kv": scatter_about(streams_of[9], (D, 2 * D), D ** -0.5, 0.25, ((0, 32),)),
        "cross_out": scatter_about(streams_of[10], (D, D), (D // 16) ** -0.5, 1.0, ((0, 32),)),
        "ffn_in": scatter_about(streams_of[11], (D, FF), D ** -0.5, 0.25, ((0, 32),)),
        "ffn_out": scatter_about(streams_of[12], (FF, D), FF ** -0.5, 0.125, ((0, 32),)),
        "self_bias": scatter_about(streams_of[13], (3 * D,), 0.5, 3.0, ((0, 32),)),
        "self_gain": jnp.clip(1.0 + 0.1 * jax.random.normal(streams_of[14], (D,), jnp.float32), 0.5, 1.5).astype(jnp.bfloat16),
        "self_shift": scatter_about(streams_of[15], (D,), 0.3, 2.0, ((0, 32),)),
        "cross_bias": scatter_about(streams_of[16], (3 * D,), 0.5, 3.0, ((0, 32),)),
        "cross_gain": jnp.clip(1.0 + 0.1 * jax.random.normal(streams_of[17], (D,), jnp.float32), 0.5, 1.5).astype(jnp.bfloat16),
        "cross_shift": scatter_about(streams_of[18], (D,), 0.3, 2.0, ((0, 32),)),
        "ffn_in_bias": scatter_about(streams_of[19], (FF,), 0.5, 3.0, ((0, 32),)),
        "ffn_out_bias": scatter_about(streams_of[20], (D,), 0.3, 2.0, ((0, 32),)),
        "ffn_gain": jnp.clip(1.0 + 0.1 * jax.random.normal(streams_of[21], (D,), jnp.float32), 0.5, 1.5).astype(jnp.bfloat16),
        "ffn_shift": scatter_about(streams_of[22], (D,), 0.3, 2.0, ((0, 32),)),
    }


EPSILON = 1e-05
MASKED = -1e+30

@jax.custom_vjp
def low(v):
    return lax.optimization_barrier(v.astype(jnp.bfloat16)).astype(jnp.float32)

@jax.custom_vjp
def low_back(v):
    return v

def low_keep(v):
    return (low(v), None)

def low_pass(kept, grad):
    return (grad,)

def back_keep(v):
    return (v, None)

def back_low(kept, grad):
    return (low(grad),)
low.defvjp(low_keep, low_pass)
low_back.defvjp(back_keep, back_low)

def round_both(values):
    return low(low_back(values))

def product(left_side, right_side):
    return jnp.dot(left_side, right_side, precision=lax.Precision.HIGHEST)

def layer_norm(hidden, gain, shift):
    average = lax.optimization_barrier(jnp.mean(hidden, axis=-1, keepdims=True))
    centred = hidden - average
    variance = lax.optimization_barrier(jnp.mean(centred * centred, axis=-1, keepdims=True))
    return centred * lax.rsqrt(variance + EPSILON) * gain + shift

def softmax_mix(queries, key_rows, value_rows, allowed):
    scaling = 1.0 / math.sqrt(queries.shape[-1])
    scores = low_back(jnp.einsum('qhe,khe->hqk', queries, key_rows, precision=lax.Precision.HIGHEST) * scaling)
    scores = jnp.where(allowed[None], scores, MASKED)
    highest = lax.optimization_barrier(jnp.max(scores, axis=-1, keepdims=True))
    weights = jnp.exp(scores - highest)
    prob_rows = low(weights / lax.optimization_barrier(jnp.sum(weights, axis=-1, keepdims=True)))
    return jnp.einsum('hqk,khe->qhe', prob_rows, value_rows, precision=lax.Precision.HIGHEST)

def self_row(pieces):
    queries, key_rows, value_rows, segment, position = pieces
    allowed = (segment[:, None] == segment[None, :]) & (position[None, :] <= position[:, None])
    return softmax_mix(queries, key_rows, value_rows, allowed)

def cross_row(pieces):
    queries, key_rows, value_rows, segment, source = pieces
    allowed = segment[:, None] == source[None, :]
    return softmax_mix(queries, key_rows, value_rows, allowed)

def forward(target, memory, params, target_segments, source_segments, target_positions):
    self_qkv, self_out, cross_query, cross_kv, cross_out, ffn_in, ffn_out, self_bias, self_gain, self_shift, cross_bias, cross_gain, cross_shift, ffn_in_bias, ffn_out_bias, ffn_gain, ffn_shift = params
    model_width = target.shape[1]
    row_count = target_segments.shape[0]
    head_size = model_width // HEADS
    zeros_row = jnp.zeros((model_width,), jnp.float32)

    def split_heads(flat_values):
        return flat_values.reshape(row_count, -1, HEADS, head_size)
    joined_bias = jnp.concatenate([self_bias[:model_width], zeros_row, self_bias[model_width:2 * model_width]])
    projected = round_both(product(target, self_qkv) + joined_bias)
    self_mix = lax.map(jax.checkpoint(self_row), (split_heads(projected[:, :model_width]), split_heads(projected[:, model_width:2 * model_width]), split_heads(projected[:, 2 * model_width:]), target_segments, target_positions))
    self_mix = round_both(self_mix.reshape(-1, model_width))
    branch_one = low_back(product(self_mix, self_out) + self_bias[2 * model_width:])
    first_out = layer_norm(target + branch_one, self_gain, self_shift)
    first_low = low(first_out)
    cross_queries = round_both(product(first_low, cross_query) + cross_bias[:model_width])
    cross_pairs = round_both(product(memory, cross_kv) + jnp.concatenate([zeros_row, cross_bias[model_width:2 * model_width]]))
    cross_mix = lax.map(jax.checkpoint(cross_row), (split_heads(cross_queries), split_heads(cross_pairs[:, :model_width]), split_heads(cross_pairs[:, model_width:]), target_segments, source_segments))
    cross_mix = round_both(cross_mix.reshape(-1, model_width))
    branch_two = low_back(product(cross_mix, cross_out) + cross_bias[2 * model_width:])
    second = layer_norm(first_out + branch_two, cross_gain, cross_shift)
    second_low = low(second)
    pre_act = low_back(product(second_low, ffn_in) + ffn_in_bias)
    activated = low(jax.nn.silu(pre_act))
    branch_three = low_back(product(activated, ffn_out) + ffn_out_bias)
    return layer_norm(second + branch_three, ffn_gain, ffn_shift)

def reference(target, memory, out_grad, target_segments, source_segments, target_positions, self_qkv, self_out, cross_query, cross_kv, cross_out, ffn_in, ffn_out, self_bias, self_gain, self_shift, cross_bias, cross_gain, cross_shift, ffn_in_bias, ffn_out_bias, ffn_gain, ffn_shift):
    params = tuple((member.astype(jnp.float32) for member in (self_qkv, self_out, cross_query, cross_kv, cross_out, ffn_in, ffn_out, self_bias, self_gain, self_shift, cross_bias, cross_gain, cross_shift, ffn_in_bias, ffn_out_bias, ffn_gain, ffn_shift)))
    rows_each = 4
    steps_count = target_segments.shape[0] // rows_each
    model_width = target.shape[1]

    def tokens_view(values):
        return values.reshape(steps_count, rows_each * SEQ, model_width)

    def rows_view(values):
        return values.reshape(steps_count, rows_each, SEQ)

    def step(totals, pieces):
        target_rows, memory_rows, grad_rows, segment_rows, source_rows, position_rows = pieces

        def run(target_in, memory_in, params_in):
            return forward(target_in, memory_in, params_in, segment_rows, source_rows, position_rows)
        result, pull = jax.vjp(run, target_rows.astype(jnp.float32), memory_rows.astype(jnp.float32), params)
        target_back, memory_back, params_back = pull(grad_rows.astype(jnp.float32))
        totals = jax.tree.map(lambda kept, added: kept + added, totals, params_back)
        return (totals, (result.astype(jnp.bfloat16), target_back.astype(jnp.bfloat16), memory_back.astype(jnp.bfloat16)))
    initial = tuple((jnp.zeros(member.shape, jnp.float32) for member in params))
    totals, (results, target_backs, memory_backs) = lax.scan(step, initial, (tokens_view(target), tokens_view(memory), tokens_view(out_grad), rows_view(target_segments), rows_view(source_segments), rows_view(target_positions)))
    flat_shape = (target.shape[0], model_width)
    return (results.reshape(flat_shape), target_backs.reshape(flat_shape), memory_backs.reshape(flat_shape), totals[0], totals[1], totals[2], totals[3], totals[4], totals[5], totals[6], totals[7], totals[8], totals[9], totals[10], totals[11], totals[12], totals[13], totals[14], totals[15], totals[16])
```

```python
import functools

import jax
import jax.numpy as jnp
from jax import lax
from jax.experimental import pallas as pl
from jax.experimental.pallas import tpu as pltpu
from jax.sharding import PartitionSpec as P

HEADS = 8
MASKED = -1e30
BLOCK = 128
WINDOW = 256
NT = (((1,), (1,)), ((), ()))
TN = (((0,), (0,)), ((), ()))
NN = (((1,), (0,)), ((), ()))


def mxu(a, b, dims):
    return lax.dot_general(a, b, dims, preferred_element_type=jnp.float32)


def lane_masks(scale):
    lane = lax.broadcasted_iota(jnp.int32, (1, 128), 1)
    low = jnp.where(lane < 64, scale, 0.0).astype(jnp.bfloat16)
    high = jnp.where(lane < 64, 0.0, scale).astype(jnp.bfloat16)
    return low, high


def stacked(pair, masks):
    return jnp.concatenate([pair * masks[0], pair * masks[1]], axis=0)


def pick(both):
    sub = lax.broadcasted_iota(jnp.int32, (128, BLOCK), 0)
    return jnp.where(sub < 64, both[:, :BLOCK], both[:, BLOCK:])


def columns_of(row):
    return jnp.transpose(jnp.broadcast_to(row, (128, row.shape[1])))


def bias_of(seg_cols, seg_row, q0, start, low, causal):
    allowed = seg_cols == seg_row
    key = lax.broadcasted_iota(jnp.int32, (WINDOW, BLOCK), 0) + start
    if causal == "diag":
        query = lax.broadcasted_iota(jnp.int32, (WINDOW, BLOCK), 1) + q0
        allowed = allowed & (key <= query)
    elif causal == "left":
        allowed = allowed & (key < low)
    else:
        allowed = allowed & (key >= low)
    return jnp.where(allowed, 0.0, MASKED)


def window(causal, info, r, qb, c, length):
    if causal:
        end = (qb + 1) * BLOCK - c * WINDOW
        return pl.multiple_of(jnp.maximum(end - WINDOW, 0), BLOCK), end
    low = info[r, qb] + c * WINDOW
    return pl.multiple_of(jnp.minimum(low, length - WINDOW), 16), low


def forward_kernel(causal, first_ref, extra_ref, q_ref, k_ref, v_ref, qseg_ref, kseg_ref,
                   out_ref, lse_ref, cols, top, total, mix):
    r = pl.program_id(0)
    length = q_ref.shape[0]
    cols[...] = columns_of(kseg_ref[0])
    masks = lane_masks(0.125)

    def block(qb, _):
        q0 = pl.multiple_of(qb * BLOCK, BLOCK)
        seg_row = qseg_ref[0, :, pl.ds(q0, BLOCK)]

        def piece(c, kind):
            start, low = window(causal, first_ref, r, qb, c, length)
            bias = bias_of(cols[pl.ds(start, WINDOW), :], seg_row, q0, start, low, kind)
            bias = jnp.concatenate([bias, bias], axis=1)
            for p in range(4):
                lanes = slice(128 * p, 128 * p + 128)
                qs = stacked(q_ref[pl.ds(q0, BLOCK), lanes], masks)
                scores = mxu(k_ref[pl.ds(start, WINDOW), lanes], qs, NT) + bias
                yield p, scores, v_ref[pl.ds(start, WINDOW), lanes]

        for p, scores, values in piece(0, "diag" if causal else "from"):
            high = jnp.max(scores, axis=0, keepdims=True)
            weights = jnp.exp(scores - high)
            top[p] = high
            total[p] = jnp.sum(weights, axis=0, keepdims=True)
            mix[p] = pick(mxu(values, weights.astype(jnp.bfloat16), TN))

        def more(c, _):
            for p, scores, values in piece(c + 1, "left" if causal else "from"):
                old = top[p]
                high = jnp.maximum(old, jnp.max(scores, axis=0, keepdims=True))
                weights = jnp.exp(scores - high)
                fade = jnp.exp(old - high)
                top[p] = high
                total[p] = total[p] * fade + jnp.sum(weights, axis=0, keepdims=True)
                both = pick(jnp.broadcast_to(fade, (128, 2 * BLOCK)))
                mix[p] = mix[p] * both + pick(mxu(values, weights.astype(jnp.bfloat16), TN))
            return 0

        lax.fori_loop(0, extra_ref[r, qb], more, 0)
        for p in range(4):
            sums = total[p]
            inverse = pick(jnp.broadcast_to(1.0 / sums, (128, 2 * BLOCK)))
            out_ref[pl.ds(q0, BLOCK), 128 * p:128 * p + 128] = jnp.transpose(mix[p] * inverse).astype(jnp.bfloat16)
            lse = top[p] + jnp.log(sums)
            lse_ref[0, 2 * p:2 * p + 1, pl.ds(q0, BLOCK)] = lse[:, :BLOCK]
            lse_ref[0, 2 * p + 1:2 * p + 2, pl.ds(q0, BLOCK)] = lse[:, BLOCK:]
        return 0

    lax.fori_loop(0, length // BLOCK, block, 0)


def smem():
    return pl.BlockSpec(memory_space=pltpu.SMEM)


def attend_forward(first, extra, queries, keys, values, qseg, kseg, causal):
    rows, length = qseg.shape
    spec = lambda col: pl.BlockSpec((length, 512), lambda r, col=col: (r, col))
    seg = pl.BlockSpec((1, 1, length), lambda r: (r, 0, 0))
    return pl.pallas_call(
        functools.partial(forward_kernel, causal),
        grid=(rows,),
        in_specs=[smem(), smem(), spec(queries[1]), spec(keys[1]), spec(values[1]), seg, seg],
        out_specs=[spec(0), pl.BlockSpec((1, 8, length), lambda r: (r, 0, 0))],
        out_shape=[jax.ShapeDtypeStruct((rows * length, 512), jnp.bfloat16),
                   jax.ShapeDtypeStruct((rows, 8, length), jnp.float32)],
        scratch_shapes=[pltpu.VMEM((length, 128), jnp.float32),
                        pltpu.VMEM((4, 1, 2 * BLOCK), jnp.float32),
                        pltpu.VMEM((4, 1, 2 * BLOCK), jnp.float32),
                        pltpu.VMEM((4, 128, BLOCK), jnp.float32)],
        compiler_params=pltpu.CompilerParams(vmem_limit_bytes=40 << 20),
        cost_estimate=pl.CostEstimate(flops=2 * 10**9, bytes_accessed=10 << 20, transcendentals=0),
        name="attend_self" if causal else "attend_cross",
    )(first, extra, queries[0], keys[0], values[0], qseg[:, None, :].astype(jnp.float32), kseg[:, None, :].astype(jnp.float32))


def backward_kernel(causal, first_ref, extra_ref, q_ref, k_ref, v_ref, mix_ref, grad_ref, lse_ref, qseg_ref, kseg_ref,
                    dq_ref, dk_ref, dv_ref, cols, dk, dv, dq):
    r = pl.program_id(0)
    length = q_ref.shape[0]
    cols[...] = columns_of(kseg_ref[0])
    dk[...] = jnp.zeros_like(dk)
    dv[...] = jnp.zeros_like(dv)
    masks = lane_masks(0.125)
    ones = lane_masks(1.0)
    pair_rows = jnp.concatenate([ones[0], ones[1], jnp.zeros((14, 128), jnp.bfloat16)], axis=0)

    def block(qb, _):
        q0 = pl.multiple_of(qb * BLOCK, BLOCK)
        seg_row = qseg_ref[0, :, pl.ds(q0, BLOCK)]

        def piece(c, kind, first):
            start, low = window(causal, first_ref, r, qb, c, length)
            bias = bias_of(cols[pl.ds(start, WINDOW), :], seg_row, q0, start, low, kind)
            bias = jnp.concatenate([bias, bias], axis=1)
            for p in range(4):
                lanes = slice(128 * p, 128 * p + 128)
                qs = stacked(q_ref[pl.ds(q0, BLOCK), lanes], masks)
                grad = grad_ref[pl.ds(q0, BLOCK), lanes]
                gs = stacked(grad, ones)
                prod = grad.astype(jnp.float32) * mix_ref[pl.ds(q0, BLOCK), lanes].astype(jnp.float32)
                upper = prod.astype(jnp.bfloat16)
                lower = (prod - upper.astype(jnp.float32)).astype(jnp.bfloat16)
                delta = mxu(pair_rows, upper, NT) + mxu(pair_rows, lower, NT)
                delta = jnp.concatenate([delta[0:1], delta[1:2]], axis=1)
                lse = jnp.concatenate([lse_ref[0, 2 * p:2 * p + 1, pl.ds(q0, BLOCK)],
                                       lse_ref[0, 2 * p + 1:2 * p + 2, pl.ds(q0, BLOCK)]], axis=1)
                keys = k_ref[pl.ds(start, WINDOW), lanes]
                scores = mxu(keys, qs, NT) + bias
                probs = jnp.exp(scores - lse)
                dprobs = mxu(v_ref[pl.ds(start, WINDOW), lanes], gs, NT)
                dscores = (probs * (dprobs - delta)).astype(jnp.bfloat16)
                dv[pl.ds(start, WINDOW), lanes] += mxu(probs.astype(jnp.bfloat16), gs, NN)
                dk[pl.ds(start, WINDOW), lanes] += mxu(dscores, qs, NN)
                part = pick(mxu(keys, dscores, TN))
                if first:
                    dq[p] = part
                else:
                    dq[p] += part

        piece(0, "diag" if causal else "from", True)

        def more(c, _):
            piece(c + 1, "left" if causal else "from", False)
            return 0

        lax.fori_loop(0, extra_ref[r, qb], more, 0)
        for p in range(4):
            dq_ref[pl.ds(q0, BLOCK), 128 * p:128 * p + 128] = (jnp.transpose(dq[p]) * 0.125).astype(jnp.bfloat16)
        return 0

    lax.fori_loop(0, length // BLOCK, block, 0)
    dk_ref[...] = dk[...].astype(jnp.bfloat16)
    dv_ref[...] = dv[...].astype(jnp.bfloat16)


def attend_backward(first, extra, queries, keys, values, mix, grad, lse, qseg, kseg, causal):
    rows, length = qseg.shape
    spec = lambda col: pl.BlockSpec((length, 512), lambda r, col=col: (r, col))
    seg = pl.BlockSpec((1, 1, length), lambda r: (r, 0, 0))
    return pl.pallas_call(
        functools.partial(backward_kernel, causal),
        grid=(rows,),
        in_specs=[smem(), smem(), spec(queries[1]), spec(keys[1]), spec(values[1]), spec(0), spec(0),
                  pl.BlockSpec((1, 8, length), lambda r: (r, 0, 0)), seg, seg],
        out_specs=[spec(0)] * 3,
        out_shape=[jax.ShapeDtypeStruct((rows * length, 512), jnp.bfloat16)] * 3,
        scratch_shapes=[pltpu.VMEM((length, 128), jnp.float32),
                        pltpu.VMEM((length, 512), jnp.float32),
                        pltpu.VMEM((length, 512), jnp.float32),
                        pltpu.VMEM((4, 128, BLOCK), jnp.float32)],
        compiler_params=pltpu.CompilerParams(vmem_limit_bytes=48 << 20),
        cost_estimate=pl.CostEstimate(flops=6 * 10**9, bytes_accessed=16 << 20, transcendentals=0),
        name="back_self" if causal else "back_cross",
    )(first, extra, queries[0], keys[0], values[0], mix, grad, lse,
      qseg[:, None, :].astype(jnp.float32), kseg[:, None, :].astype(jnp.float32))


def plan_self(seg, positions):
    rows, length = seg.shape
    starts = jnp.arange(0, length, BLOCK, dtype=jnp.int32)
    begin = starts[None, :] - positions[:, ::BLOCK]
    left = jnp.maximum(starts[None, :] + BLOCK - WINDOW - begin, 0)
    return jnp.zeros_like(begin), (left + WINDOW - 1) // WINDOW


def plan_cross(tseg, sseg):
    last = jnp.int32(1 << 20)
    tkey = jnp.where(tseg == 0, last, tseg)
    skey = jnp.where(sseg == 0, last, sseg)
    low = jnp.sum(skey[:, None, :] < tkey[:, ::BLOCK, None], axis=2, dtype=jnp.int32)
    high = jnp.sum(skey[:, None, :] <= tkey[:, BLOCK - 1::BLOCK, None], axis=2, dtype=jnp.int32)
    first = (low // 16) * 16
    return first, jnp.maximum((high - first + WINDOW - 1) // WINDOW - 1, 0)


AXES = ("wide", "narrow")


class Net:
    def __init__(self):
        self.wide = lax.axis_size("wide")
        self.narrow = lax.axis_size("narrow")
        self.count = self.wide * self.narrow
        self.wide_bits = self.wide.bit_length() - 1
        self.narrow_bits = self.narrow.bit_length() - 1
        self.bits = self.wide_bits + self.narrow_bits
        self.me = lax.axis_index("wide") * self.narrow + lax.axis_index("narrow")

    def orders(self):
        n = self.narrow_bits
        inner = list(range(n))
        core = [n] if self.wide_bits else []
        second = [n + 1] if self.wide_bits > 1 else []
        far = list(range(self.bits - 1, n + 1, -1))
        return far + inner + second + core, far + second + inner + core

    def exchange(self, x, bit):
        if bit < self.narrow_bits:
            return lax.ppermute(x, "narrow", [(i, i ^ (1 << bit)) for i in range(self.narrow)])
        bit -= self.narrow_bits
        return lax.ppermute(x, "wide", [(i, i ^ (1 << bit)) for i in range(self.wide)])

    def gather(self, x, order):
        late = 2 if len(order) >= 2 else 0
        for bit in order[:len(order) - late]:
            x = jnp.concatenate([x, self.exchange(x, bit)], axis=0)
        pieces = [x]
        for bit in order[len(order) - late:]:
            pieces = pieces + [self.exchange(piece, bit) for piece in pieces]
        return pieces

    def masks(self, order):
        return [sum(((r >> s) & 1) << bit for s, bit in enumerate(order)) for r in range(self.count)]

    def reduce(self, keep, send, order):
        for s, bit in enumerate(order):
            got = self.exchange(send, bit)
            half = keep.shape[0] // 2
            if s + 1 == len(order):
                return keep.astype(jnp.float32) + got.astype(jnp.float32)
            send = (keep[half:].astype(jnp.float32) + got[half:].astype(jnp.float32)).astype(jnp.bfloat16)
            keep = (keep[:half].astype(jnp.float32) + got[:half].astype(jnp.float32)).astype(jnp.bfloat16)
        return keep


def arrange_kernel(plan, count, me_ref, *refs):
    chains, moves = plan
    n_in = sum(len(c[0]) for c in chains)
    ins, outs = refs[:n_in], refs[n_in:]
    me = me_ref[0]
    base = 0
    for c, (sizes, masks) in enumerate(chains):
        entry = 0
        for piece, size in enumerate(sizes):
            ref = ins[base + piece]
            for j in range(size):
                owner = me ^ masks[entry]
                entry += 1
                for chain, col, width, out, out_col, blocks, which in moves:
                    if chain != c:
                        continue
                    row = pl.multiple_of((owner * blocks + which) * 16, 16)
                    outs[out][pl.ds(row, 16), out_col:out_col + width] = ref[j, :, col:col + width]
        base += len(sizes)


def arrange(net, chains, moves, shapes):
    plan = ([([p.shape[0] for p in pieces], masks) for pieces, masks in chains], moves)
    pieces = [p for chain in chains for p in chain[0]]
    whole = pl.BlockSpec(memory_space=pltpu.VMEM)
    return pl.pallas_call(
        functools.partial(arrange_kernel, plan, net.count),
        in_specs=[smem()] + [whole] * len(pieces),
        out_specs=[whole] * len(shapes),
        out_shape=[jax.ShapeDtypeStruct(s, jnp.bfloat16) for s in shapes],
        compiler_params=pltpu.CompilerParams(vmem_limit_bytes=40 << 20),
        name="arrange",
    )(net.me[None].astype(jnp.int32), *pieces)


def spread_kernel(plan, me_ref, *refs):
    masks, moves, n_in = plan
    ins, outs = refs[:n_in], refs[n_in:]
    me = me_ref[0]
    for c, chain_masks in enumerate(masks):
        half = len(chain_masks) // 2
        for r, mask in enumerate(chain_masks):
            out = outs[2 * c + r // half]
            for chain, col, width, source, source_col, blocks, which in moves:
                if chain != c:
                    continue
                row = pl.multiple_of(((me ^ mask) * blocks + which) * 16, 16)
                out[r % half, :, col:col + width] = ins[source][pl.ds(row, 16), source_col:source_col + width].astype(jnp.bfloat16)


def spread(net, grads, masks, moves, widths):
    whole = pl.BlockSpec(memory_space=pltpu.VMEM)
    half = net.count // 2
    shapes = [(half, 16, w) for w in widths for _ in range(2)]
    return pl.pallas_call(
        functools.partial(spread_kernel, (masks, moves, len(grads))),
        in_specs=[smem()] + [whole] * len(grads),
        out_specs=[whole] * len(shapes),
        out_shape=[jax.ShapeDtypeStruct(s, jnp.bfloat16) for s in shapes],
        compiler_params=pltpu.CompilerParams(vmem_limit_bytes=48 << 20),
        name="spread",
    )(net.me[None].astype(jnp.int32), *grads)


SELF_MOVES = [(0, 0, 1024, 0, 0, 1, 0), (0, 1024, 128, 2, 0, 1, 0), (1, 0, 512, 0, 1024, 1, 0), (1, 512, 512, 1, 0, 1, 0)]
CROSS_MOVES = [(0, 0, 512, 0, 0, 1, 0), (0, 512, 512, 2, 0, 1, 0), (1, 0, 1024, 1, 0, 1, 0)]
FFN_MOVES = [(0, 0, 2048, 0, 0, 1, 0)] + [(1, 512 * b, 512, 1, 0, 4, b) for b in range(4)]


def fetch_all(net, big, small):
    if big[0].shape[0] % 16 or net.count < 4:
        whole = lax.all_gather((big, small), AXES, axis=0, tiled=True)
        return whole
    self_qkv, self_out, cross_query, cross_kv, cross_out, ffn_in, ffn_out = big
    line = jnp.concatenate(small)
    per_row = line.shape[0] // 16
    table = jnp.pad(line.reshape(16, per_row), ((0, 0), (0, 128 - per_row)))
    blocks = ffn_out.shape[0] // 16
    groups = [
        ((jnp.concatenate([self_qkv[:, :1024], table], axis=1), jnp.concatenate([self_qkv[:, 1024:], self_out], axis=1)),
         SELF_MOVES, [(512, 1536), (512, 512), (512, 128)]),
        ((jnp.concatenate([cross_query, cross_out], axis=1), cross_kv),
         CROSS_MOVES, [(512, 512), (512, 1024), (512, 512)]),
        ((ffn_in, jnp.concatenate([ffn_out[16 * b:16 * b + 16] for b in range(blocks)], axis=1)),
         FFN_MOVES, [(512, 2048), (2048, 512)]),
    ]
    orders = net.orders()
    results = []
    for shards, moves, shapes in groups:
        chains = [(net.gather(shard[None], order), net.masks(order)) for shard, order in zip(shards, orders)]
        results.extend(arrange(net, chains, moves, shapes))
    qkv, s_out, gathered, c_query, c_kv, c_out, f_in, f_out = results
    lines = gathered[:, :per_row].reshape(net.count, 16 * per_row)
    vectors, at = [], 0
    for part in small:
        vectors.append(lines[:, at:at + part.shape[0]].reshape(-1))
        at += part.shape[0]
    return (qkv, s_out, c_query, c_kv, c_out, f_in, f_out), tuple(vectors)


def reduce_group(net, grads, moves, widths):
    if grads[0].shape[0] // net.count % 16 or net.count < 4:
        return tuple(lax.psum_scatter(g.astype(jnp.bfloat16), AXES, scatter_dimension=0, tiled=True).astype(jnp.float32) for g in grads)
    orders = [order[::-1] for order in net.orders()]
    masks = []
    for order in orders:
        n = len(order)
        masks.append([sum(((r >> (n - 1 - s)) & 1) << bit for s, bit in enumerate(order)) for r in range(net.count)])
    halves = spread(net, grads, masks, moves, widths)
    sums = [net.reduce(halves[2 * c], halves[2 * c + 1], orders[c])[0] for c in range(2)]
    results = []
    for g, grad in enumerate(grads):
        rows = grad.shape[0] // net.count
        parts = sorted((m for m in moves if m[3] == g), key=lambda m: (m[6], m[4]))
        cols = [sums[m[0]][:, m[1]:m[1] + m[2]] for m in parts]
        results.append(cols[0] if len(cols) == 1 else jnp.concatenate(cols, axis=0 if rows > 16 else 1))
    return tuple(results)


def reduce_small(net, grads):
    rows = jnp.concatenate([g.reshape(net.count, -1) for g in grads], axis=1).astype(jnp.bfloat16)
    if net.count < 4:
        total = lax.psum_scatter(rows, AXES, scatter_dimension=0, tiled=True).astype(jnp.float32)
    else:
        order = list(range(net.bits - 1, -1, -1))
        half = net.count // 2
        bit = net.me >> (net.bits - 1)
        keep = lax.dynamic_slice_in_dim(rows, bit * half, half)
        send = lax.dynamic_slice_in_dim(rows, (1 - bit) * half, half)
        for s, b in enumerate(order):
            got = net.exchange(send, b)
            total = keep.astype(jnp.float32) + got.astype(jnp.float32)
            if s + 1 < len(order):
                half //= 2
                bit = (net.me >> order[s + 1]) & 1
                low = total.astype(jnp.bfloat16)
                keep = lax.dynamic_slice_in_dim(low, bit * half, half)
                send = lax.dynamic_slice_in_dim(low, (1 - bit) * half, half)
    line, out, at = total.reshape(-1), [], 0
    for g in grads:
        size = g.shape[0] // net.count
        out.append(line[at:at + size])
        at += size
    return tuple(out)


EPSILON = 1e-05


def matmul_plain(a, b):
    return mxu(a, b, NN)


def matmul_left_t(a, b):
    return mxu(a, b, TN)


def matmul_right_t(a, b):
    return mxu(a, b, NT)


def column_sums(values):
    return jnp.sum(values, axis=0, dtype=jnp.float32)


def norm_forward(hidden, gain, shift):
    average = jnp.mean(hidden, axis=-1, keepdims=True)
    centred = hidden - average
    inverse = lax.rsqrt(jnp.mean(centred * centred, axis=-1, keepdims=True) + EPSILON)
    normed = centred * inverse
    return (normed * gain + shift, normed, inverse)


def norm_backward(grad_in, normed, inverse, gain):
    gain_grad = jnp.sum(grad_in * normed, axis=0)
    shift_grad = jnp.sum(grad_in, axis=0)
    scaled = grad_in * gain
    hidden_grad = inverse * (
        scaled
        - jnp.mean(scaled, axis=-1, keepdims=True)
        - normed * jnp.mean(scaled * normed, axis=-1, keepdims=True)
    )
    return (gain_grad, shift_grad, hidden_grad)


def per_device(
    target, memory, out_grad, target_segments, source_segments, target_positions,
    self_qkv, self_out, cross_query, cross_kv, cross_out, ffn_in, ffn_out,
    self_bias, self_gain, self_shift, cross_bias, cross_gain, cross_shift,
    ffn_in_bias, ffn_out_bias, ffn_gain, ffn_shift,
):
    width = target.shape[1]
    f32 = lambda x: x.astype(jnp.float32)
    low = lambda x: x.astype(jnp.bfloat16)
    net = Net()
    zeros_row = jnp.zeros((width,), jnp.float32)
    self_first, self_extra = plan_self(target_segments, target_positions)
    cross_first, cross_extra = plan_cross(target_segments, source_segments)
    big, vectors = fetch_all(
        net,
        (self_qkv, self_out, cross_query, cross_kv, cross_out, ffn_in, ffn_out),
        (self_bias, self_gain, self_shift, cross_bias, cross_gain, cross_shift,
         ffn_in_bias, ffn_out_bias, ffn_gain, ffn_shift),
    )
    self_qkv, self_out, cross_query, cross_kv, cross_out, ffn_in, ffn_out = big
    (self_bias, self_gain, self_shift, cross_bias, cross_gain, cross_shift,
     ffn_in_bias, ffn_out_bias, ffn_gain, ffn_shift) = (f32(v) for v in vectors)

    joined_bias = jnp.concatenate([self_bias[:width], zeros_row, self_bias[width:2 * width]])
    projected = low(matmul_plain(target, self_qkv) + joined_bias)
    parts = ((projected, 0), (projected, 1), (projected, 2))
    self_mix, self_lse = attend_forward(self_first, self_extra, *parts, target_segments, target_segments, True)
    hidden_one = f32(target) + matmul_plain(self_mix, self_out) + self_bias[2 * width:]
    first_out, normed_one, inverse_one = norm_forward(hidden_one, self_gain, self_shift)
    first_low = low(first_out)
    cross_q = low(matmul_plain(first_low, cross_query) + cross_bias[:width])
    pairs = low(matmul_plain(memory, cross_kv) + jnp.concatenate([zeros_row, cross_bias[width:2 * width]]))
    cross_parts = ((cross_q, 0), (pairs, 0), (pairs, 1))
    cross_mix, cross_lse = attend_forward(cross_first, cross_extra, *cross_parts, target_segments, source_segments, False)
    hidden_two = first_out + matmul_plain(cross_mix, cross_out) + cross_bias[2 * width:]
    second_out, normed_two, inverse_two = norm_forward(hidden_two, cross_gain, cross_shift)
    second_low = low(second_out)
    pre = matmul_plain(second_low, ffn_in) + ffn_in_bias
    act = low(jax.nn.silu(pre))
    hidden_three = second_out + matmul_plain(act, ffn_out) + ffn_out_bias
    final, normed_three, inverse_three = norm_forward(hidden_three, ffn_gain, ffn_shift)
    output = low(final)

    gain_three, shift_three, back_three = norm_backward(f32(out_grad), normed_three, inverse_three, ffn_gain)
    low_three = low(back_three)
    ffn_out_grad = matmul_left_t(act, low_three)
    sig = jax.nn.sigmoid(pre)
    pre_grad = low(matmul_right_t(low_three, ffn_out) * sig * (1.0 + pre * (1.0 - sig)))
    ffn_in_grad = matmul_left_t(second_low, pre_grad)
    second_grad = back_three + matmul_right_t(pre_grad, ffn_in)
    ffn_grads = reduce_group(net, (ffn_in_grad, ffn_out_grad), FFN_MOVES, (2048, 2048))

    gain_two, shift_two, back_two = norm_backward(second_grad, normed_two, inverse_two, cross_gain)
    low_two = low(back_two)
    cross_out_grad = matmul_left_t(cross_mix, low_two)
    mix_grad = low(matmul_right_t(low_two, cross_out))
    cq, ck, cv = attend_backward(cross_first, cross_extra, *cross_parts, cross_mix, mix_grad, cross_lse,
                                 target_segments, source_segments, False)
    pair_grad = jnp.concatenate([ck, cv], axis=1)
    cross_query_grad = matmul_left_t(first_low, cq)
    cross_kv_grad = matmul_left_t(memory, pair_grad)
    memory_grad = low(matmul_right_t(pair_grad, cross_kv))
    cross_bias_grad = jnp.concatenate([column_sums(cq), column_sums(cv), column_sums(low_two)])
    first_grad = back_two + matmul_right_t(cq, cross_query)
    cross_grads = reduce_group(net, (cross_query_grad, cross_kv_grad, cross_out_grad), CROSS_MOVES, (1024, 1024))

    gain_one, shift_one, back_one = norm_backward(first_grad, normed_one, inverse_one, self_gain)
    low_one = low(back_one)
    self_out_grad = matmul_left_t(self_mix, low_one)
    mix_grad = low(matmul_right_t(low_one, self_out))
    sq, sk, sv = attend_backward(self_first, self_extra, *parts, self_mix, mix_grad, self_lse,
                                 target_segments, target_segments, True)
    joined = jnp.concatenate([sq, sk, sv], axis=1)
    self_qkv_grad = matmul_left_t(target, joined)
    self_bias_grad = jnp.concatenate([column_sums(sq), column_sums(sv), column_sums(low_one)])
    self_grads = reduce_group(net, (self_qkv_grad, self_out_grad),
                              [m for m in SELF_MOVES if m[3] != 2], (1024, 1024))
    target_grad = low(back_one + matmul_right_t(joined, self_qkv))
    small = reduce_small(net, (
        self_bias_grad, gain_one, shift_one, cross_bias_grad, gain_two, shift_two,
        column_sums(pre_grad), column_sums(low_three), gain_three, shift_three))
    return (output, target_grad, memory_grad, *self_grads, *cross_grads, *ffn_grads, *small)


def solution(mesh):
    both = ("wide", "narrow")
    matrix, vector = P(both, None), P(both)
    return jax.shard_map(
        per_device,
        mesh=mesh,
        in_specs=(matrix,) * 13 + (vector,) * 10,
        out_specs=(matrix,) * 10 + (vector,) * 10,
        check_vma=False,
    )
```

```python
import functools

import jax
import jax.numpy as jnp
from jax import lax
from jax.experimental import pallas as pl
from jax.experimental.pallas import tpu as pltpu
from jax.sharding import PartitionSpec as P

MASKED = -1e30
EPSILON = 1e-05
BLOCK = 128
WINDOW = 256
UNIT = 16
AXES = ("wide", "narrow")
NT = (((1,), (1,)), ((), ()))
TN = (((0,), (0,)), ((), ()))
NN = (((1,), (0,)), ((), ()))
BF = jnp.bfloat16
F32 = jnp.float32


def mxu(a, b, dims=NN):
    return lax.dot_general(a, b, dims, preferred_element_type=F32)


def low(x):
    return x.astype(BF)


def wide(x):
    return x.astype(F32)


def shape_of(shape, dtype=BF):
    return jax.ShapeDtypeStruct(shape, dtype)


def smem():
    return pl.BlockSpec(memory_space=pltpu.SMEM)


def vmem():
    return pl.BlockSpec(memory_space=pltpu.VMEM)


def fixed(shape, *index):
    return pl.BlockSpec(shape, lambda i, index=index: index, pipeline_mode=pl.Buffered(1))


def tiled(rows, cols, col=0):
    return pl.BlockSpec((rows, cols), lambda i, col=col: (i, col))


def params(mib):
    return pltpu.CompilerParams(vmem_limit_bytes=mib << 20)


def cost(micros):
    return pl.CostEstimate(flops=int(micros * 1e9), bytes_accessed=1 << 20, transcendentals=0)


def lane_masks(scale):
    lane = lax.broadcasted_iota(jnp.int32, (1, 128), 1)
    return low(jnp.where(lane < 64, scale, 0.0)), low(jnp.where(lane < 64, 0.0, scale))


def stacked(pair, masks):
    return jnp.concatenate([pair * masks[0], pair * masks[1]], axis=0)


def pick(both):
    sub = lax.broadcasted_iota(jnp.int32, (128, BLOCK), 0)
    return jnp.where(sub < 64, both[:, :BLOCK], both[:, BLOCK:])


def columns_of(row):
    return jnp.transpose(jnp.broadcast_to(row, (128, row.shape[1])))


def bias_of(seg_cols, seg_row, q0, start, bound, kind):
    allowed = seg_cols == seg_row
    key = lax.broadcasted_iota(jnp.int32, (WINDOW, BLOCK), 0) + start
    if kind == "diag":
        allowed = allowed & (key <= lax.broadcasted_iota(jnp.int32, (WINDOW, BLOCK), 1) + q0)
    elif kind == "left":
        allowed = allowed & (key < bound)
    else:
        allowed = allowed & (key >= bound)
    return jnp.where(allowed, 0.0, MASKED)


def window(causal, first_ref, r, qb, c, length):
    if causal:
        end = (qb + 1) * BLOCK - c * WINDOW
        return pl.multiple_of(jnp.maximum(end - WINDOW, 0), BLOCK), end
    begin = first_ref[r, qb] + c * WINDOW
    return pl.multiple_of(jnp.minimum(begin, length - WINDOW), 16), begin


def lanes_at(offset, p):
    return slice(offset + 128 * p, offset + 128 * p + 128)


def attend(causal, r, first_ref, extra_ref, q, k, v, qseg_ref, cols, out_ref, lse_ref, top, total, mix):
    length = q[0].shape[0]
    masks = lane_masks(0.125)

    def block(qb, _):
        q0 = pl.multiple_of(qb * BLOCK, BLOCK)
        seg_row = qseg_ref[0, :, pl.ds(q0, BLOCK)]

        def pieces(c, kind):
            start, bound = window(causal, first_ref, r, qb, c, length)
            bias = bias_of(cols[pl.ds(start, WINDOW), :], seg_row, q0, start, bound, kind)
            bias = jnp.concatenate([bias, bias], axis=1)
            scores = []
            for p in range(4):
                qs = stacked(q[0][pl.ds(q0, BLOCK), lanes_at(q[1], p)], masks)
                keys = k[0][pl.ds(start, WINDOW), lanes_at(k[1], p)]
                scores.append(mxu(keys, qs, NT) + bias)
            return scores, [v[0][pl.ds(start, WINDOW), lanes_at(v[1], p)] for p in range(4)]

        scores, values = pieces(0, "diag" if causal else "from")
        for p in range(4):
            high = jnp.max(scores[p], axis=0, keepdims=True)
            weights = jnp.exp(scores[p] - high)
            top[p] = high
            total[p] = jnp.sum(weights, axis=0, keepdims=True)
            mix[p] = pick(mxu(values[p], low(weights), TN))

        def more(c, _):
            scores, values = pieces(c + 1, "left" if causal else "from")
            for p in range(4):
                old = top[p]
                high = jnp.maximum(old, jnp.max(scores[p], axis=0, keepdims=True))
                weights = jnp.exp(scores[p] - high)
                fade = jnp.exp(old - high)
                top[p] = high
                total[p] = total[p] * fade + jnp.sum(weights, axis=0, keepdims=True)
                mix[p] = mix[p] * pick(jnp.broadcast_to(fade, (128, 2 * BLOCK))) + pick(mxu(values[p], low(weights), TN))
            return 0

        lax.fori_loop(0, extra_ref[r, qb], more, 0)
        for p in range(4):
            sums = total[p]
            inverse = pick(jnp.broadcast_to(1.0 / sums, (128, 2 * BLOCK)))
            out_ref[pl.ds(q0, BLOCK), lanes_at(0, p)] = low(jnp.transpose(mix[p] * inverse))
            lse = top[p] + jnp.log(sums)
            lse_ref[0, 2 * p:2 * p + 1, pl.ds(q0, BLOCK)] = lse[:, :BLOCK]
            lse_ref[0, 2 * p + 1:2 * p + 2, pl.ds(q0, BLOCK)] = lse[:, BLOCK:]
        return 0

    lax.fori_loop(0, length // BLOCK, block, 0)


ATTEND_SCRATCH = lambda length: [
    pltpu.VMEM((length, 128), F32), pltpu.VMEM((4, 1, 2 * BLOCK), F32),
    pltpu.VMEM((4, 1, 2 * BLOCK), F32), pltpu.VMEM((4, 128, BLOCK), F32)]


def norm(hidden):
    average = jnp.mean(hidden, axis=-1, keepdims=True)
    centred = hidden - average
    inverse = lax.rsqrt(jnp.mean(centred * centred, axis=-1, keepdims=True) + EPSILON)
    return centred * inverse, inverse


def norm_back(grad, normed, inverse, gain):
    scaled = grad * gain
    return inverse * (scaled - jnp.mean(scaled, axis=-1, keepdims=True)
                      - normed * jnp.mean(scaled * normed, axis=-1, keepdims=True))


def sum_rows(x):
    return jnp.sum(wide(x), axis=0, keepdims=True)


S_BIAS, S_GAIN, S_SHIFT, C_BIAS, C_GAIN, C_SHIFT, I_BIAS, O_BIAS, F_GAIN, F_SHIFT = range(10)


def vec(ref, row, block=0, size=512):
    return ref[row:row + 1, block * size:(block + 1) * size]


def self_kernel(first_ref, extra_ref, x_ref, w_ref, vec_ref, seg_ref, qkv_ref, mix_ref, lse_ref, cols, *state):
    r = pl.program_id(0)
    cols[...] = columns_of(seg_ref[0])
    x = x_ref[...]
    qkv_ref[:, :512] = low(mxu(x, w_ref[:, :512]) + vec(vec_ref, S_BIAS, 0))
    qkv_ref[:, 512:1024] = low(mxu(x, w_ref[:, 512:1024]))
    qkv_ref[:, 1024:] = low(mxu(x, w_ref[:, 1024:]) + vec(vec_ref, S_BIAS, 1))
    attend(True, r, first_ref, extra_ref, (qkv_ref, 0), (qkv_ref, 512), (qkv_ref, 1024), seg_ref, cols, mix_ref, lse_ref, *state)


def self_forward(plan, x, w, vectors, seg):
    rows, _, length = seg.shape
    return pl.pallas_call(
        self_kernel, grid=(rows,),
        in_specs=[smem(), smem(), tiled(length, 512), fixed((512, 1536), 0, 0), fixed((16, 2048), 0, 0),
                  pl.BlockSpec((1, 1, length), lambda i: (i, 0, 0))],
        out_specs=[tiled(length, 1536), tiled(length, 512), pl.BlockSpec((1, 8, length), lambda i: (i, 0, 0))],
        out_shape=[shape_of((rows * length, 1536)), shape_of((rows * length, 512)), shape_of((rows, 8, length), F32)],
        scratch_shapes=ATTEND_SCRATCH(length), compiler_params=params(40), cost_estimate=cost(20), name="self_forward",
    )(*plan, x, w, vectors, seg)


def cross_kernel(first_ref, extra_ref, x_ref, mix_ref, mem_ref, wo_ref, wq_ref, wkv_ref, vec_ref, qseg_ref, kseg_ref,
                 hid_ref, q_ref, kv_ref, out_ref, lse_ref, cols, *state):
    r = pl.program_id(0)
    cols[...] = columns_of(kseg_ref[0])
    hidden = wide(x_ref[...]) + mxu(mix_ref[...], wo_ref[...]) + vec(vec_ref, S_BIAS, 2)
    hid_ref[...] = hidden
    first = low(norm(hidden)[0] * vec(vec_ref, S_GAIN) + vec(vec_ref, S_SHIFT))
    q_ref[...] = low(mxu(first, wq_ref[...]) + vec(vec_ref, C_BIAS, 0))
    mem = mem_ref[...]
    kv_ref[:, :512] = low(mxu(mem, wkv_ref[:, :512]))
    kv_ref[:, 512:] = low(mxu(mem, wkv_ref[:, 512:]) + vec(vec_ref, C_BIAS, 1))
    attend(False, r, first_ref, extra_ref, (q_ref, 0), (kv_ref, 0), (kv_ref, 512), qseg_ref, cols, out_ref, lse_ref, *state)


def cross_forward(plan, x, mix, mem, rest, vectors, qseg, kseg):
    rows, _, length = qseg.shape
    seg = pl.BlockSpec((1, 1, length), lambda i: (i, 0, 0))
    total = rows * length
    return pl.pallas_call(
        cross_kernel, grid=(rows,),
        in_specs=[smem(), smem(), tiled(length, 512), tiled(length, 512), tiled(length, 512),
                  fixed((512, 512), 0, 10), fixed((512, 512), 0, 11), fixed((512, 1024), 0, 4), fixed((16, 2048), 0, 0), seg, seg],
        out_specs=[tiled(length, 512), tiled(length, 512), tiled(length, 1024), tiled(length, 512),
                   pl.BlockSpec((1, 8, length), lambda i: (i, 0, 0))],
        out_shape=[shape_of((total, 512), F32), shape_of((total, 512)), shape_of((total, 1024)), shape_of((total, 512)),
                   shape_of((rows, 8, length), F32)],
        scratch_shapes=ATTEND_SCRATCH(length), compiler_params=params(48), cost_estimate=cost(25), name="cross_forward",
    )(*plan, x, mix, mem, rest, rest, rest, vectors, qseg, kseg)


def back_kernel(causal, row, first_ref, extra_ref, q_ref, k_ref, v_ref, mix_ref, grad_ref, lse_ref, qseg_ref, kseg_ref, *refs):
    dq_ref, dk_ref, dv_ref, cols, dk, dv, dq = refs[-7:]
    r = row
    length = q_ref.shape[0]
    cols[...] = columns_of(kseg_ref[0])
    dk[...] = jnp.zeros_like(dk)
    dv[...] = jnp.zeros_like(dv)
    masks = lane_masks(0.125)
    ones = lane_masks(1.0)
    pair_rows = jnp.concatenate([ones[0], ones[1], jnp.zeros((14, 128), BF)], axis=0)

    def block(qb, _):
        q0 = pl.multiple_of(qb * BLOCK, BLOCK)
        seg_row = qseg_ref[0, :, pl.ds(q0, BLOCK)]

        def piece(c, kind, first):
            start, bound = window(causal, first_ref, r, qb, c, length)
            bias = bias_of(cols[pl.ds(start, WINDOW), :], seg_row, q0, start, bound, kind)
            bias = jnp.concatenate([bias, bias], axis=1)
            here = pl.ds(start, WINDOW)
            parts, new_dv, new_dk = [], [], []
            for p in range(4):
                lanes = lanes_at(0, p)
                qs = stacked(q_ref[pl.ds(q0, BLOCK), lanes], masks)
                grad = grad_ref[pl.ds(q0, BLOCK), lanes]
                gs = stacked(grad, ones)
                prod = wide(grad) * wide(mix_ref[pl.ds(q0, BLOCK), lanes])
                upper = low(prod)
                delta = mxu(pair_rows, upper, NT) + mxu(pair_rows, low(prod - wide(upper)), NT)
                delta = jnp.concatenate([delta[0:1], delta[1:2]], axis=1)
                lse = jnp.concatenate([lse_ref[0, 2 * p:2 * p + 1, pl.ds(q0, BLOCK)],
                                       lse_ref[0, 2 * p + 1:2 * p + 2, pl.ds(q0, BLOCK)]], axis=1)
                keys = k_ref[here, lanes]
                probs = jnp.exp(mxu(keys, qs, NT) + bias - lse)
                dprobs = mxu(v_ref[here, lanes], gs, NT)
                dscores = low(probs * (dprobs - delta))
                new_dv.append(mxu(low(probs), gs))
                new_dk.append(mxu(dscores, qs))
                parts.append(pick(mxu(keys, dscores, TN)))
            for p in range(4):
                lanes = lanes_at(0, p)
                dv[here, lanes] += new_dv[p]
                dk[here, lanes] += new_dk[p]
                if first:
                    dq[p] = parts[p]
                else:
                    dq[p] += parts[p]

        piece(0, "diag" if causal else "from", True)

        def more(c, _):
            piece(c + 1, "left" if causal else "from", False)
            return 0

        lax.fori_loop(0, extra_ref[r, qb], more, 0)
        for p in range(4):
            dq_ref[pl.ds(q0, BLOCK), lanes_at(0, p)] = low(jnp.transpose(dq[p]) * 0.125)
        return 0

    lax.fori_loop(0, length // BLOCK, block, 0)
    dk_ref[...] = low(dk[...])
    dv_ref[...] = low(dv[...])


def attend_back(causal, row, plan, q, k, v, mix, grad, lse, qseg, kseg, before, after=()):
    rows, _, length = qseg.shape
    spec = lambda col: pl.BlockSpec((length, 512), lambda i, col=col: (row, col))
    seg = pl.BlockSpec((1, 1, length), lambda i: (row, 0, 0))
    out = pl.BlockSpec((length, 512), lambda i: (row, 0))
    extra = tuple(before) + tuple(after)
    return pl.pallas_call(
        functools.partial(back_kernel, causal, row), grid=(1,),
        in_specs=[smem(), smem(), spec(q[1]), spec(k[1]), spec(v[1]), spec(0), spec(0),
                  pl.BlockSpec((1, 8, length), lambda i: (row, 0, 0)), seg, seg]
        + [pl.BlockSpec(memory_space=pl.ANY)] * len(extra),
        out_specs=[out] * 3, out_shape=[shape_of((rows * length, 512))] * 3,
        input_output_aliases={10 + i: i for i in range(len(before))},
        scratch_shapes=[pltpu.VMEM((length, 128), F32), pltpu.VMEM((length, 512), F32),
                        pltpu.VMEM((length, 512), F32), pltpu.VMEM((4, 128, BLOCK), F32)],
        compiler_params=params(40), cost_estimate=cost(14), name="self_back" if causal else "cross_back",
    )(*plan, q[0], k[0], v[0], mix, grad, lse, qseg, kseg, *extra)


def emit(out_ref, col, acc, index_ref, acc_col, width, blocks=1, which=0):
    for r in range(512 // UNIT):
        row = pl.multiple_of((index_ref[r] * blocks + which) * UNIT, UNIT)
        out_ref[r, :, col:col + width] = low(acc[pl.ds(row, UNIT), acc_col:acc_col + width])


MID_TILE = 256
CHUNK = 512


def mid_kernel(index_a, index_b, hid_ref, mix_ref, grad_ref, win_ref, gout_ref, wco_ref, vec_ref,
               out_ref, h2_ref, mg_ref, a_ref, b_ref, co_ref, small_ref,
               wout, dwin, dwout, dwco, act, slope):
    step = pl.program_id(0)
    hidden_width = win_ref.shape[1]
    tokens = hid_ref.shape[0]

    @pl.when(step == 0)
    def _():
        for d in range(512 // UNIT):
            for b in range(4):
                wout[(4 * d + b) * UNIT:(4 * d + b + 1) * UNIT, :] = gout_ref[d * UNIT:(d + 1) * UNIT, 512 * b:512 * b + 512]
        dwin[...] = jnp.zeros_like(dwin)
        dwout[...] = jnp.zeros_like(dwout)
        dwco[...] = jnp.zeros_like(dwco)
        small_ref[...] = jnp.zeros_like(small_ref)

    chunks = [slice(c, c + CHUNK) for c in range(0, hidden_width, CHUNK)]
    first = norm(hid_ref[...])[0] * vec(vec_ref, S_GAIN) + vec(vec_ref, S_SHIFT)
    mix = mix_ref[...]
    normed2, inverse2 = norm(first + mxu(mix, wco_ref[...]) + vec(vec_ref, C_BIAS, 2))
    second = normed2 * vec(vec_ref, C_GAIN) + vec(vec_ref, C_SHIFT)
    second_low = low(second)
    hidden3 = second + vec(vec_ref, O_BIAS)
    for c in chunks:
        pre = mxu(second_low, win_ref[:, c]) + vec_ref[I_BIAS:I_BIAS + 1, c]
        sig = 1.0 / (1.0 + jnp.exp(-pre))
        active = low(pre * sig)
        act[:, c] = active
        slope[:, c] = sig * (1.0 + pre * (1.0 - sig))
        hidden3 += mxu(active, wout[c, :])
    normed3, inverse3 = norm(hidden3)
    out_ref[...] = low(normed3 * vec(vec_ref, F_GAIN) + vec(vec_ref, F_SHIFT))
    grad = wide(grad_ref[...])
    back3 = norm_back(grad, normed3, inverse3, vec(vec_ref, F_GAIN))
    b3 = low(back3)
    small_ref[1:2, :512] += sum_rows(b3)
    small_ref[2:3, :512] += sum_rows(grad * normed3)
    small_ref[3:4, :512] += sum_rows(grad)
    second_t = jnp.transpose(second_low)
    b3_t = jnp.transpose(b3)
    grad2 = back3
    for c in chunks:
        u = low(mxu(b3, wout[c, :], NT) * slope[:, c])
        dwin[:, c] += mxu(second_t, u)
        dwout[:, c] += mxu(b3_t, act[:, c])
        small_ref[0:1, c] += sum_rows(u)
        grad2 += mxu(u, win_ref[:, c], NT)
    h2 = norm_back(grad2, normed2, inverse2, vec(vec_ref, C_GAIN))
    h2_ref[...] = h2
    b2 = low(h2)
    small_ref[4:5, :512] += sum_rows(grad2 * normed2)
    small_ref[5:6, :512] += sum_rows(grad2)
    small_ref[6:7, :512] += sum_rows(b2)
    dwco[...] += mxu(jnp.transpose(mix), b2)
    mg_ref[...] = low(mxu(b2, wco_ref[...], NT))

    @pl.when(step == pl.num_programs(0) - 1)
    def _():
        emit(a_ref, 0, dwin, index_a, 0, hidden_width)
        for c in chunks:
            wout[c, :] = low(jnp.transpose(dwout[:, c]))
        for r in range(512 // UNIT):
            for b in range(4):
                row = pl.multiple_of((index_b[r] * 4 + b) * UNIT, UNIT)
                b_ref[r, :, 512 * b:512 * b + 512] = wout[pl.ds(row, UNIT), :]
        co_ref[...] = dwco[...]


def middle(index_a, index_b, hid, mix, grad, rest, vectors):
    total = hid.shape[0]
    t = MID_TILE
    blocks = 512 // UNIT
    return pl.pallas_call(
        mid_kernel, grid=(total // t,),
        in_specs=[smem(), smem(), tiled(t, 512), tiled(t, 512), tiled(t, 512),
                  fixed((512, 2048), 0, 0), fixed((512, 2048), 0, 1), fixed((512, 512), 0, 12), fixed((16, 2048), 0, 0)],
        out_specs=[tiled(t, 512), tiled(t, 512), tiled(t, 512), fixed((blocks, UNIT, 2048), 0, 0, 0),
                   fixed((blocks, UNIT, 2048), 0, 0, 0), fixed((512, 512), 0, 0), fixed((8, 2048), 0, 0)],
        out_shape=[shape_of((total, 512)), shape_of((total, 512), F32), shape_of((total, 512)),
                   shape_of((blocks, UNIT, 2048)), shape_of((blocks, UNIT, 2048)), shape_of((512, 512), F32), shape_of((8, 2048), F32)],
        scratch_shapes=[pltpu.VMEM((2048, 512), BF), pltpu.VMEM((512, 2048), F32), pltpu.VMEM((512, 2048), F32),
                        pltpu.VMEM((512, 512), F32), pltpu.VMEM((t, 2048), BF), pltpu.VMEM((t, 2048), F32)],
        compiler_params=params(56), cost_estimate=cost(40), name="middle",
    )(index_a, index_b, hid, mix, grad, rest, rest, rest, vectors)


def cross_dense_kernel(index_a, index_b, cq_ref, ck_ref, cv_ref, mem_ref, hid_ref, h2_ref, mix_ref,
                       wq_ref, wkv_ref, wo_ref, co_ref, vec_ref,
                       memgrad_ref, h1_ref, mg_ref, a_ref, b_ref, small_ref, dq, dkv, do):
    step = pl.program_id(0)

    @pl.when(step == 0)
    def _():
        dq[...] = jnp.zeros_like(dq)
        dkv[...] = jnp.zeros_like(dkv)
        do[...] = jnp.zeros_like(do)
        small_ref[...] = jnp.zeros_like(small_ref)

    cq, ck, cv = cq_ref[...], ck_ref[...], cv_ref[...]
    normed, inverse = norm(hid_ref[...])
    first = low(normed * vec(vec_ref, S_GAIN) + vec(vec_ref, S_SHIFT))
    grad1 = h2_ref[...] + mxu(cq, wq_ref[...], NT)
    h1 = norm_back(grad1, normed, inverse, vec(vec_ref, S_GAIN))
    h1_ref[...] = h1
    b1 = low(h1)
    mg_ref[...] = low(mxu(b1, wo_ref[...], NT))
    memgrad_ref[...] = low(mxu(ck, wkv_ref[:, :512], NT) + mxu(cv, wkv_ref[:, 512:], NT))
    dq[...] += mxu(jnp.transpose(first), cq)
    mem_t = jnp.transpose(mem_ref[...])
    dkv[:, :512] += mxu(mem_t, ck)
    dkv[:, 512:] += mxu(mem_t, cv)
    do[...] += mxu(jnp.transpose(mix_ref[...]), b1)
    small_ref[0:1, :] += sum_rows(cq)
    small_ref[1:2, :] += sum_rows(cv)
    small_ref[2:3, :] += sum_rows(grad1 * normed)
    small_ref[3:4, :] += sum_rows(grad1)
    small_ref[4:5, :] += sum_rows(b1)

    @pl.when(step == pl.num_programs(0) - 1)
    def _():
        emit(a_ref, 0, dq, index_a, 0, 512)
        emit(a_ref, 512, co_ref, index_a, 0, 512)
        emit(a_ref, 1024, do, index_a, 0, 256)
        emit(b_ref, 0, dkv, index_b, 0, 1024)
        emit(b_ref, 1024, do, index_b, 256, 256)


def cross_dense(index_a, index_b, grads, mem, hid, h2, mix, rest, dco, vectors):
    total = hid.shape[0]
    t = 256
    blocks = 512 // UNIT
    return pl.pallas_call(
        cross_dense_kernel, grid=(total // t,),
        in_specs=[smem(), smem()] + [tiled(t, 512)] * 7
        + [fixed((512, 512), 0, 11), fixed((512, 1024), 0, 4), fixed((512, 512), 0, 10), fixed((512, 512), 0, 0), fixed((16, 2048), 0, 0)],
        out_specs=[tiled(t, 512)] * 3 + [fixed((blocks, UNIT, 1280), 0, 0, 0)] * 2 + [fixed((8, 512), 0, 0)],
        out_shape=[shape_of((total, 512)), shape_of((total, 512), F32), shape_of((total, 512)),
                   shape_of((blocks, UNIT, 1280)), shape_of((blocks, UNIT, 1280)), shape_of((8, 512), F32)],
        scratch_shapes=[pltpu.VMEM((512, 512), F32), pltpu.VMEM((512, 1024), F32), pltpu.VMEM((512, 512), F32)],
        compiler_params=params(40), cost_estimate=cost(12), name="cross_dense",
    )(index_a, index_b, *grads, mem, hid, h2, mix, rest, rest, rest, dco, vectors)


VECTORS = (1536, 512, 512, 1536, 512, 512, 2048, 512, 512, 512)


def places(n, per, count, axis):
    shape = (1, n)
    at = wide(lax.broadcasted_iota(jnp.int32, shape, 1))
    owner = jnp.floor((at + 0.5) * (1.0 / per))
    return owner, at - owner * per


def one_hot(n, per):
    _, place = places(n, per, n // per, 1)
    return low(jnp.where(wide(lax.broadcasted_iota(jnp.int32, (128, n), 0)) == place, 1.0, 0.0))


def owned(n, per, count):
    owner, _ = places(n, per, count, 1)
    return wide(lax.broadcasted_iota(jnp.int32, (count, n), 0)) == owner


def self_grad_kernel(count, index_a, index_b, dq_ref, dk_ref, dv_ref, x_ref, mid_ref, small_ref, a_ref, b_ref, lines_ref, dw, table):
    step = pl.program_id(0)

    @pl.when(step == 0)
    def _():
        dw[...] = jnp.zeros_like(dw)
        lines_ref[...] = jnp.zeros_like(lines_ref)

    x_t = jnp.transpose(x_ref[...])
    dw[:, :512] += mxu(x_t, dq_ref[...])
    dw[:, 512:1024] += mxu(x_t, dk_ref[...])
    dw[:, 1024:] += mxu(x_t, dv_ref[...])
    lines_ref[S_BIAS:S_BIAS + 1, :512] += sum_rows(dq_ref[...])
    lines_ref[S_BIAS:S_BIAS + 1, 512:1024] += sum_rows(dv_ref[...])

    @pl.when(step == pl.num_programs(0) - 1)
    def _():
        emit(a_ref, 0, dw, index_a, 0, 768)
        emit(b_ref, 0, dw, index_b, 768, 768)
        for row, col, source, source_row in (
            (S_BIAS, 1024, small_ref, 4), (S_GAIN, 0, small_ref, 2), (S_SHIFT, 0, small_ref, 3),
            (C_BIAS, 0, small_ref, 0), (C_BIAS, 512, small_ref, 1), (C_BIAS, 1024, mid_ref, 6),
            (C_GAIN, 0, mid_ref, 4), (C_SHIFT, 0, mid_ref, 5),
            (O_BIAS, 0, mid_ref, 1), (F_GAIN, 0, mid_ref, 2), (F_SHIFT, 0, mid_ref, 3),
        ):
            lines_ref[row:row + 1, col:col + 512] = source[source_row:source_row + 1, :512]
        lines_ref[I_BIAS:I_BIAS + 1, :] = mid_ref[0:1, :]
        if count:
            table[...] = jnp.zeros_like(table)
            for n in (512, 1536, 2048):
                hot, mine = one_hot(n, n // count), owned(n, n // count, count)
                for j, size in enumerate(VECTORS):
                    if size == n:
                        line = jnp.broadcast_to(lines_ref[j:j + 1, :n], (count, n))
                        table[:, j, :] = mxu(low(jnp.where(mine, line, 0.0)), hot, NT)
            for r in range(count):
                a_ref[r, :, 768:896] = low(table[index_a[r]])


def self_grad(count, index_a, index_b, grads, x, mid_small, small):
    total = x.shape[0]
    t = 256
    blocks = 512 // UNIT
    return pl.pallas_call(
        functools.partial(self_grad_kernel, count), grid=(total // t,),
        in_specs=[smem(), smem()] + [tiled(t, 512)] * 4 + [fixed((8, 2048), 0, 0), fixed((8, 512), 0, 0)],
        out_specs=[fixed((blocks, UNIT, 896), 0, 0, 0), fixed((blocks, UNIT, 768), 0, 0, 0), fixed((16, 2048), 0, 0)],
        out_shape=[shape_of((blocks, UNIT, 896)), shape_of((blocks, UNIT, 768)), shape_of((16, 2048), F32)],
        scratch_shapes=[pltpu.VMEM((512, 1536), F32), pltpu.VMEM((max(count, 8), 16, 128), F32)],
        compiler_params=params(40), cost_estimate=cost(5), name="self_grad",
    )(index_a, index_b, *grads, x, mid_small, small)


def target_kernel(h1_ref, dq_ref, dk_ref, dv_ref, w_ref, *refs):
    out_ref = refs[-1]
    total = h1_ref[...] + mxu(dq_ref[...], w_ref[:, :512], NT)
    total += mxu(dk_ref[...], w_ref[:, 512:1024], NT)
    out_ref[...] = low(total + mxu(dv_ref[...], w_ref[:, 1024:], NT))


def target_grad(h1, grads, w, after=()):
    total = h1.shape[0]
    t = 512
    return pl.pallas_call(
        target_kernel, grid=(total // t,), in_specs=[tiled(t, 512)] * 4 + [fixed((512, 1536), 0, 0)]
        + [pl.BlockSpec(memory_space=pl.ANY)] * len(after),
        out_specs=tiled(t, 512), out_shape=shape_of((total, 512)), compiler_params=params(40), cost_estimate=cost(5), name="target_grad",
    )(h1, *grads, w, *after)


class Net:
    def __init__(self):
        self.wide = lax.axis_size("wide")
        self.narrow = lax.axis_size("narrow")
        self.count = self.wide * self.narrow
        self.wide_bits = self.wide.bit_length() - 1
        self.narrow_bits = self.narrow.bit_length() - 1
        self.bits = self.wide_bits + self.narrow_bits
        self.me = lax.axis_index("wide") * self.narrow + lax.axis_index("narrow")
        inner = list(range(self.narrow_bits))
        core, second = [self.narrow_bits], [self.narrow_bits + 1]
        far = list(range(self.narrow_bits + 2, self.bits))
        self.orders = (core + second + inner + far, core + inner + second + far)

    def exchange(self, x, bit):
        if bit < self.narrow_bits:
            return lax.ppermute(x, "narrow", [(i, i ^ (1 << bit)) for i in range(self.narrow)])
        bit -= self.narrow_bits
        return lax.ppermute(x, "wide", [(i, i ^ (1 << bit)) for i in range(self.wide)])

    def index(self, chain):
        order, n = self.orders[chain], self.bits
        mask = [sum(((r >> (n - 1 - s)) & 1) << bit for s, bit in enumerate(order)) for r in range(self.count)]
        return jnp.array(mask, jnp.int32) ^ self.me

    def gather_index(self, chain):
        order = self.orders[chain][::-1]
        mask = [sum(((r >> s) & 1) << bit for s, bit in enumerate(order)) for r in range(self.count)]
        return jnp.array(mask, jnp.int32) ^ self.me


def pack_kernel(*refs):
    vectors, (qkv, so, cq, ckv, co, fin, fout, a_ref, b_ref, rest_ref) = refs[:10], refs[10:20]
    lines, sem = refs[20:30], refs[30]
    moves = list(zip(vectors, lines))
    moves += [(qkv.at[:, :768], a_ref.at[0, :, :768]), (qkv.at[:, 768:], b_ref.at[0]), (fin, rest_ref.at[:, :2048])]
    moves += [(fout.at[UNIT * b:UNIT * b + UNIT, :], rest_ref.at[:, 2048 + 512 * b:2560 + 512 * b]) for b in range(4)]
    moves += [(ckv, rest_ref.at[:, 4096:5120]), (so, rest_ref.at[:, 5120:5632]),
              (cq, rest_ref.at[:, 5632:6144]), (co, rest_ref.at[:, 6144:])]
    copies = [pltpu.make_async_copy(src, dst, sem.at[i]) for i, (src, dst) in enumerate(moves)]
    for copy in copies:
        copy.start()
    for copy in copies:
        copy.wait()
    rows = []
    for v in lines:
        line = wide(v[...])
        rows.append(jnp.concatenate([line, jnp.zeros((1, 128 - line.shape[1]), F32)], axis=1))
    rows.append(jnp.zeros((6, 128), F32))
    a_ref[0, :, 768:] = low(jnp.concatenate(rows, axis=0))


def unpack_kernel(count, index_a, index_b, *refs):
    n = (len(refs) - 3) // 2
    pieces_a, pieces_b, (w_ref, vec_ref, table) = refs[:n], refs[n:2 * n], refs[2 * n:]
    for pieces, index, col, width in ((pieces_a, index_a, 0, 768), (pieces_b, index_b, 768, 768)):
        r = 0
        for piece in pieces:
            for j in range(piece.shape[0]):
                owner = index[r]
                w_ref[pl.ds(pl.multiple_of(owner * UNIT, UNIT), UNIT), col:col + width] = piece[j, :, :width]
                if col == 0:
                    table[owner] = wide(piece[j, :, 768:896])
                r += 1
    vec_ref[...] = jnp.zeros_like(vec_ref)
    for n in (512, 1536, 2048):
        hot, mine = one_hot(n, n // count), owned(n, n // count, count)
        for j, size in enumerate(VECTORS):
            if size == n:
                spread = mxu(low(table[:, j, :]), hot)
                vec_ref[j:j + 1, :n] = jnp.sum(jnp.where(mine, spread, 0.0), axis=0, keepdims=True)


def gather_weights(net, small, big):
    qkv, so, cq, ckv, co, fin, fout = big
    if qkv.shape[0] % UNIT or net.bits < 5:
        small, big = lax.all_gather((small, big), AXES, axis=0, tiled=True) if net.count > 1 else (small, big)
        qkv, so, cq, ckv, co, fin, fout = big
        fout = fout.reshape(-1, 4, UNIT, 512).transpose(0, 2, 1, 3).reshape(512, 2048)
        rows = [jnp.pad(wide(v), (0, 2048 - v.shape[0])) for v in small]
        vectors = jnp.stack(rows + [jnp.zeros((2048,), F32)] * 6)
        return qkv, vectors, jnp.concatenate([fin, fout, ckv, so, cq, co], axis=1)
    a, b, rest = pl.pallas_call(
        pack_kernel, in_specs=[pl.BlockSpec(memory_space=pl.ANY)] * 17, out_specs=[vmem()] * 3,
        out_shape=[shape_of((1, UNIT, 896)), shape_of((1, UNIT, 768)), shape_of((UNIT, 6656))],
        scratch_shapes=[pltpu.VMEM((1, v.shape[0]), BF) for v in small] + [pltpu.SemaphoreType.DMA((21,))],
        compiler_params=params(60), cost_estimate=cost(2), name="pack",
    )(*[v[None] for v in small], *big)
    rest = lax.all_gather(rest, AXES, axis=0, tiled=True)
    orders = [order[::-1] for order in net.orders]
    far = net.bits - 3
    both = [a, b]
    for s in range(far):
        both = [jnp.concatenate([x, net.exchange(x, order[s])], axis=0) for x, order in zip(both, orders)]
    both = [jnp.concatenate([x, net.exchange(x, order[far])], axis=0) for x, order in zip(both, orders)]
    pieces = [[x] for x in both]
    for s in (far + 1, far + 2):
        got = [[net.exchange(x, order[s]) for x in chain] for chain, order in zip(pieces, orders)]
        pieces = [chain + more for chain, more in zip(pieces, got)]
    w, vectors = pl.pallas_call(
        functools.partial(unpack_kernel, net.count), in_specs=[smem(), smem()] + [vmem()] * (len(pieces[0]) * 2), out_specs=[vmem()] * 2,
        out_shape=[shape_of((512, 1536)), shape_of((16, 2048), F32)],
        scratch_shapes=[pltpu.VMEM((net.count, 16, 128), F32)],
        compiler_params=params(40), cost_estimate=cost(2), name="unpack",
    )(net.gather_index(0), net.gather_index(1), *pieces[0], *pieces[1])
    return w, vectors, rest


class Reduction:
    def __init__(self, net, blocks):
        self.net = net
        half = net.count // 2
        self.keep = [x[:half] for x in blocks]
        self.send = [x[half:] for x in blocks]
        self.stage = 0
        self.sums = None

    def state(self):
        return tuple(self.send) if self.sums is None else ()

    def start(self):
        if self.sums is None:
            self.got = [self.net.exchange(x, order[self.stage]) for x, order in zip(self.send, self.net.orders)]

    def add(self):
        if self.sums is not None:
            return
        self.stage += 1
        sums = [wide(k) + wide(g) for k, g in zip(self.keep, self.got)]
        if self.stage == self.net.bits:
            self.sums = [s[0] for s in sums]
            return
        half = sums[0].shape[0] // 2
        self.keep = [low(s[:half]) for s in sums]
        self.send = [low(s[half:]) for s in sums]


def together(groups):
    if groups:
        state = lax.optimization_barrier([(group.keep, group.send) for group in groups])
        for group, (keep, send) in zip(groups, state):
            group.keep, group.send = keep, send


def plan_self(seg, positions):
    rows, length = seg.shape
    starts = jnp.arange(0, length, BLOCK, dtype=jnp.int32)
    begin = starts[None, :] - positions[:, ::BLOCK]
    left = jnp.maximum(starts[None, :] + BLOCK - WINDOW - begin, 0)
    return jnp.zeros_like(begin), (left + WINDOW - 1) // WINDOW


def plan_cross(tseg, sseg):
    last = jnp.int32(1 << 20)
    tkey = jnp.where(tseg == 0, last, tseg)
    skey = jnp.where(sseg == 0, last, sseg)
    begin = jnp.sum(skey[:, None, :] < tkey[:, ::BLOCK, None], axis=2, dtype=jnp.int32)
    end = jnp.sum(skey[:, None, :] <= tkey[:, BLOCK - 1::BLOCK, None], axis=2, dtype=jnp.int32)
    first = (begin // 16) * 16
    return first, jnp.maximum((end - first + WINDOW - 1) // WINDOW - 1, 0)


def per_device(
    target, memory, out_grad, target_segments, source_segments, target_positions,
    self_qkv, self_out, cross_query, cross_kv, cross_out, ffn_in, ffn_out, *small,
):
    net = Net()
    rows = target_segments.shape[0]
    fast = self_qkv.shape[0] % UNIT == 0 and net.bits >= 5
    self_plan = plan_self(target_segments, target_positions)
    cross_plan = plan_cross(target_segments, source_segments)
    tseg = wide(target_segments)[:, None, :]
    sseg = wide(source_segments)[:, None, :]
    w_qkv, vectors, rest = gather_weights(net, small, (self_qkv, self_out, cross_query, cross_kv, cross_out, ffn_in, ffn_out))
    if fast:
        index_a, index_b = net.index(0), net.index(1)
    else:
        index_a = index_b = jnp.arange(512 // UNIT, dtype=jnp.int32)

    qkv, self_mix, self_lse = self_forward(self_plan, target, w_qkv, vectors, tseg)
    hid, cq, pairs, cross_mix, cross_lse = cross_forward(cross_plan, target, self_mix, memory, rest, vectors, tseg, sseg)
    output, h2, cross_mg, ffn_a, ffn_b, dco, mid_small = middle(index_a, index_b, hid, cross_mix, out_grad, rest, vectors)

    groups = [Reduction(net, (ffn_a, ffn_b))] if fast else []

    def backward(causal, plan, q, k, v, mix, grad, lse, kseg):
        out = ()
        for row in range(rows):
            tied = tuple(x for group in groups for x in group.state())
            for group in groups:
                group.start()
            out = attend_back(causal, row, plan, q, k, v, mix, grad, lse, tseg, kseg, out, tied)
            for group in groups:
                group.add()
        return out

    cross_grads = backward(False, cross_plan, (cq, 0), (pairs, 0), (pairs, 1), cross_mix, cross_mg, cross_lse, sseg)
    for group in groups:
        group.start()
    memory_grad, h1, self_mg, cross_a, cross_b, small_sums = cross_dense(
        index_a, index_b, cross_grads, memory, hid, h2, self_mix, rest, dco, vectors)
    for group in groups:
        group.add()
    if fast:
        groups.append(Reduction(net, (cross_a, cross_b)))
    self_grads = backward(True, self_plan, (qkv, 0), (qkv, 1), (qkv, 2), self_mix, self_mg, self_lse, tseg)
    self_a, self_b, lines = self_grad(net.count if fast else 0, index_a, index_b, self_grads, target, mid_small, small_sums)

    if not fast:
        target_out = target_grad(h1, self_grads, w_qkv)
        total = lambda x: lax.psum_scatter(low(x), AXES, scatter_dimension=0, tiled=True).astype(F32) if net.count > 1 else wide(x)
        whole = lambda x: x.reshape(512, -1)
        a, b = whole(cross_a), whole(cross_b)
        d_out = whole(ffn_b).reshape(-1, UNIT, 4, 512).transpose(0, 2, 1, 3).reshape(2048, 512)
        weights = (jnp.concatenate([whole(self_a)[:, :768], whole(self_b)], axis=1), jnp.concatenate([a[:, 1024:], b[:, 1024:]], axis=1),
                   a[:, :512], b[:, :1024], a[:, 512:1024], whole(ffn_a), d_out)
        return (output, target_out, memory_grad, *[total(w) for w in weights], *[total(lines[j, :n]) for j, n in enumerate(VECTORS)])

    groups.append(Reduction(net, (self_a, self_b)))
    target_out = None
    while any(group.sums is None for group in groups):
        open_groups = [group for group in groups if group.sums is None]
        tied = tuple(x for group in open_groups for x in group.state())
        for group in open_groups:
            group.start()
        if groups[-1].stage == 1:
            target_out = target_grad(h1, self_grads, w_qkv, tied)
        for group in open_groups:
            group.add()
        together([group for group in open_groups if group.sums is None])
    (ffn_a, ffn_b), (cross_a, cross_b), (self_a, self_b) = (group.sums for group in groups)
    table = self_a[:, 768:]
    vectors_out = [table[j, :n // net.count] for j, n in enumerate(VECTORS)]
    return (
        output, target_out, memory_grad,
        jnp.concatenate([self_a[:, :768], self_b], axis=1),
        jnp.concatenate([cross_a[:, 1024:], cross_b[:, 1024:]], axis=1),
        cross_a[:, :512], cross_b[:, :1024], cross_a[:, 512:1024],
        ffn_a, jnp.concatenate([ffn_b[:, 512 * b:512 * b + 512] for b in range(4)], axis=0),
        *vectors_out,
    )


def solution(mesh):
    both = ("wide", "narrow")
    matrix, vector = P(both, None), P(both)
    return jax.shard_map(
        per_device, mesh=mesh,
        in_specs=(matrix,) * 13 + (vector,) * 10,
        out_specs=(matrix,) * 10 + (vector,) * 10,
        check_vma=False,
    )
```

```python
import functools

import jax
import jax.numpy as jnp
from jax import lax
from jax.experimental import pallas as pl
from jax.experimental.pallas import tpu as pltpu
from jax.sharding import PartitionSpec as P

MASKED = -1e30
EPSILON = 1e-05
BLOCK = 128
WINDOW = 256
UNIT = 16
AXES = ("wide", "narrow")
NT = (((1,), (1,)), ((), ()))
TN = (((0,), (0,)), ((), ()))
NN = (((1,), (0,)), ((), ()))
BF = jnp.bfloat16
F32 = jnp.float32


def mxu(a, b, dims=NN):
    return lax.dot_general(a, b, dims, preferred_element_type=F32)


def low(x):
    return x.astype(BF)


def wide(x):
    return x.astype(F32)


def shape_of(shape, dtype=BF):
    return jax.ShapeDtypeStruct(shape, dtype)


def smem():
    return pl.BlockSpec(memory_space=pltpu.SMEM)


def vmem():
    return pl.BlockSpec(memory_space=pltpu.VMEM)


def fixed(shape, *index):
    return pl.BlockSpec(shape, lambda i, index=index: index, pipeline_mode=pl.Buffered(1))


def tiled(rows, cols, col=0):
    return pl.BlockSpec((rows, cols), lambda i, col=col: (i, col))


def params(mib):
    return pltpu.CompilerParams(vmem_limit_bytes=mib << 20)


def cost(micros):
    return pl.CostEstimate(flops=int(micros * 1e9), bytes_accessed=1 << 20, transcendentals=0)


def lane_masks(scale):
    lane = lax.broadcasted_iota(jnp.int32, (1, 128), 1)
    return low(jnp.where(lane < 64, scale, 0.0)), low(jnp.where(lane < 64, 0.0, scale))


def stacked(pair, masks):
    return jnp.concatenate([pair * masks[0], pair * masks[1]], axis=0)


def pick(both):
    sub = lax.broadcasted_iota(jnp.int32, (128, BLOCK), 0)
    return jnp.where(sub < 64, both[:, :BLOCK], both[:, BLOCK:])


def columns_of(row):
    return jnp.transpose(jnp.broadcast_to(row, (128, row.shape[1])))


def bias_of(seg_cols, seg_row, q0, start, bound, kind):
    allowed = seg_cols == seg_row
    key = lax.broadcasted_iota(jnp.int32, (WINDOW, BLOCK), 0) + start
    if kind == "diag":
        allowed = allowed & (key <= lax.broadcasted_iota(jnp.int32, (WINDOW, BLOCK), 1) + q0)
    elif kind == "left":
        allowed = allowed & (key < bound)
    else:
        allowed = allowed & (key >= bound)
    return jnp.where(allowed, 0.0, MASKED)


def window(causal, first_ref, r, qb, c, length):
    if causal:
        end = (qb + 1) * BLOCK - c * WINDOW
        return pl.multiple_of(jnp.maximum(end - WINDOW, 0), BLOCK), end
    begin = first_ref[r, qb] + c * WINDOW
    return pl.multiple_of(jnp.minimum(begin, length - WINDOW), 16), begin


def lanes_at(offset, p):
    return slice(offset + 128 * p, offset + 128 * p + 128)


UNROLL = 2


def bias_pair(cols, seg_row, q0, start, bound, kind):
    bias = bias_of(cols[pl.ds(start, WINDOW), :], seg_row, q0, start, bound, kind)
    return jnp.concatenate([bias, bias], axis=1)


def attend(causal, r, first_ref, extra_ref, q, k, v, qseg_ref, cols, out_ref, lse_ref, top, total, mix):
    length = q[0].shape[0]
    masks = lane_masks(0.125)
    kinds = ("diag", "left") if causal else ("from", "from")

    def windows(qbs, c, kind):
        scores, values = [], []
        for qb in qbs:
            q0 = pl.multiple_of(qb * BLOCK, BLOCK)
            start, bound = window(causal, first_ref, r, qb, c, length)
            bias = bias_pair(cols, qseg_ref[0, :, pl.ds(q0, BLOCK)], q0, start, bound, kind)
            for p in range(4):
                qs = stacked(q[0][pl.ds(q0, BLOCK), lanes_at(q[1], p)], masks)
                scores.append(mxu(k[0][pl.ds(start, WINDOW), lanes_at(k[1], p)], qs, NT) + bias)
                values.append(v[0][pl.ds(start, WINDOW), lanes_at(v[1], p)])
        return scores, values

    def step(i, _):
        qbs = [i * UNROLL + u for u in range(UNROLL)]
        scores, values = windows(qbs, 0, kinds[0])
        highs = [jnp.max(x, axis=0, keepdims=True) for x in scores]
        weights = [jnp.exp(x - high) for x, high in zip(scores, highs)]
        sums = [jnp.sum(x, axis=0, keepdims=True) for x in weights]
        mixed = [pick(mxu(val, low(x), TN)) for val, x in zip(values, weights)]
        for n in range(4 * UNROLL):
            top[n] = highs[n]
            total[n] = sums[n]
            mix[n] = mixed[n]
        for u, qb in enumerate(qbs):
            def more(c, _, u=u, qb=qb):
                scores, values = windows([qb], c + 1, kinds[1])
                highs = [jnp.maximum(top[4 * u + p], jnp.max(x, axis=0, keepdims=True)) for p, x in enumerate(scores)]
                weights = [jnp.exp(x - high) for x, high in zip(scores, highs)]
                mixed = [pick(mxu(val, low(x), TN)) for val, x in zip(values, weights)]
                for p in range(4):
                    n = 4 * u + p
                    fade = jnp.exp(top[n] - highs[p])
                    top[n] = highs[p]
                    total[n] = total[n] * fade + jnp.sum(weights[p], axis=0, keepdims=True)
                    mix[n] = mix[n] * pick(jnp.broadcast_to(fade, (128, 2 * BLOCK))) + mixed[p]
                return 0

            lax.fori_loop(0, extra_ref[r, qb], more, 0)
        for u, qb in enumerate(qbs):
            q0 = pl.multiple_of(qb * BLOCK, BLOCK)
            for p in range(4):
                sums = total[4 * u + p]
                inverse = pick(jnp.broadcast_to(1.0 / sums, (128, 2 * BLOCK)))
                out_ref[pl.ds(q0, BLOCK), lanes_at(0, p)] = low(jnp.transpose(mix[4 * u + p] * inverse))
                lse = top[4 * u + p] + jnp.log(sums)
                lse_ref[0, 2 * p:2 * p + 1, pl.ds(q0, BLOCK)] = lse[:, :BLOCK]
                lse_ref[0, 2 * p + 1:2 * p + 2, pl.ds(q0, BLOCK)] = lse[:, BLOCK:]
        return 0

    lax.fori_loop(0, length // BLOCK // UNROLL, step, 0)


ATTEND_SCRATCH = lambda length: [
    pltpu.VMEM((length, 128), F32), pltpu.VMEM((4 * UNROLL, 1, 2 * BLOCK), F32),
    pltpu.VMEM((4 * UNROLL, 1, 2 * BLOCK), F32), pltpu.VMEM((4 * UNROLL, 128, BLOCK), F32)]


def norm(hidden):
    average = jnp.mean(hidden, axis=-1, keepdims=True)
    centred = hidden - average
    inverse = lax.rsqrt(jnp.mean(centred * centred, axis=-1, keepdims=True) + EPSILON)
    return centred * inverse, inverse


def norm_back(grad, normed, inverse, gain):
    scaled = grad * gain
    return inverse * (scaled - jnp.mean(scaled, axis=-1, keepdims=True)
                      - normed * jnp.mean(scaled * normed, axis=-1, keepdims=True))


def sum_rows(x):
    return jnp.sum(wide(x), axis=0, keepdims=True)


S_BIAS, S_GAIN, S_SHIFT, C_BIAS, C_GAIN, C_SHIFT, I_BIAS, O_BIAS, F_GAIN, F_SHIFT = range(10)


def vec(ref, row, block=0, size=512):
    return ref[row:row + 1, block * size:(block + 1) * size]


def self_kernel(first_ref, extra_ref, x_ref, w_ref, vec_ref, seg_ref, qkv_ref, mix_ref, lse_ref, cols, *state):
    r = pl.program_id(0)
    cols[...] = columns_of(seg_ref[0])
    x = x_ref[...]
    qkv_ref[:, :512] = low(mxu(x, w_ref[:, :512]) + vec(vec_ref, S_BIAS, 0))
    qkv_ref[:, 512:1024] = low(mxu(x, w_ref[:, 512:1024]))
    qkv_ref[:, 1024:] = low(mxu(x, w_ref[:, 1024:]) + vec(vec_ref, S_BIAS, 1))
    attend(True, r, first_ref, extra_ref, (qkv_ref, 0), (qkv_ref, 512), (qkv_ref, 1024), seg_ref, cols, mix_ref, lse_ref, *state)


def self_forward(plan, x, w, vectors, seg):
    rows, _, length = seg.shape
    return pl.pallas_call(
        self_kernel, grid=(rows,),
        in_specs=[smem(), smem(), tiled(length, 512), fixed((512, 1536), 0, 0), fixed((16, 2048), 0, 0),
                  pl.BlockSpec((1, 1, length), lambda i: (i, 0, 0))],
        out_specs=[tiled(length, 1536), tiled(length, 512), pl.BlockSpec((1, 8, length), lambda i: (i, 0, 0))],
        out_shape=[shape_of((rows * length, 1536)), shape_of((rows * length, 512)), shape_of((rows, 8, length), F32)],
        scratch_shapes=ATTEND_SCRATCH(length), compiler_params=params(40), cost_estimate=cost(20), name="self_forward",
    )(*plan, x, w, vectors, seg)


def cross_kernel(first_ref, extra_ref, x_ref, mix_ref, mem_ref, wo_ref, wq_ref, wkv_ref, vec_ref, qseg_ref, kseg_ref,
                 hid_ref, q_ref, kv_ref, out_ref, lse_ref, cols, *state):
    r = pl.program_id(0)
    cols[...] = columns_of(kseg_ref[0])
    hidden = wide(x_ref[...]) + mxu(mix_ref[...], wo_ref[...]) + vec(vec_ref, S_BIAS, 2)
    hid_ref[...] = hidden
    first = low(norm(hidden)[0] * vec(vec_ref, S_GAIN) + vec(vec_ref, S_SHIFT))
    q_ref[...] = low(mxu(first, wq_ref[...]) + vec(vec_ref, C_BIAS, 0))
    mem = mem_ref[...]
    kv_ref[:, :512] = low(mxu(mem, wkv_ref[:, :512]))
    kv_ref[:, 512:] = low(mxu(mem, wkv_ref[:, 512:]) + vec(vec_ref, C_BIAS, 1))
    attend(False, r, first_ref, extra_ref, (q_ref, 0), (kv_ref, 0), (kv_ref, 512), qseg_ref, cols, out_ref, lse_ref, *state)


def cross_forward(plan, x, mix, mem, rest, vectors, qseg, kseg):
    rows, _, length = qseg.shape
    seg = pl.BlockSpec((1, 1, length), lambda i: (i, 0, 0))
    total = rows * length
    return pl.pallas_call(
        cross_kernel, grid=(rows,),
        in_specs=[smem(), smem(), tiled(length, 512), tiled(length, 512), tiled(length, 512),
                  fixed((512, 512), 0, 10), fixed((512, 512), 0, 11), fixed((512, 1024), 0, 4), fixed((16, 2048), 0, 0), seg, seg],
        out_specs=[tiled(length, 512), tiled(length, 512), tiled(length, 1024), tiled(length, 512),
                   pl.BlockSpec((1, 8, length), lambda i: (i, 0, 0))],
        out_shape=[shape_of((total, 512), F32), shape_of((total, 512)), shape_of((total, 1024)), shape_of((total, 512)),
                   shape_of((rows, 8, length), F32)],
        scratch_shapes=ATTEND_SCRATCH(length), compiler_params=params(48), cost_estimate=cost(25), name="cross_forward",
    )(*plan, x, mix, mem, rest, rest, rest, vectors, qseg, kseg)


def back_kernel(causal, row, first_ref, extra_ref, q_ref, k_ref, v_ref, mix_ref, grad_ref, lse_ref, qseg_ref, kseg_ref, *refs):
    dq_ref, dk_ref, dv_ref, cols, dk, dv, dq = refs[-7:]
    r = row
    length = q_ref.shape[0]
    cols[...] = columns_of(kseg_ref[0])
    dk[...] = jnp.zeros_like(dk)
    dv[...] = jnp.zeros_like(dv)
    masks = lane_masks(0.125)
    ones = lane_masks(1.0)
    pair_rows = jnp.concatenate([ones[0], ones[1], jnp.zeros((14, 128), BF)], axis=0)

    kinds = ("diag", "left") if causal else ("from", "from")

    def windows(qbs, c, kind):
        places, qs, gs, deltas, lses, keys, biases = [], [], [], [], [], [], []
        for qb in qbs:
            q0 = pl.multiple_of(qb * BLOCK, BLOCK)
            start, bound = window(causal, first_ref, r, qb, c, length)
            bias = bias_pair(cols, qseg_ref[0, :, pl.ds(q0, BLOCK)], q0, start, bound, kind)
            for p in range(4):
                lanes = lanes_at(0, p)
                grad = grad_ref[pl.ds(q0, BLOCK), lanes]
                prod = wide(grad) * wide(mix_ref[pl.ds(q0, BLOCK), lanes])
                upper = low(prod)
                delta = mxu(pair_rows, upper, NT) + mxu(pair_rows, low(prod - wide(upper)), NT)
                deltas.append(jnp.concatenate([delta[0:1], delta[1:2]], axis=1))
                lses.append(jnp.concatenate([lse_ref[0, 2 * p:2 * p + 1, pl.ds(q0, BLOCK)],
                                             lse_ref[0, 2 * p + 1:2 * p + 2, pl.ds(q0, BLOCK)]], axis=1))
                qs.append(stacked(q_ref[pl.ds(q0, BLOCK), lanes], masks))
                gs.append(stacked(grad, ones))
                keys.append(k_ref[pl.ds(start, WINDOW), lanes])
                places.append((pl.ds(start, WINDOW), lanes))
                biases.append(bias)
        scores = [mxu(key, x, NT) for key, x in zip(keys, qs)]
        dprobs = [mxu(v_ref[place], g, NT) for place, g in zip(places, gs)]
        probs = [jnp.exp(x + bias - lse) for x, bias, lse in zip(scores, biases, lses)]
        dscores = [low(x * (d - delta)) for x, d, delta in zip(probs, dprobs, deltas)]
        new_dv = [mxu(low(x), g) for x, g in zip(probs, gs)]
        new_dk = [mxu(d, x) for d, x in zip(dscores, qs)]
        parts = [pick(mxu(key, d, TN)) for key, d in zip(keys, dscores)]
        for place, more_dv, more_dk in zip(places, new_dv, new_dk):
            dv[place] += more_dv
            dk[place] += more_dk
        return parts

    def step(i, _):
        qbs = [i * UNROLL + u for u in range(UNROLL)]
        for n, part in enumerate(windows(qbs, 0, kinds[0])):
            dq[n] = part
        for u, qb in enumerate(qbs):
            def more(c, _, u=u, qb=qb):
                for p, part in enumerate(windows([qb], c + 1, kinds[1])):
                    dq[4 * u + p] += part
                return 0

            lax.fori_loop(0, extra_ref[r, qb], more, 0)
        for u, qb in enumerate(qbs):
            q0 = pl.multiple_of(qb * BLOCK, BLOCK)
            for p in range(4):
                dq_ref[pl.ds(q0, BLOCK), lanes_at(0, p)] = low(jnp.transpose(dq[4 * u + p]) * 0.125)
        return 0

    lax.fori_loop(0, length // BLOCK // UNROLL, step, 0)
    dk_ref[...] = low(dk[...])
    dv_ref[...] = low(dv[...])


def attend_back(causal, row, plan, q, k, v, mix, grad, lse, qseg, kseg, before, after=()):
    rows, _, length = qseg.shape
    spec = lambda col: pl.BlockSpec((length, 512), lambda i, col=col: (row, col))
    seg = pl.BlockSpec((1, 1, length), lambda i: (row, 0, 0))
    out = pl.BlockSpec((length, 512), lambda i: (row, 0))
    extra = tuple(before) + tuple(after)
    return pl.pallas_call(
        functools.partial(back_kernel, causal, row), grid=(1,),
        in_specs=[smem(), smem(), spec(q[1]), spec(k[1]), spec(v[1]), spec(0), spec(0),
                  pl.BlockSpec((1, 8, length), lambda i: (row, 0, 0)), seg, seg]
        + [pl.BlockSpec(memory_space=pl.ANY)] * len(extra),
        out_specs=[out] * 3, out_shape=[shape_of((rows * length, 512))] * 3,
        input_output_aliases={10 + i: i for i in range(len(before))},
        scratch_shapes=[pltpu.VMEM((length, 128), F32), pltpu.VMEM((length, 512), F32),
                        pltpu.VMEM((length, 512), F32), pltpu.VMEM((4 * UNROLL, 128, BLOCK), F32)],
        compiler_params=params(40), cost_estimate=cost(14), name="self_back" if causal else "cross_back",
    )(*plan, q[0], k[0], v[0], mix, grad, lse, qseg, kseg, *extra)


def emit(outs, col, acc, index_ref, acc_col, width):
    half = outs[0].shape[0]
    for r in range(512 // UNIT):
        row = pl.multiple_of(index_ref[r] * UNIT, UNIT)
        outs[r // half][r % half, :, col:col + width] = low(acc[pl.ds(row, UNIT), acc_col:acc_col + width])


def halves(width):
    half = 512 // UNIT // 2
    return [fixed((half, UNIT, width), 0, 0, 0)] * 2, [shape_of((half, UNIT, width))] * 2


MID_TILE = 512
PARTS = 2
CHUNK = 1024


def mid_kernel(index_a, index_b, hid_ref, mix_ref, grad_ref, win_ref, gout_ref, wco_ref, vec_ref,
               out_ref, h2_ref, mg_ref, keep_ref, send_ref, co_ref, small_ref,
               wout, dwin, dwout, dwco, act, slope):
    step = pl.program_id(0)
    hidden_width = win_ref.shape[1]
    tokens = hid_ref.shape[0]

    @pl.when(step == 0)
    def _():
        for d in range(512 // UNIT):
            for b in range(4):
                wout[(4 * d + b) * UNIT:(4 * d + b + 1) * UNIT, :] = gout_ref[d * UNIT:(d + 1) * UNIT, 512 * b:512 * b + 512]
        dwin[...] = jnp.zeros_like(dwin)
        dwout[...] = jnp.zeros_like(dwout)
        dwco[...] = jnp.zeros_like(dwco)
        small_ref[...] = jnp.zeros_like(small_ref)

    chunks = [slice(c, c + CHUNK) for c in range(0, hidden_width, CHUNK)]
    part = tokens // PARTS
    parts = [slice(i * part, i * part + part) for i in range(PARTS)]
    firsts = [norm(hid_ref[t, :])[0] * vec(vec_ref, S_GAIN) + vec(vec_ref, S_SHIFT) for t in parts]
    norms2 = [norm(first + mxu(mix_ref[t, :], wco_ref[...]) + vec(vec_ref, C_BIAS, 2)) for t, first in zip(parts, firsts)]
    seconds = [normed * vec(vec_ref, C_GAIN) + vec(vec_ref, C_SHIFT) for normed, _ in norms2]
    lows = [low(second) for second in seconds]
    norms3 = []
    for t, second, second_low in zip(parts, seconds, lows):
        hidden3 = second + vec(vec_ref, O_BIAS)
        for c in chunks:
            pre = mxu(second_low, win_ref[:, c]) + vec_ref[I_BIAS:I_BIAS + 1, c]
            sig = 0.5 + 0.5 * jnp.tanh(0.5 * pre)
            active = low(pre * sig)
            act[t, c] = active
            slope[t, c] = sig * (1.0 + pre * (1.0 - sig))
            hidden3 += mxu(active, wout[c, :])
        norms3.append(norm(hidden3))
    backs3 = []
    for t, (normed3, inverse3) in zip(parts, norms3):
        out_ref[t, :] = low(normed3 * vec(vec_ref, F_GAIN) + vec(vec_ref, F_SHIFT))
        grad = wide(grad_ref[t, :])
        backs3.append(norm_back(grad, normed3, inverse3, vec(vec_ref, F_GAIN)))
        small_ref[2:3, :512] += sum_rows(grad * normed3)
        small_ref[3:4, :512] += sum_rows(grad)
    b3s = [low(back3) for back3 in backs3]
    us = [[] for _ in chunks]
    grads2 = []
    for t, back3, b3 in zip(parts, backs3, b3s):
        grad2 = back3
        for n, c in enumerate(chunks):
            u = low(mxu(b3, wout[c, :], NT) * slope[t, c])
            us[n].append(u)
            grad2 += mxu(u, win_ref[:, c], NT)
        grads2.append(grad2)
    b2s = []
    for t, grad2, (normed2, inverse2) in zip(parts, grads2, norms2):
        h2 = norm_back(grad2, normed2, inverse2, vec(vec_ref, C_GAIN))
        h2_ref[t, :] = h2
        b2 = low(h2)
        b2s.append(b2)
        small_ref[4:5, :512] += sum_rows(grad2 * normed2)
        small_ref[5:6, :512] += sum_rows(grad2)
    second_low = jnp.concatenate(lows, axis=0)
    b3 = jnp.concatenate(b3s, axis=0)
    second_t, b3_t = jnp.transpose(second_low), jnp.transpose(b3)
    small_ref[1:2, :512] += sum_rows(b3)
    for n, c in enumerate(chunks):
        u = jnp.concatenate(us[n], axis=0)
        dwin[:, c] += mxu(second_t, u)
        dwout[:, c] += mxu(b3_t, act[:, c])
        small_ref[0:1, c] += sum_rows(u)
    b2 = jnp.concatenate(b2s, axis=0)
    small_ref[6:7, :512] += sum_rows(b2)
    dwco[...] += mxu(jnp.transpose(mix_ref[...]), b2)
    mg_ref[...] = low(mxu(b2, wco_ref[...], NT))

    @pl.when(step == pl.num_programs(0) - 1)
    def _():
        outs = keep_ref, send_ref
        emit(outs, 0, dwin, index_a, 0, hidden_width)
        for c in chunks:
            wout[c, :] = low(jnp.transpose(dwout[:, c]))
        half = keep_ref.shape[0]
        for r in range(512 // UNIT):
            for b in range(4):
                row = pl.multiple_of((index_b[r] * 4 + b) * UNIT, UNIT)
                outs[r // half][r % half, :, 2048 + 512 * b:2560 + 512 * b] = wout[pl.ds(row, UNIT), :]
        co_ref[...] = dwco[...]


def middle(index_a, index_b, hid, mix, grad, rest, vectors):
    total = hid.shape[0]
    t = MID_TILE
    specs, shapes = halves(4096)
    return pl.pallas_call(
        mid_kernel, grid=(total // t,),
        in_specs=[smem(), smem(), tiled(t, 512), tiled(t, 512), tiled(t, 512),
                  fixed((512, 2048), 0, 0), fixed((512, 2048), 0, 1), fixed((512, 512), 0, 12), fixed((16, 2048), 0, 0)],
        out_specs=[tiled(t, 512)] * 3 + specs + [fixed((512, 512), 0, 0), fixed((8, 2048), 0, 0)],
        out_shape=[shape_of((total, 512)), shape_of((total, 512), F32), shape_of((total, 512))] + shapes
        + [shape_of((512, 512), F32), shape_of((8, 2048), F32)],
        scratch_shapes=[pltpu.VMEM((2048, 512), BF), pltpu.VMEM((512, 2048), F32), pltpu.VMEM((512, 2048), F32),
                        pltpu.VMEM((512, 512), F32), pltpu.VMEM((t, 2048), BF), pltpu.VMEM((t, 2048), F32)],
        compiler_params=params(56), cost_estimate=cost(40), name="middle",
    )(index_a, index_b, hid, mix, grad, rest, rest, rest, vectors)


DENSE_TILE = 512
SELF_TILE = 1024


def cross_dense_kernel(index_a, index_b, cq_ref, ck_ref, cv_ref, mem_ref, hid_ref, h2_ref, mix_ref,
                       wq_ref, wkv_ref, wo_ref, co_ref, vec_ref,
                       memgrad_ref, h1_ref, mg_ref, keep_ref, send_ref, small_ref, dq, dkv, do):
    step = pl.program_id(0)

    @pl.when(step == 0)
    def _():
        dq[...] = jnp.zeros_like(dq)
        dkv[...] = jnp.zeros_like(dkv)
        do[...] = jnp.zeros_like(do)
        small_ref[...] = jnp.zeros_like(small_ref)

    cq, ck, cv = cq_ref[...], ck_ref[...], cv_ref[...]
    normed, inverse = norm(hid_ref[...])
    first = low(normed * vec(vec_ref, S_GAIN) + vec(vec_ref, S_SHIFT))
    grad1 = h2_ref[...] + mxu(cq, wq_ref[...], NT)
    h1 = norm_back(grad1, normed, inverse, vec(vec_ref, S_GAIN))
    h1_ref[...] = h1
    b1 = low(h1)
    mg_ref[...] = low(mxu(b1, wo_ref[...], NT))
    memgrad_ref[...] = low(mxu(ck, wkv_ref[:, :512], NT) + mxu(cv, wkv_ref[:, 512:], NT))
    dq[...] += mxu(jnp.transpose(first), cq)
    mem_t = jnp.transpose(mem_ref[...])
    dkv[:, :512] += mxu(mem_t, ck)
    dkv[:, 512:] += mxu(mem_t, cv)
    do[...] += mxu(jnp.transpose(mix_ref[...]), b1)
    small_ref[0:1, :] += sum_rows(cq)
    small_ref[1:2, :] += sum_rows(cv)
    small_ref[2:3, :] += sum_rows(grad1 * normed)
    small_ref[3:4, :] += sum_rows(grad1)
    small_ref[4:5, :] += sum_rows(b1)

    @pl.when(step == pl.num_programs(0) - 1)
    def _():
        outs = keep_ref, send_ref
        emit(outs, 0, dq, index_a, 0, 512)
        emit(outs, 512, co_ref, index_a, 0, 512)
        emit(outs, 1024, do, index_a, 0, 256)
        emit(outs, 1280, do, index_b, 256, 256)
        emit(outs, 1536, dkv, index_b, 0, 1024)


def cross_dense(index_a, index_b, grads, mem, hid, h2, mix, rest, dco, vectors):
    total = hid.shape[0]
    t = DENSE_TILE
    specs, shapes = halves(2560)
    return pl.pallas_call(
        cross_dense_kernel, grid=(total // t,),
        in_specs=[smem(), smem()] + [tiled(t, 512)] * 7
        + [fixed((512, 512), 0, 11), fixed((512, 1024), 0, 4), fixed((512, 512), 0, 10), fixed((512, 512), 0, 0), fixed((16, 2048), 0, 0)],
        out_specs=[tiled(t, 512)] * 3 + specs + [fixed((8, 512), 0, 0)],
        out_shape=[shape_of((total, 512)), shape_of((total, 512), F32), shape_of((total, 512))] + shapes + [shape_of((8, 512), F32)],
        scratch_shapes=[pltpu.VMEM((512, 512), F32), pltpu.VMEM((512, 1024), F32), pltpu.VMEM((512, 512), F32)],
        compiler_params=params(40), cost_estimate=cost(12), name="cross_dense",
    )(index_a, index_b, *grads, mem, hid, h2, mix, rest, rest, rest, dco, vectors)


VECTORS = (1536, 512, 512, 1536, 512, 512, 2048, 512, 512, 512)


def places(n, per, count, axis):
    shape = (1, n)
    at = wide(lax.broadcasted_iota(jnp.int32, shape, 1))
    owner = jnp.floor((at + 0.5) * (1.0 / per))
    return owner, at - owner * per


def one_hot(n, per):
    _, place = places(n, per, n // per, 1)
    return low(jnp.where(wide(lax.broadcasted_iota(jnp.int32, (128, n), 0)) == place, 1.0, 0.0))


def owned(n, per, count):
    owner, _ = places(n, per, count, 1)
    return wide(lax.broadcasted_iota(jnp.int32, (count, n), 0)) == owner


def self_grad_kernel(count, index_a, index_b, dq_ref, dk_ref, dv_ref, x_ref, mid_ref, small_ref, keep_ref, send_ref, lines_ref, dw, table):
    step = pl.program_id(0)

    @pl.when(step == 0)
    def _():
        dw[...] = jnp.zeros_like(dw)
        lines_ref[...] = jnp.zeros_like(lines_ref)

    x_t = jnp.transpose(x_ref[...])
    dw[:, :512] += mxu(x_t, dq_ref[...])
    dw[:, 512:1024] += mxu(x_t, dk_ref[...])
    dw[:, 1024:] += mxu(x_t, dv_ref[...])
    lines_ref[S_BIAS:S_BIAS + 1, :512] += sum_rows(dq_ref[...])
    lines_ref[S_BIAS:S_BIAS + 1, 512:1024] += sum_rows(dv_ref[...])

    @pl.when(step == pl.num_programs(0) - 1)
    def _():
        outs = keep_ref, send_ref
        emit(outs, 0, dw, index_a, 0, 768)
        emit(outs, 896, dw, index_b, 768, 768)
        for row, col, source, source_row in (
            (S_BIAS, 1024, small_ref, 4), (S_GAIN, 0, small_ref, 2), (S_SHIFT, 0, small_ref, 3),
            (C_BIAS, 0, small_ref, 0), (C_BIAS, 512, small_ref, 1), (C_BIAS, 1024, mid_ref, 6),
            (C_GAIN, 0, mid_ref, 4), (C_SHIFT, 0, mid_ref, 5),
            (O_BIAS, 0, mid_ref, 1), (F_GAIN, 0, mid_ref, 2), (F_SHIFT, 0, mid_ref, 3),
        ):
            lines_ref[row:row + 1, col:col + 512] = source[source_row:source_row + 1, :512]
        lines_ref[I_BIAS:I_BIAS + 1, :] = mid_ref[0:1, :]
        if count:
            table[...] = jnp.zeros_like(table)
            for n in (512, 1536, 2048):
                hot, mine = one_hot(n, n // count), owned(n, n // count, count)
                for j, size in enumerate(VECTORS):
                    if size == n:
                        line = jnp.broadcast_to(lines_ref[j:j + 1, :n], (count, n))
                        table[:, j, :] = mxu(low(jnp.where(mine, line, 0.0)), hot, NT)
            for r in range(count):
                outs[2 * r // count][r % (count // 2), :, 768:896] = low(table[index_a[r]])


def self_grad(count, index_a, index_b, grads, x, mid_small, small):
    total = x.shape[0]
    t = SELF_TILE
    specs, shapes = halves(1664)
    return pl.pallas_call(
        functools.partial(self_grad_kernel, count), grid=(total // t,),
        in_specs=[smem(), smem()] + [tiled(t, 512)] * 4 + [fixed((8, 2048), 0, 0), fixed((8, 512), 0, 0)],
        out_specs=specs + [fixed((16, 2048), 0, 0)],
        out_shape=shapes + [shape_of((16, 2048), F32)],
        scratch_shapes=[pltpu.VMEM((512, 1536), F32), pltpu.VMEM((max(count, 8), 16, 128), F32)],
        compiler_params=params(40), cost_estimate=cost(5), name="self_grad",
    )(index_a, index_b, *grads, x, mid_small, small)


def target_kernel(h1_ref, dq_ref, dk_ref, dv_ref, w_ref, *refs):
    out_ref = refs[-1]
    total = h1_ref[...] + mxu(dq_ref[...], w_ref[:, :512], NT)
    total += mxu(dk_ref[...], w_ref[:, 512:1024], NT)
    out_ref[...] = low(total + mxu(dv_ref[...], w_ref[:, 1024:], NT))


def target_grad(h1, grads, w, after=()):
    total = h1.shape[0]
    t = 512
    return pl.pallas_call(
        target_kernel, grid=(total // t,), in_specs=[tiled(t, 512)] * 4 + [fixed((512, 1536), 0, 0)]
        + [pl.BlockSpec(memory_space=pl.ANY)] * len(after),
        out_specs=tiled(t, 512), out_shape=shape_of((total, 512)), compiler_params=params(40), cost_estimate=cost(5), name="target_grad",
    )(h1, *grads, w, *after)


class Net:
    def __init__(self):
        self.wide = lax.axis_size("wide")
        self.narrow = lax.axis_size("narrow")
        self.count = self.wide * self.narrow
        self.wide_bits = self.wide.bit_length() - 1
        self.narrow_bits = self.narrow.bit_length() - 1
        self.bits = self.wide_bits + self.narrow_bits
        self.me = lax.axis_index("wide") * self.narrow + lax.axis_index("narrow")
        inner = list(range(self.narrow_bits))
        core, second = [self.narrow_bits], [self.narrow_bits + 1]
        far = list(range(self.narrow_bits + 2, self.bits))
        self.near = self.bits - len(far)
        self.orders = (core + second + inner + far, core + inner + second + far)

    def exchange(self, x, bit):
        if bit < self.narrow_bits:
            return lax.ppermute(x, "narrow", [(i, i ^ (1 << bit)) for i in range(self.narrow)])
        bit -= self.narrow_bits
        return lax.ppermute(x, "wide", [(i, i ^ (1 << bit)) for i in range(self.wide)])

    def index(self, chain):
        order, n = self.orders[chain], self.bits
        mask = [sum(((r >> (n - 1 - s)) & 1) << bit for s, bit in enumerate(order)) for r in range(self.count)]
        return jnp.array(mask, jnp.int32) ^ self.me

    def gather_index(self, chain):
        order = self.orders[chain][::-1]
        mask = [sum(((r >> s) & 1) << bit for s, bit in enumerate(order)) for r in range(self.count)]
        return jnp.array(mask, jnp.int32) ^ self.me


def pack_kernel(*refs):
    vectors, (qkv, so, cq, ckv, co, fin, fout, packed_ref, rest_ref) = refs[:10], refs[10:19]
    lines, sem = refs[19:29], refs[29]
    moves = list(zip(vectors, lines))
    moves += [(qkv.at[:, :768], packed_ref.at[0, :, :768]), (qkv.at[:, 768:], packed_ref.at[0, :, 896:]), (fin, rest_ref.at[:, :2048])]
    moves += [(fout.at[UNIT * b:UNIT * b + UNIT, :], rest_ref.at[:, 2048 + 512 * b:2560 + 512 * b]) for b in range(4)]
    moves += [(ckv, rest_ref.at[:, 4096:5120]), (so, rest_ref.at[:, 5120:5632]),
              (cq, rest_ref.at[:, 5632:6144]), (co, rest_ref.at[:, 6144:])]
    copies = [pltpu.make_async_copy(src, dst, sem.at[i]) for i, (src, dst) in enumerate(moves)]
    for copy in copies:
        copy.start()
    for copy in copies:
        copy.wait()
    rows = []
    for v in lines:
        line = wide(v[...])
        rows.append(jnp.concatenate([line, jnp.zeros((1, 128 - line.shape[1]), F32)], axis=1))
    rows.append(jnp.zeros((6, 128), F32))
    packed_ref[0, :, 768:896] = low(jnp.concatenate(rows, axis=0))


def unpack_kernel(count, index_a, index_b, *refs):
    n = (len(refs) - 3) // 2
    pieces_a, pieces_b, (w_ref, vec_ref, table) = refs[:n], refs[n:2 * n], refs[2 * n:]
    for pieces, index, col, width in ((pieces_a, index_a, 0, 768), (pieces_b, index_b, 768, 768)):
        r = 0
        for piece in pieces:
            for j in range(piece.shape[0]):
                owner = index[r]
                w_ref[pl.ds(pl.multiple_of(owner * UNIT, UNIT), UNIT), col:col + width] = piece[j, :, :width]
                if col == 0:
                    table[owner] = wide(piece[j, :, 768:896])
                r += 1
    vec_ref[...] = jnp.zeros_like(vec_ref)
    for n in (512, 1536, 2048):
        hot, mine = one_hot(n, n // count), owned(n, n // count, count)
        for j, size in enumerate(VECTORS):
            if size == n:
                spread = mxu(low(table[:, j, :]), hot)
                vec_ref[j:j + 1, :n] = jnp.sum(jnp.where(mine, spread, 0.0), axis=0, keepdims=True)


def gather_weights(net, small, big):
    qkv, so, cq, ckv, co, fin, fout = big
    if qkv.shape[0] % UNIT or net.bits < 5:
        small, big = lax.all_gather((small, big), AXES, axis=0, tiled=True) if net.count > 1 else (small, big)
        qkv, so, cq, ckv, co, fin, fout = big
        fout = fout.reshape(-1, 4, UNIT, 512).transpose(0, 2, 1, 3).reshape(512, 2048)
        rows = [jnp.pad(wide(v), (0, 2048 - v.shape[0])) for v in small]
        vectors = jnp.stack(rows + [jnp.zeros((2048,), F32)] * 6)
        return qkv, vectors, jnp.concatenate([fin, fout, ckv, so, cq, co], axis=1)
    packed, rest = pl.pallas_call(
        pack_kernel, in_specs=[pl.BlockSpec(memory_space=pl.ANY)] * 17, out_specs=[vmem()] * 2,
        out_shape=[shape_of((1, UNIT, 1664)), shape_of((UNIT, 6656))],
        scratch_shapes=[pltpu.VMEM((1, v.shape[0]), BF) for v in small] + [pltpu.SemaphoreType.DMA((21,))],
        compiler_params=params(60), cost_estimate=cost(2), name="pack",
    )(*[v[None] for v in small], *big)
    rest = lax.all_gather(rest, AXES, axis=0, tiled=True)
    orders = [order[::-1] for order in net.orders]
    far = net.bits - net.near
    for bit in orders[0][:far]:
        packed = jnp.concatenate([packed, net.exchange(packed, bit)], axis=0)
    both = [packed[:, :, :896], packed[:, :, 896:]]
    both = [jnp.concatenate([x, net.exchange(x, order[far])], axis=0) for x, order in zip(both, orders)]
    pieces = [[x] for x in both]
    for s in (far + 1, far + 2):
        got = [[net.exchange(x, order[s]) for x in chain] for chain, order in zip(pieces, orders)]
        pieces = [chain + more for chain, more in zip(pieces, got)]
    w, vectors = pl.pallas_call(
        functools.partial(unpack_kernel, net.count), in_specs=[smem(), smem()] + [vmem()] * (len(pieces[0]) * 2), out_specs=[vmem()] * 2,
        out_shape=[shape_of((512, 1536)), shape_of((16, 2048), F32)],
        scratch_shapes=[pltpu.VMEM((net.count, 16, 128), F32)],
        compiler_params=params(40), cost_estimate=cost(2), name="unpack",
    )(net.gather_index(0), net.gather_index(1), *pieces[0], *pieces[1])
    return w, vectors, rest


class Reduction:
    def __init__(self, net, keep, send, cut):
        self.net, self.cut = net, cut
        self.keep, self.send = [keep], [send]
        self.stage = 0
        self.sums = None

    def state(self):
        return tuple(self.send) if self.sums is None else ()

    def start(self):
        if self.sums is None:
            self.got = [self.net.exchange(x, order[self.stage]) for x, order in zip(self.send, self.net.orders)]

    def add(self):
        if self.sums is not None:
            return
        self.stage += 1
        sums = [wide(k) + wide(g) for k, g in zip(self.keep, self.got)]
        if self.stage == self.net.bits:
            self.sums = sums[0][0]
            return
        if self.stage == 1:
            sums = [sums[0][:, :, :self.cut], sums[0][:, :, self.cut:]]
        elif self.stage == self.net.near:
            sums = [jnp.concatenate(sums, axis=2)]
        half = sums[0].shape[0] // 2
        self.keep = [low(s[:half]) for s in sums]
        self.send = [low(s[half:]) for s in sums]


def together(groups):
    if groups:
        state = lax.optimization_barrier([(group.keep, group.send) for group in groups])
        for group, (keep, send) in zip(groups, state):
            group.keep, group.send = keep, send


def plan_self(seg, positions):
    rows, length = seg.shape
    starts = jnp.arange(0, length, BLOCK, dtype=jnp.int32)
    begin = starts[None, :] - positions[:, ::BLOCK]
    left = jnp.maximum(starts[None, :] + BLOCK - WINDOW - begin, 0)
    return jnp.zeros_like(begin), (left + WINDOW - 1) // WINDOW


def plan_cross(tseg, sseg):
    last = jnp.int32(1 << 20)
    tkey = jnp.where(tseg == 0, last, tseg)
    skey = jnp.where(sseg == 0, last, sseg)
    begin = jnp.sum(skey[:, None, :] < tkey[:, ::BLOCK, None], axis=2, dtype=jnp.int32)
    end = jnp.sum(skey[:, None, :] <= tkey[:, BLOCK - 1::BLOCK, None], axis=2, dtype=jnp.int32)
    first = (begin // 16) * 16
    return first, jnp.maximum((end - first + WINDOW - 1) // WINDOW - 1, 0)


def per_device(
    target, memory, out_grad, target_segments, source_segments, target_positions,
    self_qkv, self_out, cross_query, cross_kv, cross_out, ffn_in, ffn_out, *small,
):
    net = Net()
    rows = target_segments.shape[0]
    fast = self_qkv.shape[0] % UNIT == 0 and net.bits >= 5
    self_plan = plan_self(target_segments, target_positions)
    cross_plan = plan_cross(target_segments, source_segments)
    tseg = wide(target_segments)[:, None, :]
    sseg = wide(source_segments)[:, None, :]
    w_qkv, vectors, rest = gather_weights(net, small, (self_qkv, self_out, cross_query, cross_kv, cross_out, ffn_in, ffn_out))
    if fast:
        index_a, index_b = net.index(0), net.index(1)
    else:
        index_a = index_b = jnp.arange(512 // UNIT, dtype=jnp.int32)

    qkv, self_mix, self_lse = self_forward(self_plan, target, w_qkv, vectors, tseg)
    hid, cq, pairs, cross_mix, cross_lse = cross_forward(cross_plan, target, self_mix, memory, rest, vectors, tseg, sseg)
    output, h2, cross_mg, ffn_keep, ffn_send, dco, mid_small = middle(index_a, index_b, hid, cross_mix, out_grad, rest, vectors)

    groups = [Reduction(net, ffn_keep, ffn_send, 2048)] if fast else []

    def backward(causal, plan, q, k, v, mix, grad, lse, kseg):
        out = ()
        for row in range(rows):
            tied = tuple(x for group in groups for x in group.state())
            for group in groups:
                group.start()
            out = attend_back(causal, row, plan, q, k, v, mix, grad, lse, tseg, kseg, out, tied)
            for group in groups:
                group.add()
        return out

    cross_grads = backward(False, cross_plan, (cq, 0), (pairs, 0), (pairs, 1), cross_mix, cross_mg, cross_lse, sseg)
    for group in groups:
        group.start()
    memory_grad, h1, self_mg, cross_keep, cross_send, small_sums = cross_dense(
        index_a, index_b, cross_grads, memory, hid, h2, self_mix, rest, dco, vectors)
    for group in groups:
        group.add()
    if fast:
        groups.append(Reduction(net, cross_keep, cross_send, 1280))
    self_grads = backward(True, self_plan, (qkv, 0), (qkv, 1), (qkv, 2), self_mix, self_mg, self_lse, tseg)
    self_keep, self_send, lines = self_grad(net.count if fast else 0, index_a, index_b, self_grads, target, mid_small, small_sums)

    if not fast:
        target_out = target_grad(h1, self_grads, w_qkv)
        total = lambda x: lax.psum_scatter(low(x), AXES, scatter_dimension=0, tiled=True).astype(F32) if net.count > 1 else wide(x)
        whole = lambda keep, send: jnp.concatenate([keep, send], axis=0).reshape(512, -1)
        d_self, d_cross, d_ffn = whole(self_keep, self_send), whole(cross_keep, cross_send), whole(ffn_keep, ffn_send)
        d_out = d_ffn[:, 2048:].reshape(-1, UNIT, 4, 512).transpose(0, 2, 1, 3).reshape(2048, 512)
        weights = (jnp.concatenate([d_self[:, :768], d_self[:, 896:]], axis=1), d_cross[:, 1024:1536],
                   d_cross[:, :512], d_cross[:, 1536:], d_cross[:, 512:1024], d_ffn[:, :2048], d_out)
        return (output, target_out, memory_grad, *[total(w) for w in weights], *[total(lines[j, :n]) for j, n in enumerate(VECTORS)])

    groups.append(Reduction(net, self_keep, self_send, 896))
    target_out = None
    while any(group.sums is None for group in groups):
        open_groups = [group for group in groups if group.sums is None]
        tied = tuple(x for group in open_groups for x in group.state())
        for group in open_groups:
            group.start()
        if groups[-1].stage == 1:
            target_out = target_grad(h1, self_grads, w_qkv, tied)
        for group in open_groups:
            group.add()
        together([group for group in open_groups if group.sums is None])
    d_ffn, d_cross, d_self = (group.sums for group in groups)
    vectors_out = [d_self[j, 768:768 + n // net.count] for j, n in enumerate(VECTORS)]
    return (
        output, target_out, memory_grad,
        jnp.concatenate([d_self[:, :768], d_self[:, 896:]], axis=1), d_cross[:, 1024:1536],
        d_cross[:, :512], d_cross[:, 1536:], d_cross[:, 512:1024],
        d_ffn[:, :2048], jnp.concatenate([d_ffn[:, 2048 + 512 * b:2560 + 512 * b] for b in range(4)], axis=0),
        *vectors_out,
    )


def solution(mesh):
    both = ("wide", "narrow")
    matrix, vector = P(both, None), P(both)
    return jax.shard_map(
        per_device, mesh=mesh,
        in_specs=(matrix,) * 13 + (vector,) * 10,
        out_specs=(matrix,) * 10 + (vector,) * 10,
        check_vma=False,
    )
```

```python
import functools

import jax
import jax.numpy as jnp
from jax import lax
from jax.experimental import pallas as pl
from jax.experimental.pallas import tpu as pltpu
from jax.sharding import PartitionSpec as P

MASKED = -1e30
EPSILON = 1e-05
BLOCK = 128
WINDOW = 256
UNIT = 16
AXES = ("wide", "narrow")
NT = (((1,), (1,)), ((), ()))
TN = (((0,), (0,)), ((), ()))
NN = (((1,), (0,)), ((), ()))
BF = jnp.bfloat16
F32 = jnp.float32


def mxu(a, b, dims=NN):
    return lax.dot_general(a, b, dims, preferred_element_type=F32)


def low(x):
    return x.astype(BF)


def wide(x):
    return x.astype(F32)


def shape_of(shape, dtype=BF):
    return jax.ShapeDtypeStruct(shape, dtype)


def smem():
    return pl.BlockSpec(memory_space=pltpu.SMEM)


def vmem():
    return pl.BlockSpec(memory_space=pltpu.VMEM)


def fixed(shape, *index):
    return pl.BlockSpec(shape, lambda i, index=index: index, pipeline_mode=pl.Buffered(1))


def tiled(rows, cols, col=0):
    return pl.BlockSpec((rows, cols), lambda i, col=col: (i, col))


def params(mib):
    return pltpu.CompilerParams(vmem_limit_bytes=mib << 20)


def cost(micros):
    return pl.CostEstimate(flops=int(micros * 1e9), bytes_accessed=1 << 20, transcendentals=0)


def lane_masks(scale):
    lane = lax.broadcasted_iota(jnp.int32, (1, 128), 1)
    return low(jnp.where(lane < 64, scale, 0.0)), low(jnp.where(lane < 64, 0.0, scale))


def stacked(pair, masks):
    return jnp.concatenate([pair * masks[0], pair * masks[1]], axis=0)


def pick(both):
    sub = lax.broadcasted_iota(jnp.int32, (128, BLOCK), 0)
    return jnp.where(sub < 64, both[:, :BLOCK], both[:, BLOCK:])


def columns_of(row):
    return jnp.transpose(jnp.broadcast_to(row, (128, row.shape[1])))


def prepare_masks(causal, qseg_ref, kseg_ref, qone, kout, still):
    lane = wide(lax.broadcasted_iota(jnp.int32, (1, 128), 1))
    qone[...] = low(jnp.where(columns_of(qseg_ref[0]) == lane, 1.0, 0.0))
    kout[...] = low(jnp.where(columns_of(kseg_ref[0]) == lane, 0.0, MASKED))
    if causal:
        key = lax.broadcasted_iota(jnp.int32, (WINDOW, BLOCK), 0)
        query = lax.broadcasted_iota(jnp.int32, (WINDOW, BLOCK), 1)
        still[0] = jnp.where(key <= query, 0.0, MASKED)
        still[1] = jnp.where(key <= query + BLOCK, 0.0, MASKED)
        still[2] = jnp.zeros((WINDOW, BLOCK), F32)
        still[3] = jnp.where(key < BLOCK, 0.0, MASKED)


MASK_SCRATCH = lambda length: [pltpu.VMEM((length, 128), BF), pltpu.VMEM((length, 128), BF), pltpu.VMEM((4, WINDOW, BLOCK), F32)]


def bias_of(causal, still, qb, c, start, bound):
    if causal:
        at = jnp.minimum(qb, 1) if c is None else jnp.where(bound < WINDOW, 3, 2)
        return still[at]
    if c is None:
        return None
    key = lax.broadcasted_iota(jnp.int32, (WINDOW, BLOCK), 0) + start
    return jnp.where(key >= bound, 0.0, MASKED)


def masked(scores, bias):
    return scores if bias is None else scores + jnp.concatenate([bias, bias], axis=1)


def window(causal, first_ref, r, qb, c, length):
    c = 0 if c is None else c
    if causal:
        end = (qb + 1) * BLOCK - c * WINDOW
        return pl.multiple_of(jnp.maximum(end - WINDOW, 0), BLOCK), end
    begin = first_ref[r, qb] + c * WINDOW
    return pl.multiple_of(jnp.minimum(begin, length - WINDOW), 16), begin


def lanes_at(offset, p):
    return slice(offset + 128 * p, offset + 128 * p + 128)


UNROLL = 4


def most(extra_ref, r, qbs):
    count = extra_ref[r, qbs[0]]
    for qb in qbs[1:]:
        count = jnp.maximum(count, extra_ref[r, qb])
    return count


def attend(causal, r, first_ref, extra_ref, q, k, v, out_ref, lse_ref, masking, top, total, mix):
    length = q[0].shape[0]
    masks = lane_masks(0.125)
    joint = 2 if causal else 1
    qone, kout, still = masking

    def windows(qbs, c):
        scores, values, biases = [], [], []
        for qb in qbs:
            q0 = pl.multiple_of(qb * BLOCK, BLOCK)
            start, bound = window(causal, first_ref, r, qb, c, length)
            bias = bias_of(causal, still, qb, c, start, bound)
            queries, keys = qone[pl.ds(q0, BLOCK), :], kout[pl.ds(start, WINDOW), :]
            queries = jnp.concatenate([queries, queries], axis=0)
            for p in range(4):
                qs = jnp.concatenate([stacked(q[0][pl.ds(q0, BLOCK), lanes_at(q[1], p)], masks), queries], axis=1)
                ks = jnp.concatenate([k[0][pl.ds(start, WINDOW), lanes_at(k[1], p)], keys], axis=1)
                scores.append(mxu(ks, qs, NT))
                values.append(v[0][pl.ds(start, WINDOW), lanes_at(v[1], p)])
                biases.append(bias)
        return [masked(x, bias) for x, bias in zip(scores, biases)], values

    def step(i, _):
        qbs = [i * UNROLL + u for u in range(UNROLL)]
        scores, values = windows(qbs, None)
        highs = [jnp.max(x, axis=0, keepdims=True) for x in scores]
        weights = [jnp.exp(x - high) for x, high in zip(scores, highs)]
        sums = [jnp.sum(x, axis=0, keepdims=True) for x in weights]
        mixed = [pick(mxu(val, low(x), TN)) for val, x in zip(values, weights)]
        for n in range(4 * UNROLL):
            top[n] = highs[n]
            total[n] = sums[n]
            mix[n] = mixed[n]
        for u in range(0, UNROLL, joint):
            def more(c, _, u=u):
                scores, values = windows(qbs[u:u + joint], c + 1)
                highs = [jnp.maximum(top[4 * u + p], jnp.max(x, axis=0, keepdims=True)) for p, x in enumerate(scores)]
                weights = [jnp.exp(x - high) for x, high in zip(scores, highs)]
                mixed = [pick(mxu(val, low(x), TN)) for val, x in zip(values, weights)]
                for p in range(4 * joint):
                    n = 4 * u + p
                    fade = jnp.exp(top[n] - highs[p])
                    top[n] = highs[p]
                    total[n] = total[n] * fade + jnp.sum(weights[p], axis=0, keepdims=True)
                    mix[n] = mix[n] * pick(jnp.broadcast_to(fade, (128, 2 * BLOCK))) + mixed[p]
                return 0

            lax.fori_loop(0, most(extra_ref, r, qbs[u:u + joint]), more, 0)
        for u, qb in enumerate(qbs):
            q0 = pl.multiple_of(qb * BLOCK, BLOCK)
            for p in range(4):
                sums = total[4 * u + p]
                inverse = pick(jnp.broadcast_to(1.0 / sums, (128, 2 * BLOCK)))
                out_ref[pl.ds(q0, BLOCK), lanes_at(0, p)] = low(jnp.transpose(mix[4 * u + p] * inverse))
                lse = top[4 * u + p] + jnp.log(sums)
                lse_ref[0, 2 * p:2 * p + 1, pl.ds(q0, BLOCK)] = lse[:, :BLOCK]
                lse_ref[0, 2 * p + 1:2 * p + 2, pl.ds(q0, BLOCK)] = lse[:, BLOCK:]
        return 0

    lax.fori_loop(0, length // BLOCK // UNROLL, step, 0)


ATTEND_SCRATCH = lambda length: MASK_SCRATCH(length) + [
    pltpu.VMEM((4 * UNROLL, 1, 2 * BLOCK), F32),
    pltpu.VMEM((4 * UNROLL, 1, 2 * BLOCK), F32), pltpu.VMEM((4 * UNROLL, 128, BLOCK), F32)]


def norm(hidden):
    average = jnp.mean(hidden, axis=-1, keepdims=True)
    centred = hidden - average
    inverse = lax.rsqrt(jnp.mean(centred * centred, axis=-1, keepdims=True) + EPSILON)
    return centred * inverse, inverse


def norm_back(grad, normed, inverse, gain):
    scaled = grad * gain
    return inverse * (scaled - jnp.mean(scaled, axis=-1, keepdims=True)
                      - normed * jnp.mean(scaled * normed, axis=-1, keepdims=True))


def head_sums(grad, mix):
    lane = lax.broadcasted_iota(jnp.int32, (16, 512), 1) // 64
    heads = low(jnp.where(lane == lax.broadcasted_iota(jnp.int32, (16, 512), 0), 1.0, 0.0))
    prod = wide(grad) * wide(mix)
    upper = low(prod)
    return (mxu(heads, upper, NT) + mxu(heads, low(prod - wide(upper)), NT))[:8]


def rows_spec(t, length):
    per = length // t
    return pl.BlockSpec((1, 8, t), lambda i: (i // per, 0, i % per))


def sum_rows(x):
    return jnp.sum(wide(x), axis=0, keepdims=True)


S_BIAS, S_GAIN, S_SHIFT, C_BIAS, C_GAIN, C_SHIFT, I_BIAS, O_BIAS, F_GAIN, F_SHIFT = range(10)


def vec(ref, row, block=0, size=512):
    return ref[row:row + 1, block * size:(block + 1) * size]


def self_kernel(first_ref, extra_ref, x_ref, w_ref, vec_ref, seg_ref, qkv_ref, mix_ref, lse_ref, qone, kout, still, *state):
    r = pl.program_id(0)
    prepare_masks(True, seg_ref, seg_ref, qone, kout, still)
    x = x_ref[...]
    qkv_ref[:, :512] = low(mxu(x, w_ref[:, :512]) + vec(vec_ref, S_BIAS, 0))
    qkv_ref[:, 512:1024] = low(mxu(x, w_ref[:, 512:1024]))
    qkv_ref[:, 1024:] = low(mxu(x, w_ref[:, 1024:]) + vec(vec_ref, S_BIAS, 1))
    attend(True, r, first_ref, extra_ref, (qkv_ref, 0), (qkv_ref, 512), (qkv_ref, 1024), mix_ref, lse_ref,
           (qone, kout, still), *state)


def self_forward(plan, x, w, vectors, seg):
    rows, _, length = seg.shape
    return pl.pallas_call(
        self_kernel, grid=(rows,),
        in_specs=[smem(), smem(), tiled(length, 512), fixed((512, 1536), 0, 0), fixed((16, 2048), 0, 0),
                  pl.BlockSpec((1, 1, length), lambda i: (i, 0, 0))],
        out_specs=[tiled(length, 1536), tiled(length, 512), pl.BlockSpec((1, 8, length), lambda i: (i, 0, 0))],
        out_shape=[shape_of((rows * length, 1536)), shape_of((rows * length, 512)), shape_of((rows, 8, length), F32)],
        scratch_shapes=ATTEND_SCRATCH(length), compiler_params=params(40), cost_estimate=cost(20), name="self_forward",
    )(*plan, x, w, vectors, seg)


def cross_kernel(first_ref, extra_ref, x_ref, mix_ref, mem_ref, wo_ref, wq_ref, wkv_ref, vec_ref, qseg_ref, kseg_ref,
                 hid_ref, q_ref, kv_ref, out_ref, lse_ref, qone, kout, still, *state):
    r = pl.program_id(0)
    prepare_masks(False, qseg_ref, kseg_ref, qone, kout, still)
    hidden = wide(x_ref[...]) + mxu(mix_ref[...], wo_ref[...]) + vec(vec_ref, S_BIAS, 2)
    hid_ref[...] = hidden
    first = low(norm(hidden)[0] * vec(vec_ref, S_GAIN) + vec(vec_ref, S_SHIFT))
    q_ref[...] = low(mxu(first, wq_ref[...]) + vec(vec_ref, C_BIAS, 0))
    mem = mem_ref[...]
    kv_ref[:, :512] = low(mxu(mem, wkv_ref[:, :512]))
    kv_ref[:, 512:] = low(mxu(mem, wkv_ref[:, 512:]) + vec(vec_ref, C_BIAS, 1))
    attend(False, r, first_ref, extra_ref, (q_ref, 0), (kv_ref, 0), (kv_ref, 512), out_ref, lse_ref,
           (qone, kout, still), *state)


def cross_forward(plan, x, mix, mem, weights, vectors, qseg, kseg):
    rows, _, length = qseg.shape
    seg = pl.BlockSpec((1, 1, length), lambda i: (i, 0, 0))
    total = rows * length
    return pl.pallas_call(
        cross_kernel, grid=(rows,),
        in_specs=[smem(), smem(), tiled(length, 512), tiled(length, 512), tiled(length, 512),
                  fixed((512, 512), 0, 0), fixed((512, 512), 0, 1), fixed((512, 1024), 0, 1), fixed((16, 2048), 0, 0), seg, seg],
        out_specs=[tiled(length, 512), tiled(length, 512), tiled(length, 1024), tiled(length, 512),
                   pl.BlockSpec((1, 8, length), lambda i: (i, 0, 0))],
        out_shape=[shape_of((total, 512), F32), shape_of((total, 512)), shape_of((total, 1024)), shape_of((total, 512)),
                   shape_of((rows, 8, length), F32)],
        scratch_shapes=ATTEND_SCRATCH(length), compiler_params=params(48), cost_estimate=cost(25), name="cross_forward",
    )(*plan, x, mix, mem, weights, weights, weights, vectors, qseg, kseg)


def pair_row(ref, p, q0):
    return jnp.concatenate([ref[0, 2 * p + h:2 * p + h + 1, pl.ds(q0, BLOCK)] for h in range(2)], axis=1)


def back_kernel(causal, first_ref, extra_ref, q_ref, k_ref, v_ref, delta_ref, grad_ref, lse_ref, qseg_ref, kseg_ref, *refs):
    dq_ref, dk_ref, dv_ref, qone, kout, still, dk, dv, dq = refs[-9:]
    r = pl.program_id(0)
    length = q_ref.shape[0]
    joint = 2 if causal else 1
    prepare_masks(causal, qseg_ref, kseg_ref, qone, kout, still)
    dk[...] = jnp.zeros_like(dk)
    dv[...] = jnp.zeros_like(dv)
    masks = lane_masks(0.125)
    ones = lane_masks(1.0)

    def windows(qbs, c):
        places, qs, gs, deltas, lses, keys, biases, scores = [], [], [], [], [], [], [], []
        for qb in qbs:
            q0 = pl.multiple_of(qb * BLOCK, BLOCK)
            start, bound = window(causal, first_ref, r, qb, c, length)
            bias = bias_of(causal, still, qb, c, start, bound)
            queries, outs = qone[pl.ds(q0, BLOCK), :], kout[pl.ds(start, WINDOW), :]
            queries = jnp.concatenate([queries, queries], axis=0)
            for p in range(4):
                lanes = lanes_at(0, p)
                grad = grad_ref[pl.ds(q0, BLOCK), lanes]
                deltas.append(pair_row(delta_ref, p, q0))
                lses.append(pair_row(lse_ref, p, q0))
                qs.append(stacked(q_ref[pl.ds(q0, BLOCK), lanes], masks))
                gs.append(stacked(grad, ones))
                keys.append(k_ref[pl.ds(start, WINDOW), lanes])
                places.append((pl.ds(start, WINDOW), lanes))
                biases.append(bias)
                scores.append(mxu(jnp.concatenate([keys[-1], outs], axis=1), jnp.concatenate([qs[-1], queries], axis=1), NT))
        dprobs = [mxu(v_ref[place], g, NT) for place, g in zip(places, gs)]
        probs = [jnp.exp(masked(x, bias) - lse) for x, bias, lse in zip(scores, biases, lses)]
        dscores = [low(x * (d - delta)) for x, d, delta in zip(probs, dprobs, deltas)]
        new_dv = [mxu(low(x), g) for x, g in zip(probs, gs)]
        new_dk = [mxu(d, x) for d, x in zip(dscores, qs)]
        parts = [pick(mxu(key, d, TN)) for key, d in zip(keys, dscores)]
        for place, more_dv, more_dk in zip(places, new_dv, new_dk):
            dv[place] += more_dv
            dk[place] += more_dk
        return parts

    def step(i, _):
        qbs = [i * UNROLL + u for u in range(UNROLL)]
        for n, part in enumerate(windows(qbs, None)):
            dq[n] = part
        for u in range(0, UNROLL, joint):
            def more(c, _, u=u):
                for p, part in enumerate(windows(qbs[u:u + joint], c + 1)):
                    dq[4 * u + p] += part
                return 0

            lax.fori_loop(0, most(extra_ref, r, qbs[u:u + joint]), more, 0)
        for u, qb in enumerate(qbs):
            q0 = pl.multiple_of(qb * BLOCK, BLOCK)
            for p in range(4):
                dq_ref[pl.ds(q0, BLOCK), lanes_at(0, p)] = low(jnp.transpose(dq[4 * u + p]) * 0.125)
        return 0

    lax.fori_loop(0, length // BLOCK // UNROLL, step, 0)
    dk_ref[...] = low(dk[...])
    dv_ref[...] = low(dv[...])


def attend_back(causal, plan, q, k, v, delta, grad, lse, qseg, kseg, after=()):
    rows, _, length = qseg.shape
    seg = pl.BlockSpec((1, 1, length), lambda i: (i, 0, 0))
    line = pl.BlockSpec((1, 8, length), lambda i: (i, 0, 0))
    return pl.pallas_call(
        functools.partial(back_kernel, causal), grid=(rows,),
        in_specs=[smem(), smem(), tiled(length, 512, q[1]), tiled(length, 512, k[1]), tiled(length, 512, v[1]), line,
                  tiled(length, 512), line, seg, seg] + [pl.BlockSpec(memory_space=pl.ANY)] * len(after),
        out_specs=[tiled(length, 512)] * 3, out_shape=[shape_of((rows * length, 512))] * 3,
        scratch_shapes=MASK_SCRATCH(length) + [pltpu.VMEM((length, 512), F32), pltpu.VMEM((length, 512), F32),
                                               pltpu.VMEM((4 * UNROLL, 128, BLOCK), F32)],
        compiler_params=params(40), cost_estimate=cost(20), name="self_back" if causal else "cross_back",
    )(*plan, q[0], k[0], v[0], delta, grad, lse, qseg, kseg, *after)


def emit(outs, col, acc, index_ref, acc_col, width):
    half = outs[0].shape[0]
    for r in range(512 // UNIT):
        row = pl.multiple_of(index_ref[r] * UNIT, UNIT)
        outs[r // half][r % half, :, col:col + width] = low(acc[pl.ds(row, UNIT), acc_col:acc_col + width])


def halves(width):
    half = 512 // UNIT // 2
    return [fixed((half, UNIT, width), 0, 0, 0)] * 2, [shape_of((half, UNIT, width))] * 2


MID_TILE = 512
PARTS = 2
CHUNK = 1024


def mid_kernel(index_a, index_b, hid_ref, mix_ref, grad_ref, win_ref, gout_ref, wco_ref, vec_ref,
               out_ref, h2_ref, mg_ref, delta_ref, keep_ref, send_ref, co_ref, small_ref,
               wout, dwin, dwout, dwco, act, slope):
    step = pl.program_id(0)
    hidden_width = win_ref.shape[1]
    tokens = hid_ref.shape[0]

    @pl.when(step == 0)
    def _():
        for d in range(512 // UNIT):
            for b in range(4):
                wout[(4 * d + b) * UNIT:(4 * d + b + 1) * UNIT, :] = gout_ref[d * UNIT:(d + 1) * UNIT, 512 * b:512 * b + 512]
        dwin[...] = jnp.zeros_like(dwin)
        dwout[...] = jnp.zeros_like(dwout)
        dwco[...] = jnp.zeros_like(dwco)
        small_ref[...] = jnp.zeros_like(small_ref)

    chunks = [slice(c, c + CHUNK) for c in range(0, hidden_width, CHUNK)]
    part = tokens // PARTS
    parts = [slice(i * part, i * part + part) for i in range(PARTS)]
    firsts = [norm(hid_ref[t, :])[0] * vec(vec_ref, S_GAIN) + vec(vec_ref, S_SHIFT) for t in parts]
    norms2 = [norm(first + mxu(mix_ref[t, :], wco_ref[...]) + vec(vec_ref, C_BIAS, 2)) for t, first in zip(parts, firsts)]
    seconds = [normed * vec(vec_ref, C_GAIN) + vec(vec_ref, C_SHIFT) for normed, _ in norms2]
    lows = [low(second) for second in seconds]
    norms3 = []
    for t, second, second_low in zip(parts, seconds, lows):
        hidden3 = second + vec(vec_ref, O_BIAS)
        for c in chunks:
            pre = mxu(second_low, win_ref[:, c]) + vec_ref[I_BIAS:I_BIAS + 1, c]
            sig = 0.5 + 0.5 * jnp.tanh(0.5 * pre)
            active = low(pre * sig)
            act[t, c] = active
            slope[t, c] = sig * (1.0 + pre * (1.0 - sig))
            hidden3 += mxu(active, wout[c, :])
        norms3.append(norm(hidden3))
    backs3 = []
    for t, (normed3, inverse3) in zip(parts, norms3):
        out_ref[t, :] = low(normed3 * vec(vec_ref, F_GAIN) + vec(vec_ref, F_SHIFT))
        grad = wide(grad_ref[t, :])
        backs3.append(norm_back(grad, normed3, inverse3, vec(vec_ref, F_GAIN)))
        small_ref[2:3, :512] += sum_rows(grad * normed3)
        small_ref[3:4, :512] += sum_rows(grad)
    b3s = [low(back3) for back3 in backs3]
    us = [[] for _ in chunks]
    grads2 = []
    for t, back3, b3 in zip(parts, backs3, b3s):
        grad2 = back3
        for n, c in enumerate(chunks):
            u = low(mxu(b3, wout[c, :], NT) * slope[t, c])
            us[n].append(u)
            grad2 += mxu(u, win_ref[:, c], NT)
        grads2.append(grad2)
    b2s = []
    for t, grad2, (normed2, inverse2) in zip(parts, grads2, norms2):
        h2 = norm_back(grad2, normed2, inverse2, vec(vec_ref, C_GAIN))
        b2 = low(h2)
        h2_ref[t, :] = b2
        b2s.append(b2)
        small_ref[4:5, :512] += sum_rows(grad2 * normed2)
        small_ref[5:6, :512] += sum_rows(grad2)
    second_low = jnp.concatenate(lows, axis=0)
    b3 = jnp.concatenate(b3s, axis=0)
    second_t, b3_t = jnp.transpose(second_low), jnp.transpose(b3)
    small_ref[1:2, :512] += sum_rows(b3)
    for n, c in enumerate(chunks):
        u = jnp.concatenate(us[n], axis=0)
        dwin[:, c] += mxu(second_t, u)
        dwout[:, c] += mxu(b3_t, act[:, c])
        small_ref[0:1, c] += sum_rows(u)
    b2 = jnp.concatenate(b2s, axis=0)
    small_ref[6:7, :512] += sum_rows(b2)
    dwco[...] += mxu(jnp.transpose(mix_ref[...]), b2)
    mix_grad = low(mxu(b2, wco_ref[...], NT))
    mg_ref[...] = mix_grad
    delta_ref[0] = head_sums(mix_grad, mix_ref[...])

    @pl.when(step == pl.num_programs(0) - 1)
    def _():
        outs = keep_ref, send_ref
        emit(outs, 0, dwin, index_a, 0, hidden_width)
        for c in chunks:
            wout[c, :] = low(jnp.transpose(dwout[:, c]))
        half = keep_ref.shape[0]
        for r in range(512 // UNIT):
            for b in range(4):
                row = pl.multiple_of((index_b[r] * 4 + b) * UNIT, UNIT)
                outs[r // half][r % half, :, 2048 + 512 * b:2560 + 512 * b] = wout[pl.ds(row, UNIT), :]
        co_ref[...] = dwco[...]


def middle(index_a, index_b, hid, mix, grad, rest, vectors, length):
    total = hid.shape[0]
    t = MID_TILE
    specs, shapes = halves(4096)
    return pl.pallas_call(
        mid_kernel, grid=(total // t,),
        in_specs=[smem(), smem(), tiled(t, 512), tiled(t, 512), tiled(t, 512),
                  fixed((512, 2048), 0, 0), fixed((512, 2048), 0, 1), fixed((512, 512), 0, 8), fixed((16, 2048), 0, 0)],
        out_specs=[tiled(t, 512)] * 3 + [rows_spec(t, length)] + specs + [fixed((512, 512), 0, 0), fixed((8, 2048), 0, 0)],
        out_shape=[shape_of((total, 512))] * 3 + [shape_of((total // length, 8, length), F32)] + shapes
        + [shape_of((512, 512), F32), shape_of((8, 2048), F32)],
        scratch_shapes=[pltpu.VMEM((2048, 512), BF), pltpu.VMEM((512, 2048), F32), pltpu.VMEM((512, 2048), F32),
                        pltpu.VMEM((512, 512), F32), pltpu.VMEM((t, 2048), BF), pltpu.VMEM((t, 2048), F32)],
        compiler_params=params(56), cost_estimate=cost(40), name="middle",
    )(index_a, index_b, hid, mix, grad, rest, rest, rest, vectors)


DENSE_TILE = 512
SELF_TILE = 1024


def cross_dense_kernel(index_a, index_b, cq_ref, ck_ref, cv_ref, mem_ref, hid_ref, h2_ref, mix_ref,
                       wq_ref, wo_ref, co_ref, vec_ref,
                       h1_ref, mg_ref, delta_ref, keep_ref, send_ref, small_ref, dq, dkv, do):
    step = pl.program_id(0)

    @pl.when(step == 0)
    def _():
        dq[...] = jnp.zeros_like(dq)
        dkv[...] = jnp.zeros_like(dkv)
        do[...] = jnp.zeros_like(do)
        small_ref[...] = jnp.zeros_like(small_ref)

    cq, ck, cv = cq_ref[...], ck_ref[...], cv_ref[...]
    normed, inverse = norm(hid_ref[...])
    first = low(normed * vec(vec_ref, S_GAIN) + vec(vec_ref, S_SHIFT))
    grad1 = wide(h2_ref[...]) + mxu(cq, wq_ref[...], NT)
    h1 = norm_back(grad1, normed, inverse, vec(vec_ref, S_GAIN))
    b1 = low(h1)
    h1_ref[...] = b1
    mix_grad = low(mxu(b1, wo_ref[...], NT))
    mg_ref[...] = mix_grad
    delta_ref[0] = head_sums(mix_grad, mix_ref[...])
    dq[...] += mxu(jnp.transpose(first), cq)
    mem_t = jnp.transpose(mem_ref[...])
    dkv[:, :512] += mxu(mem_t, ck)
    dkv[:, 512:] += mxu(mem_t, cv)
    do[...] += mxu(jnp.transpose(mix_ref[...]), b1)
    small_ref[0:1, :] += sum_rows(cq)
    small_ref[1:2, :] += sum_rows(cv)
    small_ref[2:3, :] += sum_rows(grad1 * normed)
    small_ref[3:4, :] += sum_rows(grad1)
    small_ref[4:5, :] += sum_rows(b1)

    @pl.when(step == pl.num_programs(0) - 1)
    def _():
        outs = keep_ref, send_ref
        emit(outs, 0, dq, index_a, 0, 512)
        emit(outs, 512, co_ref, index_a, 0, 512)
        emit(outs, 1024, do, index_a, 0, 256)
        emit(outs, 1280, do, index_b, 256, 256)
        emit(outs, 1536, dkv, index_b, 0, 1024)


def cross_dense(index_a, index_b, grads, mem, hid, h2, mix, weights, dco, vectors, length):
    total = hid.shape[0]
    t = DENSE_TILE
    specs, shapes = halves(2560)
    return pl.pallas_call(
        cross_dense_kernel, grid=(total // t,),
        in_specs=[smem(), smem()] + [tiled(t, 512)] * 7
        + [fixed((512, 512), 0, 1), fixed((512, 512), 0, 0), fixed((512, 512), 0, 0), fixed((16, 2048), 0, 0)],
        out_specs=[tiled(t, 512)] * 2 + [rows_spec(t, length)] + specs + [fixed((8, 512), 0, 0)],
        out_shape=[shape_of((total, 512))] * 2 + [shape_of((total // length, 8, length), F32)] + shapes + [shape_of((8, 512), F32)],
        scratch_shapes=[pltpu.VMEM((512, 512), F32), pltpu.VMEM((512, 1024), F32), pltpu.VMEM((512, 512), F32)],
        compiler_params=params(40), cost_estimate=cost(12), name="cross_dense",
    )(index_a, index_b, *grads, mem, hid, h2, mix, weights, weights, dco, vectors)


def memory_kernel(ck_ref, cv_ref, w_ref, *refs):
    refs[-1][...] = low(mxu(ck_ref[...], w_ref[:, :512], NT) + mxu(cv_ref[...], w_ref[:, 512:], NT))


def memory_back(ck, cv, weights, after=()):
    total = ck.shape[0]
    t = 512
    return pl.pallas_call(
        memory_kernel, grid=(total // t,), in_specs=[tiled(t, 512)] * 2 + [fixed((512, 1024), 0, 1)]
        + [pl.BlockSpec(memory_space=pl.ANY)] * len(after),
        out_specs=tiled(t, 512), out_shape=shape_of((total, 512)), compiler_params=params(40), cost_estimate=cost(4), name="memory_grad",
    )(ck, cv, weights, *after)


VECTORS = (1536, 512, 512, 1536, 512, 512, 2048, 512, 512, 512)


def places(n, per, count, axis):
    shape = (1, n)
    at = wide(lax.broadcasted_iota(jnp.int32, shape, 1))
    owner = jnp.floor((at + 0.5) * (1.0 / per))
    return owner, at - owner * per


def one_hot(n, per):
    _, place = places(n, per, n // per, 1)
    return low(jnp.where(wide(lax.broadcasted_iota(jnp.int32, (128, n), 0)) == place, 1.0, 0.0))


def owned(n, per, count):
    owner, _ = places(n, per, count, 1)
    return wide(lax.broadcasted_iota(jnp.int32, (count, n), 0)) == owner


def self_grad_kernel(count, index_a, index_b, dq_ref, dk_ref, dv_ref, x_ref, mid_ref, small_ref, keep_ref, send_ref, lines_ref, dw, table):
    step = pl.program_id(0)

    @pl.when(step == 0)
    def _():
        dw[...] = jnp.zeros_like(dw)
        lines_ref[...] = jnp.zeros_like(lines_ref)

    x_t = jnp.transpose(x_ref[...])
    dw[:, :512] += mxu(x_t, dq_ref[...])
    dw[:, 512:1024] += mxu(x_t, dk_ref[...])
    dw[:, 1024:] += mxu(x_t, dv_ref[...])
    lines_ref[S_BIAS:S_BIAS + 1, :512] += sum_rows(dq_ref[...])
    lines_ref[S_BIAS:S_BIAS + 1, 512:1024] += sum_rows(dv_ref[...])

    @pl.when(step == pl.num_programs(0) - 1)
    def _():
        outs = keep_ref, send_ref
        emit(outs, 0, dw, index_a, 0, 768)
        emit(outs, 896, dw, index_b, 768, 768)
        for row, col, source, source_row in (
            (S_BIAS, 1024, small_ref, 4), (S_GAIN, 0, small_ref, 2), (S_SHIFT, 0, small_ref, 3),
            (C_BIAS, 0, small_ref, 0), (C_BIAS, 512, small_ref, 1), (C_BIAS, 1024, mid_ref, 6),
            (C_GAIN, 0, mid_ref, 4), (C_SHIFT, 0, mid_ref, 5),
            (O_BIAS, 0, mid_ref, 1), (F_GAIN, 0, mid_ref, 2), (F_SHIFT, 0, mid_ref, 3),
        ):
            lines_ref[row:row + 1, col:col + 512] = source[source_row:source_row + 1, :512]
        lines_ref[I_BIAS:I_BIAS + 1, :] = mid_ref[0:1, :]
        if count:
            table[...] = jnp.zeros_like(table)
            for n in (512, 1536, 2048):
                hot, mine = one_hot(n, n // count), owned(n, n // count, count)
                for j, size in enumerate(VECTORS):
                    if size == n:
                        line = jnp.broadcast_to(lines_ref[j:j + 1, :n], (count, n))
                        table[:, j, :] = mxu(low(jnp.where(mine, line, 0.0)), hot, NT)
            for r in range(count):
                outs[2 * r // count][r % (count // 2), :, 768:896] = low(table[index_a[r]])


def self_grad(count, index_a, index_b, grads, x, mid_small, small):
    total = x.shape[0]
    t = SELF_TILE
    specs, shapes = halves(1664)
    return pl.pallas_call(
        functools.partial(self_grad_kernel, count), grid=(total // t,),
        in_specs=[smem(), smem()] + [tiled(t, 512)] * 4 + [fixed((8, 2048), 0, 0), fixed((8, 512), 0, 0)],
        out_specs=specs + [fixed((16, 2048), 0, 0)],
        out_shape=shapes + [shape_of((16, 2048), F32)],
        scratch_shapes=[pltpu.VMEM((512, 1536), F32), pltpu.VMEM((max(count, 8), 16, 128), F32)],
        compiler_params=params(40), cost_estimate=cost(5), name="self_grad",
    )(index_a, index_b, *grads, x, mid_small, small)


def target_kernel(h1_ref, dq_ref, dk_ref, dv_ref, w_ref, *refs):
    out_ref = refs[-1]
    total = wide(h1_ref[...]) + mxu(dq_ref[...], w_ref[:, :512], NT)
    total += mxu(dk_ref[...], w_ref[:, 512:1024], NT)
    out_ref[...] = low(total + mxu(dv_ref[...], w_ref[:, 1024:], NT))


def target_grad(h1, grads, w, after=()):
    total = h1.shape[0]
    t = 512
    return pl.pallas_call(
        target_kernel, grid=(total // t,), in_specs=[tiled(t, 512)] * 4 + [fixed((512, 1536), 0, 0)]
        + [pl.BlockSpec(memory_space=pl.ANY)] * len(after),
        out_specs=tiled(t, 512), out_shape=shape_of((total, 512)), compiler_params=params(40), cost_estimate=cost(5), name="target_grad",
    )(h1, *grads, w, *after)


class Net:
    def __init__(self):
        self.wide = lax.axis_size("wide")
        self.narrow = lax.axis_size("narrow")
        self.count = self.wide * self.narrow
        self.wide_bits = self.wide.bit_length() - 1
        self.narrow_bits = self.narrow.bit_length() - 1
        self.bits = self.wide_bits + self.narrow_bits
        self.me = lax.axis_index("wide") * self.narrow + lax.axis_index("narrow")
        inner = list(range(self.narrow_bits))
        core, second = [self.narrow_bits], [self.narrow_bits + 1]
        far = list(range(self.narrow_bits + 2, self.bits))
        self.near = self.bits - len(far)
        self.orders = (core + second + inner + far, core + inner + second + far)

    def exchange(self, x, bit):
        if bit < self.narrow_bits:
            return lax.ppermute(x, "narrow", [(i, i ^ (1 << bit)) for i in range(self.narrow)])
        return self.across(x, 1 << bit)

    def across(self, x, mask):
        mask >>= self.narrow_bits
        return lax.ppermute(x, "wide", [(i, i ^ mask) for i in range(self.wide)])

    def far_masks(self, order):
        return [sum(((r >> s) & 1) << bit for s, bit in enumerate(order)) for r in range(1 << len(order))]

    def index(self, chain):
        order, n = self.orders[chain], self.bits
        mask = [sum(((r >> (n - 1 - s)) & 1) << bit for s, bit in enumerate(order)) for r in range(self.count)]
        return jnp.array(mask, jnp.int32) ^ self.me

    def gather_index(self, chain):
        order = self.orders[chain][::-1]
        mask = [sum(((r >> s) & 1) << bit for s, bit in enumerate(order)) for r in range(self.count)]
        return jnp.array(mask, jnp.int32) ^ self.me


def pack_kernel(*refs):
    vectors, (qkv, so, cq, ckv, co, fin, fout, packed_ref, cross_ref, rest_ref) = refs[:10], refs[10:20]
    lines, sem = refs[20:30], refs[30]
    moves = list(zip(vectors, lines))
    moves += [(qkv.at[:, :768], packed_ref.at[0, :, :768]), (qkv.at[:, 768:], packed_ref.at[0, :, 896:]), (fin, rest_ref.at[:, :2048])]
    moves += [(fout.at[UNIT * b:UNIT * b + UNIT, :], rest_ref.at[:, 2048 + 512 * b:2560 + 512 * b]) for b in range(4)]
    moves += [(co, rest_ref.at[:, 4096:]), (so, cross_ref.at[0, :, :512]),
              (cq, cross_ref.at[0, :, 512:1024]), (ckv, cross_ref.at[0, :, 1024:])]
    copies = [pltpu.make_async_copy(src, dst, sem.at[i]) for i, (src, dst) in enumerate(moves)]
    for copy in copies:
        copy.start()
    for copy in copies:
        copy.wait()
    rows = []
    for v in lines:
        line = wide(v[...])
        rows.append(jnp.concatenate([line, jnp.zeros((1, 128 - line.shape[1]), F32)], axis=1))
    rows.append(jnp.zeros((6, 128), F32))
    packed_ref[0, :, 768:896] = low(jnp.concatenate(rows, axis=0))


def unpack_kernel(count, index_a, index_b, *refs):
    n = (len(refs) - 3) // 2
    pieces_a, pieces_b, (w_ref, vec_ref, table) = refs[:n], refs[n:2 * n], refs[2 * n:]
    for pieces, index, col, width in ((pieces_a, index_a, 0, 768), (pieces_b, index_b, 768, 768)):
        r = 0
        for piece in pieces:
            for j in range(piece.shape[0]):
                owner = index[r]
                w_ref[pl.ds(pl.multiple_of(owner * UNIT, UNIT), UNIT), col:col + width] = piece[j, :, :width]
                if col == 0:
                    table[owner] = wide(piece[j, :, 768:896])
                r += 1
    vec_ref[...] = jnp.zeros_like(vec_ref)
    for n in (512, 1536, 2048):
        hot, mine = one_hot(n, n // count), owned(n, n // count, count)
        for j, size in enumerate(VECTORS):
            if size == n:
                spread = mxu(low(table[:, j, :]), hot)
                vec_ref[j:j + 1, :n] = jnp.sum(jnp.where(mine, spread, 0.0), axis=0, keepdims=True)


def place_kernel(index_a, index_b, *refs):
    n = (len(refs) - 1) // 2
    w_ref = refs[-1]
    for pieces, index, col in ((refs[:n], index_a, 0), (refs[n:2 * n], index_b, 1024)):
        r = 0
        for piece in pieces:
            for j in range(piece.shape[0]):
                row = pl.multiple_of(index[r] * UNIT, UNIT)
                w_ref[pl.ds(row, UNIT), col:col + 1024] = piece[j]
                r += 1


def gather_weights(net, small, big):
    qkv, so, cq, ckv, co, fin, fout = big
    if qkv.shape[0] % UNIT or net.bits < 5:
        small, big = lax.all_gather((small, big), AXES, axis=0, tiled=True) if net.count > 1 else (small, big)
        qkv, so, cq, ckv, co, fin, fout = big
        fout = fout.reshape(-1, 4, UNIT, 512).transpose(0, 2, 1, 3).reshape(512, 2048)
        rows = [jnp.pad(wide(v), (0, 2048 - v.shape[0])) for v in small]
        vectors = jnp.stack(rows + [jnp.zeros((2048,), F32)] * 6)
        return qkv, vectors, jnp.concatenate([fin, fout, co], axis=1), lambda x: (x, jnp.concatenate([so, cq, ckv], axis=1))
    packed, cross, rest = pl.pallas_call(
        pack_kernel, in_specs=[pl.BlockSpec(memory_space=pl.ANY)] * 17, out_specs=[vmem()] * 3,
        out_shape=[shape_of((1, UNIT, 1664)), shape_of((1, UNIT, 2048)), shape_of((UNIT, 4608))],
        scratch_shapes=[pltpu.VMEM((1, v.shape[0]), BF) for v in small] + [pltpu.SemaphoreType.DMA((21,))],
        compiler_params=params(60), cost_estimate=cost(2), name="pack",
    )(*[v[None] for v in small], *big)
    rest = lax.all_gather(rest, AXES, axis=0, tiled=True)
    orders = [order[::-1] for order in net.orders]
    far = net.bits - net.near
    masks = net.far_masks(orders[0][:far])[1:]
    everywhere = lambda x: jnp.concatenate([x] + [net.across(x, mask) for mask in masks], axis=0)
    packed = everywhere(packed)
    packed, cross = lax.optimization_barrier((packed, cross))
    cross = everywhere(cross)
    parts = [packed[:, :, :896], packed[:, :, 896:], cross[:, :, :1024], cross[:, :, 1024:]]
    orders = orders + orders
    parts = [jnp.concatenate([x, net.exchange(x, order[far])], axis=0) for x, order in zip(parts, orders)]

    def spread(pieces, s):
        got = [[net.exchange(x, order[s]) for x in chain] for chain, order in zip(pieces, orders)]
        return [chain + more for chain, more in zip(pieces, got)]

    pieces = spread(spread([[x] for x in parts[:2]], far + 1), far + 2)
    later = spread([[x] for x in parts[2:]], far + 1)
    gather_index = [net.gather_index(0), net.gather_index(1)]

    def cross_weights(values):
        held, values = lax.optimization_barrier((later, values))
        held = spread(held, far + 2)
        return values, pl.pallas_call(
            place_kernel, in_specs=[smem(), smem()] + [vmem()] * (len(held[0]) * 2), out_specs=vmem(),
            out_shape=shape_of((512, 2048)), compiler_params=params(32), cost_estimate=cost(2), name="place",
        )(*gather_index, *held[0], *held[1])

    w, vectors = pl.pallas_call(
        functools.partial(unpack_kernel, net.count), in_specs=[smem(), smem()] + [vmem()] * (len(pieces[0]) * 2), out_specs=[vmem()] * 2,
        out_shape=[shape_of((512, 1536)), shape_of((16, 2048), F32)],
        scratch_shapes=[pltpu.VMEM((net.count, 16, 128), F32)],
        compiler_params=params(40), cost_estimate=cost(2), name="unpack",
    )(*gather_index, *pieces[0], *pieces[1])
    return w, vectors, rest, cross_weights


class Reduction:
    def __init__(self, net, keep, send, cut):
        self.net, self.cut = net, cut
        self.keep, self.send = [keep], [send]
        self.stage = 0
        self.sums = None

    def state(self):
        return tuple(self.send) if self.sums is None else ()

    def start(self):
        if self.sums is not None:
            return
        if self.stage < self.net.near:
            self.got = [self.net.exchange(x, order[self.stage]) for x, order in zip(self.send, self.net.orders)]
        else:
            far = self.net.far_masks(self.net.orders[0][:self.net.near - 1:-1])
            self.got = [self.net.across(x, mask) for x, mask in zip(self.send, far[1:])]

    def add(self):
        if self.sums is not None:
            return
        self.stage += 1
        if self.stage > self.net.near:
            self.sums = sum((wide(got[0]) for got in self.got), self.keep[0][0])
            return
        sums = [wide(k) + wide(g) for k, g in zip(self.keep, self.got)]
        if self.stage == 1:
            sums = [sums[0][:, :, :self.cut], sums[0][:, :, self.cut:]]
        elif self.stage == self.net.near:
            total = jnp.concatenate(sums, axis=2)
            self.keep = [total[:1]]
            self.send = [low(total[r:r + 1]) for r in range(1, total.shape[0])]
            return
        half = sums[0].shape[0] // 2
        self.keep = [low(s[:half]) for s in sums]
        self.send = [low(s[half:]) for s in sums]


def hold(groups, values):
    waiting = [group for group in groups if group.sums is None]
    if not waiting:
        return values
    got, values = lax.optimization_barrier(([group.got for group in waiting], values))
    for group, x in zip(waiting, got):
        group.got = x
    return values


def together(groups):
    if groups:
        state = lax.optimization_barrier([(group.keep, group.send) for group in groups])
        for group, (keep, send) in zip(groups, state):
            group.keep, group.send = keep, send


def plan_self(seg, positions):
    rows, length = seg.shape
    starts = jnp.arange(0, length, BLOCK, dtype=jnp.int32)
    begin = starts[None, :] - positions[:, ::BLOCK]
    left = jnp.maximum(starts[None, :] + BLOCK - WINDOW - begin, 0)
    return jnp.zeros_like(begin), (left + WINDOW - 1) // WINDOW


def plan_cross(tseg, sseg):
    last = jnp.int32(1 << 20)
    tkey = jnp.where(tseg == 0, last, tseg)
    skey = jnp.where(sseg == 0, last, sseg)
    begin = jnp.sum(skey[:, None, :] < tkey[:, ::BLOCK, None], axis=2, dtype=jnp.int32)
    end = jnp.sum(skey[:, None, :] <= tkey[:, BLOCK - 1::BLOCK, None], axis=2, dtype=jnp.int32)
    first = (begin // 16) * 16
    return first, jnp.maximum((end - first + WINDOW - 1) // WINDOW - 1, 0)


def per_device(
    target, memory, out_grad, target_segments, source_segments, target_positions,
    self_qkv, self_out, cross_query, cross_kv, cross_out, ffn_in, ffn_out, *small,
):
    net = Net()
    rows, length = target_segments.shape
    fast = self_qkv.shape[0] % UNIT == 0 and net.bits >= 5
    self_plan = plan_self(target_segments, target_positions)
    cross_plan = plan_cross(target_segments, source_segments)
    tseg = wide(target_segments)[:, None, :]
    sseg = wide(source_segments)[:, None, :]
    w_qkv, vectors, rest, cross_weights = gather_weights(net, small, (self_qkv, self_out, cross_query, cross_kv, cross_out, ffn_in, ffn_out))
    if fast:
        index_a, index_b = net.index(0), net.index(1)
    else:
        index_a = index_b = jnp.arange(512 // UNIT, dtype=jnp.int32)

    (qkv, self_mix, self_lse), cross_w = cross_weights(tuple(self_forward(self_plan, target, w_qkv, vectors, tseg)))
    hid, cq, pairs, cross_mix, cross_lse = cross_forward(cross_plan, target, self_mix, memory, cross_w, vectors, tseg, sseg)
    output, h2, cross_mg, cross_delta, ffn_keep, ffn_send, dco, mid_small = middle(index_a, index_b, hid, cross_mix, out_grad, rest, vectors, length)

    groups = [Reduction(net, ffn_keep, ffn_send, 2048)] if fast else []

    def backward(causal, plan, q, k, v, delta, grad, lse, kseg):
        tied = tuple(x for group in groups for x in group.state())
        for group in groups:
            group.start()
        out = hold(groups, attend_back(causal, plan, q, k, v, delta, grad, lse, tseg, kseg, tied))
        for group in groups:
            group.add()
        return out

    cross_grads = backward(False, cross_plan, (cq, 0), (pairs, 0), (pairs, 1), cross_delta, cross_mg, cross_lse, sseg)
    for group in groups:
        group.start()
    h1, self_mg, self_delta, cross_keep, cross_send, small_sums = cross_dense(
        index_a, index_b, cross_grads, memory, hid, h2, self_mix, cross_w, dco, vectors, length)
    h1, self_mg, self_delta, cross_keep, cross_send, small_sums = hold(
        groups, (h1, self_mg, self_delta, cross_keep, cross_send, small_sums))
    for group in groups:
        group.add()
    if fast:
        groups.append(Reduction(net, cross_keep, cross_send, 1280))
    self_grads = backward(True, self_plan, (qkv, 0), (qkv, 1), (qkv, 2), self_delta, self_mg, self_lse, tseg)
    for group in groups:
        group.start()
    self_keep, self_send, lines = self_grad(net.count if fast else 0, index_a, index_b, self_grads, target, mid_small, small_sums)
    self_keep, self_send, lines = hold(groups, (self_keep, self_send, lines))
    for group in groups:
        group.add()

    if not fast:
        target_out = target_grad(h1, self_grads, w_qkv)
        memory_grad = memory_back(*cross_grads[1:], cross_w)
        total = lambda x: lax.psum_scatter(low(x), AXES, scatter_dimension=0, tiled=True).astype(F32) if net.count > 1 else wide(x)
        whole = lambda keep, send: jnp.concatenate([keep, send], axis=0).reshape(512, -1)
        d_self, d_cross, d_ffn = whole(self_keep, self_send), whole(cross_keep, cross_send), whole(ffn_keep, ffn_send)
        d_out = d_ffn[:, 2048:].reshape(-1, UNIT, 4, 512).transpose(0, 2, 1, 3).reshape(2048, 512)
        weights = (jnp.concatenate([d_self[:, :768], d_self[:, 896:]], axis=1), d_cross[:, 1024:1536],
                   d_cross[:, :512], d_cross[:, 1536:], d_cross[:, 512:1024], d_ffn[:, :2048], d_out)
        return (output, target_out, memory_grad, *[total(w) for w in weights], *[total(lines[j, :n]) for j, n in enumerate(VECTORS)])

    groups.append(Reduction(net, self_keep, self_send, 896))
    target_out = None
    while any(group.sums is None for group in groups):
        open_groups = [group for group in groups if group.sums is None]
        tied = tuple(x for group in open_groups for x in group.state())
        for group in open_groups:
            group.start()
        if groups[-1].stage == 1:
            target_out = target_grad(h1, self_grads, w_qkv, tied)
        if groups[-1].stage == 2:
            memory_grad = memory_back(*cross_grads[1:], cross_w, tied)
        for group in open_groups:
            group.add()
        together([group for group in open_groups if group.sums is None])
    d_ffn, d_cross, d_self = (group.sums for group in groups)
    vectors_out = [d_self[j, 768:768 + n // net.count] for j, n in enumerate(VECTORS)]
    return (
        output, target_out, memory_grad,
        jnp.concatenate([d_self[:, :768], d_self[:, 896:]], axis=1), d_cross[:, 1024:1536],
        d_cross[:, :512], d_cross[:, 1536:], d_cross[:, 512:1024],
        d_ffn[:, :2048], jnp.concatenate([d_ffn[:, 2048 + 512 * b:2560 + 512 * b] for b in range(4)], axis=0),
        *vectors_out,
    )


def solution(mesh):
    both = ("wide", "narrow")
    matrix, vector = P(both, None), P(both)
    return jax.shard_map(
        per_device, mesh=mesh,
        in_specs=(matrix,) * 13 + (vector,) * 10,
        out_specs=(matrix,) * 10 + (vector,) * 10,
        check_vma=False,
    )
```

```python
import functools

import jax
import jax.numpy as jnp
from jax import lax
from jax.experimental import pallas as pl
from jax.experimental.pallas import tpu as pltpu
from jax.sharding import PartitionSpec as P

MASKED = -1e30
EPSILON = 1e-05
BLOCK = 128
WINDOW = 256
UNIT = 16
AXES = ("wide", "narrow")
NT = (((1,), (1,)), ((), ()))
TN = (((0,), (0,)), ((), ()))
NN = (((1,), (0,)), ((), ()))
BF = jnp.bfloat16
F32 = jnp.float32


def mxu(a, b, dims=NN):
    return lax.dot_general(a, b, dims, preferred_element_type=F32)


def low(x):
    return x.astype(BF)


def wide(x):
    return x.astype(F32)


def shape_of(shape, dtype=BF):
    return jax.ShapeDtypeStruct(shape, dtype)


def smem():
    return pl.BlockSpec(memory_space=pltpu.SMEM)


def vmem():
    return pl.BlockSpec(memory_space=pltpu.VMEM)


def fixed(shape, *index):
    return pl.BlockSpec(shape, lambda i, index=index: index, pipeline_mode=pl.Buffered(1))


def tiled(rows, cols, col=0):
    return pl.BlockSpec((rows, cols), lambda i, col=col: (i, col))


def params(mib):
    return pltpu.CompilerParams(vmem_limit_bytes=mib << 20)


def cost(micros):
    return pl.CostEstimate(flops=int(micros * 1e9), bytes_accessed=1 << 20, transcendentals=0)


def lane_masks(scale):
    lane = lax.broadcasted_iota(jnp.int32, (1, 128), 1)
    return low(jnp.where(lane < 64, scale, 0.0)), low(jnp.where(lane < 64, 0.0, scale))


def stacked(pair, masks):
    return jnp.concatenate([pair * masks[0], pair * masks[1]], axis=0)


def pick(both):
    sub = lax.broadcasted_iota(jnp.int32, (128, BLOCK), 0)
    return jnp.where(sub < 64, both[:, :BLOCK], both[:, BLOCK:])


def columns_of(row):
    return jnp.transpose(jnp.broadcast_to(row, (128, row.shape[1])))


def prepare_masks(causal, qseg_ref, kseg_ref, qone, kout, still):
    lane = wide(lax.broadcasted_iota(jnp.int32, (1, 128), 1))
    qone[...] = low(jnp.where(columns_of(qseg_ref[0]) == lane, 1.0, 0.0))
    kout[...] = low(jnp.where(columns_of(kseg_ref[0]) == lane, 0.0, MASKED))
    if causal:
        key = lax.broadcasted_iota(jnp.int32, (WINDOW, BLOCK), 0)
        query = lax.broadcasted_iota(jnp.int32, (WINDOW, BLOCK), 1)
        still[0] = jnp.where(key <= query, 0.0, MASKED)
        still[1] = jnp.where(key <= query + BLOCK, 0.0, MASKED)
        still[2] = jnp.zeros((WINDOW, BLOCK), F32)
        still[3] = jnp.where(key < BLOCK, 0.0, MASKED)


MASK_SCRATCH = lambda length: [pltpu.VMEM((length, 128), BF), pltpu.VMEM((length, 128), BF), pltpu.VMEM((4, WINDOW, BLOCK), F32)]


def bias_of(causal, still, qb, c, start, bound):
    if causal:
        at = jnp.minimum(qb, 1) if c is None else jnp.where(bound < WINDOW, 3, 2)
        return still[at]
    if c is None:
        return None
    key = lax.broadcasted_iota(jnp.int32, (WINDOW, BLOCK), 0) + start
    return jnp.where(key >= bound, 0.0, MASKED)


def masked(scores, bias):
    return scores if bias is None else scores + jnp.concatenate([bias, bias], axis=1)


def window(causal, first_ref, r, qb, c, length):
    c = 0 if c is None else c
    if causal:
        end = (qb + 1) * BLOCK - c * WINDOW
        return pl.multiple_of(jnp.maximum(end - WINDOW, 0), BLOCK), end
    begin = first_ref[r, qb] + c * WINDOW
    return pl.multiple_of(jnp.minimum(begin, length - WINDOW), 16), begin


def lanes_at(offset, p):
    return slice(offset + 128 * p, offset + 128 * p + 128)


UNROLL = 4


def most(extra_ref, r, qbs):
    count = extra_ref[r, qbs[0]]
    for qb in qbs[1:]:
        count = jnp.maximum(count, extra_ref[r, qb])
    return count


def attend(causal, r, first_ref, extra_ref, q, k, v, out_ref, lse_ref, masking, top, total, mix):
    length = q[0].shape[0]
    masks = lane_masks(0.125)
    joint = 2 if causal else 1
    qone, kout, still = masking

    def windows(qbs, c):
        scores, values, biases = [], [], []
        for qb in qbs:
            q0 = pl.multiple_of(qb * BLOCK, BLOCK)
            start, bound = window(causal, first_ref, r, qb, c, length)
            bias = bias_of(causal, still, qb, c, start, bound)
            queries, keys = qone[pl.ds(q0, BLOCK), :], kout[pl.ds(start, WINDOW), :]
            queries = jnp.concatenate([queries, queries], axis=0)
            for p in range(4):
                qs = jnp.concatenate([stacked(q[0][pl.ds(q0, BLOCK), lanes_at(q[1], p)], masks), queries], axis=1)
                ks = jnp.concatenate([k[0][pl.ds(start, WINDOW), lanes_at(k[1], p)], keys], axis=1)
                scores.append(mxu(ks, qs, NT))
                values.append(v[0][pl.ds(start, WINDOW), lanes_at(v[1], p)])
                biases.append(bias)
        return [masked(x, bias) for x, bias in zip(scores, biases)], values

    def step(i, _):
        qbs = [i * UNROLL + u for u in range(UNROLL)]
        scores, values = windows(qbs, None)
        highs = [jnp.max(x, axis=0, keepdims=True) for x in scores]
        weights = [jnp.exp(x - high) for x, high in zip(scores, highs)]
        sums = [jnp.sum(x, axis=0, keepdims=True) for x in weights]
        mixed = [pick(mxu(val, low(x), TN)) for val, x in zip(values, weights)]
        for n in range(4 * UNROLL):
            top[n] = highs[n]
            total[n] = sums[n]
            mix[n] = mixed[n]
        for u in range(0, UNROLL, joint):
            def more(c, _, u=u):
                scores, values = windows(qbs[u:u + joint], c + 1)
                highs = [jnp.maximum(top[4 * u + p], jnp.max(x, axis=0, keepdims=True)) for p, x in enumerate(scores)]
                weights = [jnp.exp(x - high) for x, high in zip(scores, highs)]
                mixed = [pick(mxu(val, low(x), TN)) for val, x in zip(values, weights)]
                for p in range(4 * joint):
                    n = 4 * u + p
                    fade = jnp.exp(top[n] - highs[p])
                    top[n] = highs[p]
                    total[n] = total[n] * fade + jnp.sum(weights[p], axis=0, keepdims=True)
                    mix[n] = mix[n] * pick(jnp.broadcast_to(fade, (128, 2 * BLOCK))) + mixed[p]
                return 0

            lax.fori_loop(0, most(extra_ref, r, qbs[u:u + joint]), more, 0)
        for u, qb in enumerate(qbs):
            q0 = pl.multiple_of(qb * BLOCK, BLOCK)
            for p in range(4):
                sums = total[4 * u + p]
                inverse = pick(jnp.broadcast_to(1.0 / sums, (128, 2 * BLOCK)))
                out_ref[pl.ds(q0, BLOCK), lanes_at(0, p)] = low(jnp.transpose(mix[4 * u + p] * inverse))
                lse = top[4 * u + p] + jnp.log(sums)
                lse_ref[0, 2 * p:2 * p + 1, pl.ds(q0, BLOCK)] = lse[:, :BLOCK]
                lse_ref[0, 2 * p + 1:2 * p + 2, pl.ds(q0, BLOCK)] = lse[:, BLOCK:]
        return 0

    lax.fori_loop(0, length // BLOCK // UNROLL, step, 0)


ATTEND_SCRATCH = lambda length: MASK_SCRATCH(length) + [
    pltpu.VMEM((4 * UNROLL, 1, 2 * BLOCK), F32),
    pltpu.VMEM((4 * UNROLL, 1, 2 * BLOCK), F32), pltpu.VMEM((4 * UNROLL, 128, BLOCK), F32)]


def norm(hidden):
    average = jnp.mean(hidden, axis=-1, keepdims=True)
    centred = hidden - average
    inverse = lax.rsqrt(jnp.mean(centred * centred, axis=-1, keepdims=True) + EPSILON)
    return centred * inverse, inverse


def norm_back(grad, normed, inverse, gain):
    scaled = grad * gain
    return inverse * (scaled - jnp.mean(scaled, axis=-1, keepdims=True)
                      - normed * jnp.mean(scaled * normed, axis=-1, keepdims=True))


def head_sums(grad, mix):
    lane = lax.broadcasted_iota(jnp.int32, (16, 512), 1) // 64
    heads = low(jnp.where(lane == lax.broadcasted_iota(jnp.int32, (16, 512), 0), 1.0, 0.0))
    return mxu(heads, low(wide(grad) * wide(mix)), NT)[:8]


def rows_spec(t, length):
    per = length // t
    return pl.BlockSpec((1, 8, t), lambda i: (i // per, 0, i % per))


def accumulate(ref, where, value):
    ref[where] = jnp.where(pl.program_id(0) == 0, 0.0, ref[where]) + value


def sum_rows(x):
    return jnp.sum(wide(x), axis=0, keepdims=True)


S_BIAS, S_GAIN, S_SHIFT, C_BIAS, C_GAIN, C_SHIFT, I_BIAS, O_BIAS, F_GAIN, F_SHIFT = range(10)


def vec(ref, row, block=0, size=512):
    return ref[row:row + 1, block * size:(block + 1) * size]


def self_kernel(first_ref, extra_ref, x_ref, w_ref, vec_ref, seg_ref, qkv_ref, mix_ref, lse_ref, qone, kout, still, *state):
    r = pl.program_id(0)
    prepare_masks(True, seg_ref, seg_ref, qone, kout, still)
    x = x_ref[...]
    qkv_ref[:, :512] = low(mxu(x, w_ref[:, :512]) + vec(vec_ref, S_BIAS, 0))
    qkv_ref[:, 512:1024] = low(mxu(x, w_ref[:, 512:1024]))
    qkv_ref[:, 1024:] = low(mxu(x, w_ref[:, 1024:]) + vec(vec_ref, S_BIAS, 1))
    attend(True, r, first_ref, extra_ref, (qkv_ref, 0), (qkv_ref, 512), (qkv_ref, 1024), mix_ref, lse_ref,
           (qone, kout, still), *state)


def self_forward(plan, x, w, vectors, seg):
    rows, _, length = seg.shape
    return pl.pallas_call(
        self_kernel, grid=(rows,),
        in_specs=[smem(), smem(), tiled(length, 512), fixed((512, 1536), 0, 0), fixed((16, 2048), 0, 0),
                  pl.BlockSpec((1, 1, length), lambda i: (i, 0, 0))],
        out_specs=[tiled(length, 1536), tiled(length, 512), pl.BlockSpec((1, 8, length), lambda i: (i, 0, 0))],
        out_shape=[pltpu.HBM((rows * length, 1536), BF), pltpu.HBM((rows * length, 512), BF), shape_of((rows, 8, length), F32)],
        scratch_shapes=ATTEND_SCRATCH(length), compiler_params=params(40), cost_estimate=cost(20), name="self_forward",
    )(*plan, x, w, vectors, seg)


def cross_kernel(first_ref, extra_ref, x_ref, mix_ref, mem_ref, wo_ref, wq_ref, wkv_ref, vec_ref, qseg_ref, kseg_ref,
                 hid_ref, q_ref, kv_ref, out_ref, lse_ref, qone, kout, still, *state):
    r = pl.program_id(0)
    prepare_masks(False, qseg_ref, kseg_ref, qone, kout, still)
    hidden = wide(x_ref[...]) + mxu(mix_ref[...], wo_ref[...]) + vec(vec_ref, S_BIAS, 2)
    hid_ref[...] = low(hidden)
    first = low(norm(hidden)[0] * vec(vec_ref, S_GAIN) + vec(vec_ref, S_SHIFT))
    q_ref[...] = low(mxu(first, wq_ref[...]) + vec(vec_ref, C_BIAS, 0))
    mem = mem_ref[...]
    kv_ref[:, :512] = low(mxu(mem, wkv_ref[:, :512]))
    kv_ref[:, 512:] = low(mxu(mem, wkv_ref[:, 512:]) + vec(vec_ref, C_BIAS, 1))
    attend(False, r, first_ref, extra_ref, (q_ref, 0), (kv_ref, 0), (kv_ref, 512), out_ref, lse_ref,
           (qone, kout, still), *state)


def cross_forward(plan, x, mix, mem, weights, vectors, qseg, kseg):
    rows, _, length = qseg.shape
    seg = pl.BlockSpec((1, 1, length), lambda i: (i, 0, 0))
    total = rows * length
    return pl.pallas_call(
        cross_kernel, grid=(rows,),
        in_specs=[smem(), smem(), tiled(length, 512), tiled(length, 512), tiled(length, 512),
                  fixed((512, 512), 0, 0), fixed((512, 512), 0, 1), fixed((512, 1024), 0, 1), fixed((16, 2048), 0, 0), seg, seg],
        out_specs=[tiled(length, 512), tiled(length, 512), tiled(length, 1024), tiled(length, 512),
                   pl.BlockSpec((1, 8, length), lambda i: (i, 0, 0))],
        out_shape=[shape_of((total, 512)), shape_of((total, 512)), shape_of((total, 1024)), shape_of((total, 512)),
                   shape_of((rows, 8, length), F32)],
        scratch_shapes=ATTEND_SCRATCH(length), compiler_params=params(60), cost_estimate=cost(25), name="cross_forward",
    )(*plan, x, mix, mem, weights, weights, weights, vectors, qseg, kseg)


def pair_row(ref, p, q0):
    return jnp.concatenate([ref[0, 2 * p + h:2 * p + h + 1, pl.ds(q0, BLOCK)] for h in range(2)], axis=1)


def back_kernel(causal, first_ref, extra_ref, q_ref, k_ref, v_ref, delta_ref, grad_ref, lse_ref, qseg_ref, kseg_ref, *refs):
    dq_ref, dk_ref, dv_ref, qone, kout, still, dk, dv, dq = refs[-9:]
    r = pl.program_id(0)
    length = q_ref.shape[0]
    joint = 2 if causal else 1
    prepare_masks(causal, qseg_ref, kseg_ref, qone, kout, still)
    dk[...] = jnp.zeros_like(dk)
    dv[...] = jnp.zeros_like(dv)
    masks = lane_masks(0.125)
    ones = lane_masks(1.0)

    def windows(qbs, c):
        places, qs, gs, deltas, lses, keys, biases, scores = [], [], [], [], [], [], [], []
        for qb in qbs:
            q0 = pl.multiple_of(qb * BLOCK, BLOCK)
            start, bound = window(causal, first_ref, r, qb, c, length)
            bias = bias_of(causal, still, qb, c, start, bound)
            queries, outs = qone[pl.ds(q0, BLOCK), :], kout[pl.ds(start, WINDOW), :]
            queries = jnp.concatenate([queries, queries], axis=0)
            for p in range(4):
                lanes = lanes_at(0, p)
                grad = grad_ref[pl.ds(q0, BLOCK), lanes]
                deltas.append(pair_row(delta_ref, p, q0))
                lses.append(pair_row(lse_ref, p, q0))
                qs.append(stacked(q_ref[pl.ds(q0, BLOCK), lanes], masks))
                gs.append(stacked(grad, ones))
                keys.append(k_ref[pl.ds(start, WINDOW), lanes])
                places.append((pl.ds(start, WINDOW), lanes))
                biases.append(bias)
                scores.append(mxu(jnp.concatenate([keys[-1], outs], axis=1), jnp.concatenate([qs[-1], queries], axis=1), NT))
        dprobs = [mxu(v_ref[place], g, NT) for place, g in zip(places, gs)]
        probs = [jnp.exp(masked(x, bias) - lse) for x, bias, lse in zip(scores, biases, lses)]
        dscores = [low(x * (d - delta)) for x, d, delta in zip(probs, dprobs, deltas)]
        new_dv = [mxu(low(x), g) for x, g in zip(probs, gs)]
        new_dk = [mxu(d, x) for d, x in zip(dscores, qs)]
        parts = [pick(mxu(key, d, TN)) for key, d in zip(keys, dscores)]
        for place, more_dv, more_dk in zip(places, new_dv, new_dk):
            dv[place] += more_dv
            dk[place] += more_dk
        return parts

    def step(i, _):
        qbs = [i * UNROLL + u for u in range(UNROLL)]
        for n, part in enumerate(windows(qbs, None)):
            dq[n] = part
        for u in range(0, UNROLL, joint):
            def more(c, _, u=u):
                for p, part in enumerate(windows(qbs[u:u + joint], c + 1)):
                    dq[4 * u + p] += part
                return 0

            lax.fori_loop(0, most(extra_ref, r, qbs[u:u + joint]), more, 0)
        for u, qb in enumerate(qbs):
            q0 = pl.multiple_of(qb * BLOCK, BLOCK)
            for p in range(4):
                dq_ref[pl.ds(q0, BLOCK), lanes_at(0, p)] = low(jnp.transpose(dq[4 * u + p]) * 0.125)
        return 0

    lax.fori_loop(0, length // BLOCK // UNROLL, step, 0)
    dk_ref[...] = low(dk[...])
    dv_ref[...] = low(dv[...])


def attend_back(causal, plan, q, k, v, delta, grad, lse, qseg, kseg, after=()):
    rows, _, length = qseg.shape
    seg = pl.BlockSpec((1, 1, length), lambda i: (i, 0, 0))
    line = pl.BlockSpec((1, 8, length), lambda i: (i, 0, 0))
    return pl.pallas_call(
        functools.partial(back_kernel, causal), grid=(rows,),
        in_specs=[smem(), smem(), tiled(length, 512, q[1]), tiled(length, 512, k[1]), tiled(length, 512, v[1]), line,
                  tiled(length, 512), line, seg, seg] + [pl.BlockSpec(memory_space=pl.ANY)] * len(after),
        out_specs=[tiled(length, 512)] * 3, out_shape=[shape_of((rows * length, 512))] * 3,
        scratch_shapes=MASK_SCRATCH(length) + [pltpu.VMEM((length, 512), F32), pltpu.VMEM((length, 512), F32),
                                               pltpu.VMEM((4 * UNROLL, 128, BLOCK), F32)],
        compiler_params=params(40 if causal else 60), cost_estimate=cost(20), name="self_back" if causal else "cross_back",
    )(*plan, q[0], k[0], v[0], delta, grad, lse, qseg, kseg, *after)


def emit(outs, col, acc, index_ref, acc_col, width):
    half = outs[0].shape[0]
    for r in range(512 // UNIT):
        row = pl.multiple_of(index_ref[r] * UNIT, UNIT)
        outs[r // half][r % half, :, col:col + width] = low(acc[pl.ds(row, UNIT), acc_col:acc_col + width])


def halves(width):
    half = 512 // UNIT // 2
    return [fixed((half, UNIT, width), 0, 0, 0)] * 2, [shape_of((half, UNIT, width))] * 2


MID_TILE = 512
PARTS = 2
CHUNK = 1024


def mid_kernel(index_a, index_b, hid_ref, mix_ref, grad_ref, win_ref, gout_ref, wco_ref, vec_ref,
               out_ref, h2_ref, mg_ref, delta_ref, keep_ref, send_ref, co_ref, small_ref,
               wout, dwin, dwout, dwco, act, slope):
    step = pl.program_id(0)
    hidden_width = win_ref.shape[1]
    tokens = hid_ref.shape[0]

    @pl.when(step == 0)
    def _():
        for d in range(512 // UNIT):
            for b in range(4):
                wout[(4 * d + b) * UNIT:(4 * d + b + 1) * UNIT, :] = gout_ref[d * UNIT:(d + 1) * UNIT, 512 * b:512 * b + 512]
        small_ref[...] = jnp.zeros_like(small_ref)

    chunks = [slice(c, c + CHUNK) for c in range(0, hidden_width, CHUNK)]
    part = tokens // PARTS
    parts = [slice(i * part, i * part + part) for i in range(PARTS)]
    firsts = [norm(wide(hid_ref[t, :]))[0] * vec(vec_ref, S_GAIN) + vec(vec_ref, S_SHIFT) for t in parts]
    norms2 = [norm(first + mxu(mix_ref[t, :], wco_ref[...]) + vec(vec_ref, C_BIAS, 2)) for t, first in zip(parts, firsts)]
    seconds = [normed * vec(vec_ref, C_GAIN) + vec(vec_ref, C_SHIFT) for normed, _ in norms2]
    lows = [low(second) for second in seconds]
    norms3 = []
    for t, second, second_low in zip(parts, seconds, lows):
        hidden3 = second + vec(vec_ref, O_BIAS)
        for c in chunks:
            pre = mxu(second_low, win_ref[:, c]) + vec_ref[I_BIAS:I_BIAS + 1, c]
            sig = 0.5 + 0.5 * jnp.tanh(0.5 * pre)
            active = low(pre * sig)
            act[t, c] = active
            slope[t, c] = sig * (1.0 + pre * (1.0 - sig))
            hidden3 += mxu(active, wout[c, :])
        norms3.append(norm(hidden3))
    backs3 = []
    for t, (normed3, inverse3) in zip(parts, norms3):
        out_ref[t, :] = low(normed3 * vec(vec_ref, F_GAIN) + vec(vec_ref, F_SHIFT))
        grad = wide(grad_ref[t, :])
        backs3.append(norm_back(grad, normed3, inverse3, vec(vec_ref, F_GAIN)))
        small_ref[2:3, :512] += sum_rows(grad * normed3)
        small_ref[3:4, :512] += sum_rows(grad)
    b3s = [low(back3) for back3 in backs3]
    us = [[] for _ in chunks]
    grads2 = []
    for t, back3, b3 in zip(parts, backs3, b3s):
        grad2 = back3
        for n, c in enumerate(chunks):
            u = low(mxu(b3, wout[c, :], NT) * slope[t, c])
            us[n].append(u)
            grad2 += mxu(u, win_ref[:, c], NT)
        grads2.append(grad2)
    b2s = []
    for t, grad2, (normed2, inverse2) in zip(parts, grads2, norms2):
        h2 = norm_back(grad2, normed2, inverse2, vec(vec_ref, C_GAIN))
        b2 = low(h2)
        h2_ref[t, :] = b2
        b2s.append(b2)
        small_ref[4:5, :512] += sum_rows(grad2 * normed2)
        small_ref[5:6, :512] += sum_rows(grad2)
    second_low = jnp.concatenate(lows, axis=0)
    b3 = jnp.concatenate(b3s, axis=0)
    second_t = jnp.transpose(second_low)
    small_ref[1:2, :512] += sum_rows(b3)
    for n, c in enumerate(chunks):
        u = jnp.concatenate(us[n], axis=0)
        accumulate(dwin, (slice(None), c), mxu(second_t, u))
        accumulate(dwout, (c, slice(None)), mxu(act[:, c], b3, TN))
        small_ref[0:1, c] += sum_rows(u)
    b2 = jnp.concatenate(b2s, axis=0)
    small_ref[6:7, :512] += sum_rows(b2)
    accumulate(dwco, ..., mxu(jnp.transpose(mix_ref[...]), b2))
    mix_grad = low(mxu(b2, wco_ref[...], NT))
    mg_ref[...] = mix_grad
    delta_ref[0] = head_sums(mix_grad, mix_ref[...])

    @pl.when(step == pl.num_programs(0) - 1)
    def _():
        outs = keep_ref, send_ref
        emit(outs, 0, dwin, index_a, 0, hidden_width)
        half = keep_ref.shape[0]
        for r in range(512 // UNIT):
            for b in range(4):
                row = pl.multiple_of((index_b[r] * 4 + b) * UNIT, UNIT)
                outs[r // half][r % half, :, 2048 + 512 * b:2560 + 512 * b] = low(dwout[pl.ds(row, UNIT), :])
        co_ref[...] = dwco[...]


def middle(index_a, index_b, hid, mix, grad, rest, vectors, length):
    total = hid.shape[0]
    t = MID_TILE
    specs, shapes = halves(4096)
    return pl.pallas_call(
        mid_kernel, grid=(total // t,),
        in_specs=[smem(), smem(), tiled(t, 512), tiled(t, 512), tiled(t, 512),
                  fixed((512, 2048), 0, 0), fixed((512, 2048), 0, 1), fixed((512, 512), 0, 8), fixed((16, 2048), 0, 0)],
        out_specs=[tiled(t, 512)] * 3 + [rows_spec(t, length)] + specs + [fixed((512, 512), 0, 0), fixed((8, 2048), 0, 0)],
        out_shape=[shape_of((total, 512))] * 3 + [shape_of((total // length, 8, length), F32)] + shapes
        + [shape_of((512, 512), F32), shape_of((8, 2048), F32)],
        scratch_shapes=[pltpu.VMEM((2048, 512), BF), pltpu.VMEM((512, 2048), F32), pltpu.VMEM((2048, 512), F32),
                        pltpu.VMEM((512, 512), F32), pltpu.VMEM((t, 2048), BF), pltpu.VMEM((t, 2048), F32)],
        compiler_params=params(62), cost_estimate=cost(40), name="middle",
    )(index_a, index_b, hid, mix, grad, rest, rest, rest, vectors)


DENSE_TILE = 512
SELF_TILE = 1024


def cross_dense_kernel(index_a, index_b, cq_ref, ck_ref, cv_ref, mem_ref, hid_ref, h2_ref, mix_ref,
                       wq_ref, wo_ref, co_ref, vec_ref,
                       h1_ref, mg_ref, delta_ref, keep_ref, send_ref, small_ref, dq, dkv, do):
    step = pl.program_id(0)

    @pl.when(step == 0)
    def _():
        small_ref[...] = jnp.zeros_like(small_ref)

    cq, ck, cv = cq_ref[...], ck_ref[...], cv_ref[...]
    normed, inverse = norm(wide(hid_ref[...]))
    first = low(normed * vec(vec_ref, S_GAIN) + vec(vec_ref, S_SHIFT))
    grad1 = wide(h2_ref[...]) + mxu(cq, wq_ref[...], NT)
    h1 = norm_back(grad1, normed, inverse, vec(vec_ref, S_GAIN))
    b1 = low(h1)
    h1_ref[...] = b1
    mix_grad = low(mxu(b1, wo_ref[...], NT))
    mg_ref[...] = mix_grad
    delta_ref[0] = head_sums(mix_grad, mix_ref[...])
    accumulate(dq, ..., mxu(jnp.transpose(first), cq))
    mem_t = jnp.transpose(mem_ref[...])
    accumulate(dkv, (slice(None), slice(0, 512)), mxu(mem_t, ck))
    accumulate(dkv, (slice(None), slice(512, 1024)), mxu(mem_t, cv))
    accumulate(do, ..., mxu(jnp.transpose(mix_ref[...]), b1))
    small_ref[0:1, :] += sum_rows(cq)
    small_ref[1:2, :] += sum_rows(cv)
    small_ref[2:3, :] += sum_rows(grad1 * normed)
    small_ref[3:4, :] += sum_rows(grad1)
    small_ref[4:5, :] += sum_rows(b1)

    @pl.when(step == pl.num_programs(0) - 1)
    def _():
        outs = keep_ref, send_ref
        emit(outs, 0, dq, index_a, 0, 512)
        emit(outs, 512, co_ref, index_a, 0, 512)
        emit(outs, 1024, do, index_a, 0, 256)
        emit(outs, 1280, do, index_b, 256, 256)
        emit(outs, 1536, dkv, index_b, 0, 1024)


def cross_dense(index_a, index_b, grads, mem, hid, h2, mix, weights, dco, vectors, length):
    total = hid.shape[0]
    t = DENSE_TILE
    specs, shapes = halves(2560)
    return pl.pallas_call(
        cross_dense_kernel, grid=(total // t,),
        in_specs=[smem(), smem()] + [tiled(t, 512)] * 7
        + [fixed((512, 512), 0, 1), fixed((512, 512), 0, 0), fixed((512, 512), 0, 0), fixed((16, 2048), 0, 0)],
        out_specs=[tiled(t, 512)] * 2 + [rows_spec(t, length)] + specs + [fixed((8, 512), 0, 0)],
        out_shape=[shape_of((total, 512))] * 2 + [shape_of((total // length, 8, length), F32)] + shapes + [shape_of((8, 512), F32)],
        scratch_shapes=[pltpu.VMEM((512, 512), F32), pltpu.VMEM((512, 1024), F32), pltpu.VMEM((512, 512), F32)],
        compiler_params=params(40), cost_estimate=cost(12), name="cross_dense",
    )(index_a, index_b, *grads, mem, hid, h2, mix, weights, weights, dco, vectors)


def memory_kernel(ck_ref, cv_ref, w_ref, *refs):
    refs[-1][...] = low(mxu(ck_ref[...], w_ref[:, :512], NT) + mxu(cv_ref[...], w_ref[:, 512:], NT))


def memory_back(ck, cv, weights, after=()):
    total = ck.shape[0]
    t = 512
    return pl.pallas_call(
        memory_kernel, grid=(total // t,), in_specs=[tiled(t, 512)] * 2 + [fixed((512, 1024), 0, 1)]
        + [pl.BlockSpec(memory_space=pl.ANY)] * len(after),
        out_specs=tiled(t, 512), out_shape=shape_of((total, 512)), compiler_params=params(40), cost_estimate=cost(4), name="memory_grad",
    )(ck, cv, weights, *after)


VECTORS = (1536, 512, 512, 1536, 512, 512, 2048, 512, 512, 512)


def places(n, per, count, axis):
    shape = (1, n)
    at = wide(lax.broadcasted_iota(jnp.int32, shape, 1))
    owner = jnp.floor((at + 0.5) * (1.0 / per))
    return owner, at - owner * per


def one_hot(n, per):
    _, place = places(n, per, n // per, 1)
    return low(jnp.where(wide(lax.broadcasted_iota(jnp.int32, (128, n), 0)) == place, 1.0, 0.0))


def owned(n, per, count):
    owner, _ = places(n, per, count, 1)
    return wide(lax.broadcasted_iota(jnp.int32, (count, n), 0)) == owner


def self_grad_kernel(count, index_a, index_b, dq_ref, dk_ref, dv_ref, x_ref, mid_ref, small_ref, keep_ref, send_ref, lines_ref, dw, table):
    step = pl.program_id(0)

    @pl.when(step == 0)
    def _():
        lines_ref[...] = jnp.zeros_like(lines_ref)

    x_t = jnp.transpose(x_ref[...])
    accumulate(dw, (slice(None), slice(0, 512)), mxu(x_t, dq_ref[...]))
    accumulate(dw, (slice(None), slice(512, 1024)), mxu(x_t, dk_ref[...]))
    accumulate(dw, (slice(None), slice(1024, 1536)), mxu(x_t, dv_ref[...]))
    lines_ref[S_BIAS:S_BIAS + 1, :512] += sum_rows(dq_ref[...])
    lines_ref[S_BIAS:S_BIAS + 1, 512:1024] += sum_rows(dv_ref[...])

    @pl.when(step == pl.num_programs(0) - 1)
    def _():
        outs = keep_ref, send_ref
        emit(outs, 0, dw, index_a, 0, 768)
        emit(outs, 768, dw, index_b, 768, 768)
        for row, col, source, source_row in (
            (S_BIAS, 1024, small_ref, 4), (S_GAIN, 0, small_ref, 2), (S_SHIFT, 0, small_ref, 3),
            (C_BIAS, 0, small_ref, 0), (C_BIAS, 512, small_ref, 1), (C_BIAS, 1024, mid_ref, 6),
            (C_GAIN, 0, mid_ref, 4), (C_SHIFT, 0, mid_ref, 5),
            (O_BIAS, 0, mid_ref, 1), (F_GAIN, 0, mid_ref, 2), (F_SHIFT, 0, mid_ref, 3),
        ):
            lines_ref[row:row + 1, col:col + 512] = source[source_row:source_row + 1, :512]
        lines_ref[I_BIAS:I_BIAS + 1, :] = mid_ref[0:1, :]
        if count:
            table[...] = jnp.zeros_like(table)
            for n in (512, 1536, 2048):
                hot, mine = one_hot(n, n // count), owned(n, n // count, count)
                for j, size in enumerate(VECTORS):
                    if size == n:
                        line = jnp.broadcast_to(lines_ref[j:j + 1, :n], (count, n))
                        table[:, j, :] = mxu(low(jnp.where(mine, line, 0.0)), hot, NT)
            for r in range(count):
                outs[2 * r // count][r % (count // 2), :, 1536:] = low(table[index_b[r]])


def self_grad(count, index_a, index_b, grads, x, mid_small, small):
    total = x.shape[0]
    t = SELF_TILE
    specs, shapes = halves(1664)
    return pl.pallas_call(
        functools.partial(self_grad_kernel, count), grid=(total // t,),
        in_specs=[smem(), smem()] + [tiled(t, 512)] * 4 + [fixed((8, 2048), 0, 0), fixed((8, 512), 0, 0)],
        out_specs=specs + [fixed((16, 2048), 0, 0)],
        out_shape=shapes + [shape_of((16, 2048), F32)],
        scratch_shapes=[pltpu.VMEM((512, 1536), F32), pltpu.VMEM((max(count, 8), 16, 128), F32)],
        compiler_params=params(40), cost_estimate=cost(5), name="self_grad",
    )(index_a, index_b, *grads, x, mid_small, small)


def target_kernel(h1_ref, dq_ref, dk_ref, dv_ref, w_ref, *refs):
    out_ref = refs[-1]
    total = wide(h1_ref[...]) + mxu(dq_ref[...], w_ref[:, :512], NT)
    total += mxu(dk_ref[...], w_ref[:, 512:1024], NT)
    out_ref[...] = low(total + mxu(dv_ref[...], w_ref[:, 1024:], NT))


def target_grad(h1, grads, w, after=()):
    total = h1.shape[0]
    t = 512
    return pl.pallas_call(
        target_kernel, grid=(total // t,), in_specs=[tiled(t, 512)] * 4 + [fixed((512, 1536), 0, 0)]
        + [pl.BlockSpec(memory_space=pl.ANY)] * len(after),
        out_specs=tiled(t, 512), out_shape=shape_of((total, 512)), compiler_params=params(40), cost_estimate=cost(5), name="target_grad",
    )(h1, *grads, w, *after)


class Net:
    def __init__(self):
        self.wide = lax.axis_size("wide")
        self.narrow = lax.axis_size("narrow")
        self.count = self.wide * self.narrow
        self.wide_bits = self.wide.bit_length() - 1
        self.narrow_bits = self.narrow.bit_length() - 1
        self.bits = self.wide_bits + self.narrow_bits
        self.me = lax.axis_index("wide") * self.narrow + lax.axis_index("narrow")
        inner = list(range(self.narrow_bits))
        core, second = [self.narrow_bits], [self.narrow_bits + 1]
        far = list(range(self.narrow_bits + 2, self.bits))
        self.near = self.bits - len(far)
        self.orders = (core + second + inner + far, core + inner + second + far)

    def exchange(self, x, bit):
        if bit < self.narrow_bits:
            return lax.ppermute(x, "narrow", [(i, i ^ (1 << bit)) for i in range(self.narrow)])
        return self.across(x, 1 << bit)

    def across(self, x, mask):
        mask >>= self.narrow_bits
        return lax.ppermute(x, "wide", [(i, i ^ mask) for i in range(self.wide)])

    def far_masks(self, order):
        return [sum(((r >> s) & 1) << bit for s, bit in enumerate(order)) for r in range(1 << len(order))]

    def index(self, chain):
        order, n = self.orders[chain], self.bits
        mask = [sum(((r >> (n - 1 - s)) & 1) << bit for s, bit in enumerate(order)) for r in range(self.count)]
        return jnp.array(mask, jnp.int32) ^ self.me

    def gather_index(self, chain):
        order = self.orders[chain][::-1]
        mask = [sum(((r >> s) & 1) << bit for s, bit in enumerate(order)) for r in range(self.count)]
        return jnp.array(mask, jnp.int32) ^ self.me


def pack_kernel(*refs):
    vectors, (qkv, so, cq, ckv, co, fin, fout, packed_ref, cross_ref, rest_ref) = refs[:10], refs[10:20]
    lines, sem = refs[20:30], refs[30]
    moves = list(zip(vectors, lines))
    moves += [(qkv.at[:, :768], packed_ref.at[0, :, :768]), (qkv.at[:, 768:], packed_ref.at[0, :, 896:]), (fin, rest_ref.at[:, :2048])]
    moves += [(fout.at[UNIT * b:UNIT * b + UNIT, :], rest_ref.at[:, 2048 + 512 * b:2560 + 512 * b]) for b in range(4)]
    moves += [(co, rest_ref.at[:, 4096:]), (so, cross_ref.at[0, :, :512]),
              (cq, cross_ref.at[0, :, 512:1024]), (ckv, cross_ref.at[0, :, 1024:])]
    copies = [pltpu.make_async_copy(src, dst, sem.at[i]) for i, (src, dst) in enumerate(moves)]
    for copy in copies:
        copy.start()
    for copy in copies:
        copy.wait()
    rows = []
    for v in lines:
        line = wide(v[...])
        rows.append(jnp.concatenate([line, jnp.zeros((1, 128 - line.shape[1]), F32)], axis=1))
    rows.append(jnp.zeros((6, 128), F32))
    packed_ref[0, :, 768:896] = low(jnp.concatenate(rows, axis=0))


def unpack_kernel(count, index_a, index_b, *refs):
    n = (len(refs) - 3) // 2
    pieces_a, pieces_b, (w_ref, vec_ref, table) = refs[:n], refs[n:2 * n], refs[2 * n:]
    for pieces, index, col, width in ((pieces_a, index_a, 0, 768), (pieces_b, index_b, 768, 768)):
        r = 0
        for piece in pieces:
            for j in range(piece.shape[0]):
                owner = index[r]
                w_ref[pl.ds(pl.multiple_of(owner * UNIT, UNIT), UNIT), col:col + width] = piece[j, :, :width]
                if col == 0:
                    table[owner] = wide(piece[j, :, 768:896])
                r += 1
    vec_ref[...] = jnp.zeros_like(vec_ref)
    for n in (512, 1536, 2048):
        hot, mine = one_hot(n, n // count), owned(n, n // count, count)
        for j, size in enumerate(VECTORS):
            if size == n:
                spread = mxu(low(table[:, j, :]), hot)
                vec_ref[j:j + 1, :n] = jnp.sum(jnp.where(mine, spread, 0.0), axis=0, keepdims=True)


def place_kernel(index, *refs):
    pieces, w_ref = refs[:-1], refs[-1]
    r = 0
    for piece in pieces:
        for j in range(piece.shape[0]):
            row = pl.multiple_of(index[r] * UNIT, UNIT)
            w_ref[pl.ds(row, UNIT), :] = piece[j]
            r += 1


def gather_weights(net, small, big):
    qkv, so, cq, ckv, co, fin, fout = big
    if qkv.shape[0] % UNIT or net.bits < 5:
        small, big = lax.all_gather((small, big), AXES, axis=0, tiled=True) if net.count > 1 else (small, big)
        qkv, so, cq, ckv, co, fin, fout = big
        fout = fout.reshape(-1, 4, UNIT, 512).transpose(0, 2, 1, 3).reshape(512, 2048)
        rows = [jnp.pad(wide(v), (0, 2048 - v.shape[0])) for v in small]
        vectors = jnp.stack(rows + [jnp.zeros((2048,), F32)] * 6)
        return qkv, vectors, jnp.concatenate([fin, fout, co], axis=1), lambda x: (x, jnp.concatenate([so, cq, ckv], axis=1))
    packed, cross, rest = pl.pallas_call(
        pack_kernel, in_specs=[pl.BlockSpec(memory_space=pl.ANY)] * 17, out_specs=[vmem()] * 3,
        out_shape=[shape_of((1, UNIT, 1664)), shape_of((1, UNIT, 2048)), shape_of((UNIT, 4608))],
        scratch_shapes=[pltpu.VMEM((1, v.shape[0]), BF) for v in small] + [pltpu.SemaphoreType.DMA((21,))],
        compiler_params=params(60), cost_estimate=cost(2), name="pack",
    )(*[v[None] for v in small], *big)
    rest = lax.all_gather(rest, AXES, axis=0, tiled=True)
    orders = [order[::-1] for order in net.orders]
    far = net.bits - net.near
    masks = net.far_masks(orders[0][:far])[1:]
    everywhere = lambda x: jnp.concatenate([x] + [net.across(x, mask) for mask in masks], axis=0)
    packed = everywhere(packed)
    packed, cross = lax.optimization_barrier((packed, cross))
    cross = everywhere(cross)
    parts = [packed[:, :, :896], packed[:, :, 896:], cross]
    orders = orders + orders[:1]
    parts = [jnp.concatenate([x, net.exchange(x, order[far])], axis=0) for x, order in zip(parts, orders)]

    def spread(pieces, s):
        got = [[net.exchange(x, order[s]) for x in chain] for chain, order in zip(pieces, orders)]
        return [chain + more for chain, more in zip(pieces, got)]

    pieces = spread(spread([[x] for x in parts[:2]], far + 1), far + 2)
    later = spread([[x] for x in parts[2:]], far + 1)
    gather_index = [net.gather_index(0), net.gather_index(1)]

    def cross_weights(values):
        held, values = lax.optimization_barrier((later, values))
        held = spread(held, far + 2)
        return values, pl.pallas_call(
            place_kernel, in_specs=[smem()] + [vmem()] * len(held[0]), out_specs=vmem(),
            out_shape=pltpu.HBM((512, 2048), BF), compiler_params=params(32), cost_estimate=cost(2), name="place",
        )(gather_index[0], *held[0])

    w, vectors = pl.pallas_call(
        functools.partial(unpack_kernel, net.count), in_specs=[smem(), smem()] + [vmem()] * (len(pieces[0]) * 2), out_specs=[vmem()] * 2,
        out_shape=[shape_of((512, 1536)), shape_of((16, 2048), F32)],
        scratch_shapes=[pltpu.VMEM((net.count, 16, 128), F32)],
        compiler_params=params(40), cost_estimate=cost(2), name="unpack",
    )(*gather_index, *pieces[0], *pieces[1])
    return w, vectors, rest, cross_weights


class Reduction:
    def __init__(self, net, keep, send, cut):
        self.net, self.cut = net, cut
        self.keep, self.send = [keep], [send]
        self.stage = 0
        self.sums = None

    def state(self):
        return tuple(self.send) if self.sums is None else ()

    def start(self):
        if self.sums is not None:
            return
        if self.stage < self.net.near:
            self.got = [self.net.exchange(x, order[self.stage]) for x, order in zip(self.send, self.net.orders)]
        else:
            far = self.net.far_masks(self.net.orders[0][:self.net.near - 1:-1])
            self.got = [self.net.across(x, mask) for x, mask in zip(self.send, far[1:])]

    def add(self):
        if self.sums is not None:
            return
        self.stage += 1
        if self.stage > self.net.near:
            self.sums = sum((wide(got[0]) for got in self.got), self.keep[0][0])
            return
        sums = [wide(k) + wide(g) for k, g in zip(self.keep, self.got)]
        if self.stage == 1:
            sums = [sums[0][:, :, :self.cut], sums[0][:, :, self.cut:]]
        elif self.stage == self.net.near:
            total = jnp.concatenate(sums, axis=2)
            self.keep = [total[:1]]
            self.send = [low(total[r:r + 1]) for r in range(1, total.shape[0])]
            return
        half = sums[0].shape[0] // 2
        self.keep = [low(s[:half]) for s in sums]
        self.send = [low(s[half:]) for s in sums]


def hold(groups, values):
    waiting = [group for group in groups if group.sums is None]
    if not waiting:
        return values
    got, values = lax.optimization_barrier(([group.got for group in waiting], values))
    for group, x in zip(waiting, got):
        group.got = x
    return values


def together(groups):
    if groups:
        state = lax.optimization_barrier([(group.keep, group.send) for group in groups])
        for group, (keep, send) in zip(groups, state):
            group.keep, group.send = keep, send


def plan_self(seg, positions):
    rows, length = seg.shape
    starts = jnp.arange(0, length, BLOCK, dtype=jnp.int32)
    begin = starts[None, :] - positions[:, ::BLOCK]
    left = jnp.maximum(starts[None, :] + BLOCK - WINDOW - begin, 0)
    return jnp.zeros_like(begin), (left + WINDOW - 1) // WINDOW


def plan_cross(tseg, sseg):
    last = jnp.int32(1 << 20)
    tkey = jnp.where(tseg == 0, last, tseg)
    skey = jnp.where(sseg == 0, last, sseg)
    begin = jnp.sum(skey[:, None, :] < tkey[:, ::BLOCK, None], axis=2, dtype=jnp.int32)
    end = jnp.sum(skey[:, None, :] <= tkey[:, BLOCK - 1::BLOCK, None], axis=2, dtype=jnp.int32)
    first = (begin // 16) * 16
    return first, jnp.maximum((end - first + WINDOW - 1) // WINDOW - 1, 0)


def per_device(
    target, memory, out_grad, target_segments, source_segments, target_positions,
    self_qkv, self_out, cross_query, cross_kv, cross_out, ffn_in, ffn_out, *small,
):
    net = Net()
    rows, length = target_segments.shape
    fast = self_qkv.shape[0] % UNIT == 0 and net.bits >= 5
    self_plan = plan_self(target_segments, target_positions)
    cross_plan = plan_cross(target_segments, source_segments)
    tseg = wide(target_segments)[:, None, :]
    sseg = wide(source_segments)[:, None, :]
    w_qkv, vectors, rest, cross_weights = gather_weights(net, small, (self_qkv, self_out, cross_query, cross_kv, cross_out, ffn_in, ffn_out))
    if fast:
        index_a, index_b = net.index(0), net.index(1)
    else:
        index_a = index_b = jnp.arange(512 // UNIT, dtype=jnp.int32)

    (qkv, self_mix, self_lse), cross_w = cross_weights(tuple(self_forward(self_plan, target, w_qkv, vectors, tseg)))
    hid, cq, pairs, cross_mix, cross_lse = cross_forward(cross_plan, target, self_mix, memory, cross_w, vectors, tseg, sseg)
    output, h2, cross_mg, cross_delta, ffn_keep, ffn_send, dco, mid_small = middle(index_a, index_b, hid, cross_mix, out_grad, rest, vectors, length)

    groups = [Reduction(net, ffn_keep, ffn_send, 2048)] if fast else []

    def backward(causal, plan, q, k, v, delta, grad, lse, kseg):
        tied = tuple(x for group in groups for x in group.state())
        for group in groups:
            group.start()
        out = hold(groups, attend_back(causal, plan, q, k, v, delta, grad, lse, tseg, kseg, tied))
        for group in groups:
            group.add()
        return out

    cross_grads = backward(False, cross_plan, (cq, 0), (pairs, 0), (pairs, 1), cross_delta, cross_mg, cross_lse, sseg)
    for group in groups:
        group.start()
    h1, self_mg, self_delta, cross_keep, cross_send, small_sums = cross_dense(
        index_a, index_b, cross_grads, memory, hid, h2, self_mix, cross_w, dco, vectors, length)
    h1, self_mg, self_delta, cross_keep, cross_send, small_sums = hold(
        groups, (h1, self_mg, self_delta, cross_keep, cross_send, small_sums))
    for group in groups:
        group.add()
    if fast:
        groups.append(Reduction(net, cross_keep, cross_send, 1280))
    self_grads = backward(True, self_plan, (qkv, 0), (qkv, 1), (qkv, 2), self_delta, self_mg, self_lse, tseg)
    for group in groups:
        group.start()
    self_keep, self_send, lines = self_grad(net.count if fast else 0, index_a, index_b, self_grads, target, mid_small, small_sums)
    self_keep, self_send, lines = hold(groups, (self_keep, self_send, lines))
    for group in groups:
        group.add()

    if not fast:
        target_out = target_grad(h1, self_grads, w_qkv)
        memory_grad = memory_back(*cross_grads[1:], cross_w)
        total = lambda x: lax.psum_scatter(low(x), AXES, scatter_dimension=0, tiled=True).astype(F32) if net.count > 1 else wide(x)
        whole = lambda keep, send: jnp.concatenate([keep, send], axis=0).reshape(512, -1)
        d_self, d_cross, d_ffn = whole(self_keep, self_send), whole(cross_keep, cross_send), whole(ffn_keep, ffn_send)
        d_out = d_ffn[:, 2048:].reshape(-1, UNIT, 4, 512).transpose(0, 2, 1, 3).reshape(2048, 512)
        weights = (d_self[:, :1536], d_cross[:, 1024:1536],
                   d_cross[:, :512], d_cross[:, 1536:], d_cross[:, 512:1024], d_ffn[:, :2048], d_out)
        return (output, target_out, memory_grad, *[total(w) for w in weights], *[total(lines[j, :n]) for j, n in enumerate(VECTORS)])

    groups.append(Reduction(net, self_keep, self_send, 768))
    target_out = None
    while any(group.sums is None for group in groups):
        open_groups = [group for group in groups if group.sums is None]
        tied = tuple(x for group in open_groups for x in group.state())
        for group in open_groups:
            group.start()
        if groups[-1].stage == 1:
            target_out = target_grad(h1, self_grads, w_qkv, tied)
        if groups[-1].stage == 2:
            memory_grad = memory_back(*cross_grads[1:], cross_w, tied)
        for group in open_groups:
            group.add()
        together([group for group in open_groups if group.sums is None])
    d_ffn, d_cross, d_self = (group.sums for group in groups)
    vectors_out = [d_self[j, 1536:1536 + n // net.count] for j, n in enumerate(VECTORS)]
    return (
        output, target_out, memory_grad,
        d_self[:, :1536], d_cross[:, 1024:1536],
        d_cross[:, :512], d_cross[:, 1536:], d_cross[:, 512:1024],
        d_ffn[:, :2048], jnp.concatenate([d_ffn[:, 2048 + 512 * b:2560 + 512 * b] for b in range(4)], axis=0),
        *vectors_out,
    )


def solution(mesh):
    both = ("wide", "narrow")
    matrix, vector = P(both, None), P(both)
    return jax.shard_map(
        per_device, mesh=mesh,
        in_specs=(matrix,) * 13 + (vector,) * 10,
        out_specs=(matrix,) * 10 + (vector,) * 10,
        check_vma=False,
    )
```

```python
import functools

import jax
import jax.numpy as jnp
from jax import lax
from jax.experimental import pallas as pl
from jax.experimental.pallas import tpu as pltpu
from jax.sharding import PartitionSpec as P

MASKED = -1e30
EPSILON = 1e-05
BLOCK = 128
WINDOW = 256
UNIT = 16
AXES = ("wide", "narrow")
NT = (((1,), (1,)), ((), ()))
TN = (((0,), (0,)), ((), ()))
NN = (((1,), (0,)), ((), ()))
BF = jnp.bfloat16
F32 = jnp.float32


def mxu(a, b, dims=NN):
    return lax.dot_general(a, b, dims, preferred_element_type=F32)


def low(x):
    return x.astype(BF)


def wide(x):
    return x.astype(F32)


def shape_of(shape, dtype=BF):
    return jax.ShapeDtypeStruct(shape, dtype)


def smem():
    return pl.BlockSpec(memory_space=pltpu.SMEM)


def vmem():
    return pl.BlockSpec(memory_space=pltpu.VMEM)


def fixed(shape, *index):
    return pl.BlockSpec(shape, lambda i, index=index: index, pipeline_mode=pl.Buffered(1))


def tiled(rows, cols, col=0):
    return pl.BlockSpec((rows, cols), lambda i, col=col: (i, col))


def params(mib):
    return pltpu.CompilerParams(vmem_limit_bytes=mib << 20)


def cost(micros):
    return pl.CostEstimate(flops=int(micros * 1e9), bytes_accessed=1 << 20, transcendentals=0)


def lane_masks(scale):
    lane = lax.broadcasted_iota(jnp.int32, (1, 128), 1)
    return low(jnp.where(lane < 64, scale, 0.0)), low(jnp.where(lane < 64, 0.0, scale))


def stacked(pair, masks):
    return jnp.concatenate([pair * masks[0], pair * masks[1]], axis=0)


def pick(both):
    sub = lax.broadcasted_iota(jnp.int32, (128, BLOCK), 0)
    return jnp.where(sub < 64, both[:, :BLOCK], both[:, BLOCK:])


def columns_of(row):
    return jnp.transpose(jnp.broadcast_to(row, (128, row.shape[1])))


def prepare_masks(causal, qseg_ref, kseg_ref, qone, kout, still):
    lane = wide(lax.broadcasted_iota(jnp.int32, (1, 128), 1))
    qone[...] = low(jnp.where(columns_of(qseg_ref[0]) == lane, 1.0, 0.0))
    kout[...] = low(jnp.where(columns_of(kseg_ref[0]) == lane, 0.0, MASKED))
    if causal:
        key = lax.broadcasted_iota(jnp.int32, (WINDOW, BLOCK), 0)
        query = lax.broadcasted_iota(jnp.int32, (WINDOW, BLOCK), 1)
        still[0] = jnp.where(key <= query, 0.0, MASKED)
        still[1] = jnp.where(key <= query + BLOCK, 0.0, MASKED)
        still[2] = jnp.zeros((WINDOW, BLOCK), F32)
        still[3] = jnp.where(key < BLOCK, 0.0, MASKED)


MASK_SCRATCH = lambda length: [pltpu.VMEM((length, 128), BF), pltpu.VMEM((length, 128), BF), pltpu.VMEM((4, WINDOW, BLOCK), F32)]


def bias_of(causal, still, qb, c, start, bound):
    if causal:
        at = jnp.minimum(qb, 1) if c is None else jnp.where(bound < WINDOW, 3, 2)
        return still[at]
    if c is None:
        return None
    key = lax.broadcasted_iota(jnp.int32, (WINDOW, BLOCK), 0) + start
    return jnp.where(key >= bound, 0.0, MASKED)


def masked(scores, bias):
    return scores if bias is None else scores + jnp.concatenate([bias, bias], axis=1)


def window(causal, first_ref, r, qb, c, length):
    c = 0 if c is None else c
    if causal:
        end = (qb + 1) * BLOCK - c * WINDOW
        return pl.multiple_of(jnp.maximum(end - WINDOW, 0), BLOCK), end
    begin = first_ref[r, qb] + c * WINDOW
    return pl.multiple_of(jnp.minimum(begin, length - WINDOW), 16), begin


def lanes_at(offset, p):
    return slice(offset + 128 * p, offset + 128 * p + 128)


UNROLL = 4


def most(extra_ref, r, qbs):
    count = extra_ref[r, qbs[0]]
    for qb in qbs[1:]:
        count = jnp.maximum(count, extra_ref[r, qb])
    return count


def attend(causal, r, first_ref, extra_ref, q, k, v, out_ref, lse_ref, masking, top, total, mix):
    length = q[0].shape[0]
    masks = lane_masks(0.125)
    joint = 2 if causal else 1
    qone, kout, still = masking

    def windows(qbs, c):
        scores, values, biases = [], [], []
        for qb in qbs:
            q0 = pl.multiple_of(qb * BLOCK, BLOCK)
            start, bound = window(causal, first_ref, r, qb, c, length)
            bias = bias_of(causal, still, qb, c, start, bound)
            queries, keys = qone[pl.ds(q0, BLOCK), :], kout[pl.ds(start, WINDOW), :]
            queries = jnp.concatenate([queries, queries], axis=0)
            for p in range(4):
                qs = jnp.concatenate([stacked(q[0][pl.ds(q0, BLOCK), lanes_at(q[1], p)], masks), queries], axis=1)
                ks = jnp.concatenate([k[0][pl.ds(start, WINDOW), lanes_at(k[1], p)], keys], axis=1)
                scores.append(mxu(ks, qs, NT))
                values.append(v[0][pl.ds(start, WINDOW), lanes_at(v[1], p)])
                biases.append(bias)
        return [masked(x, bias) for x, bias in zip(scores, biases)], values

    def step(i, _):
        qbs = [i * UNROLL + u for u in range(UNROLL)]
        scores, values = windows(qbs, None)
        highs = [jnp.max(x, axis=0, keepdims=True) for x in scores]
        weights = [jnp.exp(x - high) for x, high in zip(scores, highs)]
        sums = [jnp.sum(x, axis=0, keepdims=True) for x in weights]
        mixed = [pick(mxu(val, low(x), TN)) for val, x in zip(values, weights)]
        for n in range(4 * UNROLL):
            top[n] = highs[n]
            total[n] = sums[n]
            mix[n] = mixed[n]
        for u in range(0, UNROLL, joint):
            def more(c, _, u=u):
                scores, values = windows(qbs[u:u + joint], c + 1)
                highs = [jnp.maximum(top[4 * u + p], jnp.max(x, axis=0, keepdims=True)) for p, x in enumerate(scores)]
                weights = [jnp.exp(x - high) for x, high in zip(scores, highs)]
                mixed = [pick(mxu(val, low(x), TN)) for val, x in zip(values, weights)]
                for p in range(4 * joint):
                    n = 4 * u + p
                    fade = jnp.exp(top[n] - highs[p])
                    top[n] = highs[p]
                    total[n] = total[n] * fade + jnp.sum(weights[p], axis=0, keepdims=True)
                    mix[n] = mix[n] * pick(jnp.broadcast_to(fade, (128, 2 * BLOCK))) + mixed[p]
                return 0

            lax.fori_loop(0, most(extra_ref, r, qbs[u:u + joint]), more, 0)
        for u, qb in enumerate(qbs):
            q0 = pl.multiple_of(qb * BLOCK, BLOCK)
            for p in range(4):
                sums = total[4 * u + p]
                inverse = pick(jnp.broadcast_to(1.0 / sums, (128, 2 * BLOCK)))
                out_ref[pl.ds(q0, BLOCK), lanes_at(0, p)] = low(jnp.transpose(mix[4 * u + p] * inverse))
                lse = top[4 * u + p] + jnp.log(sums)
                lse_ref[0, 2 * p:2 * p + 1, pl.ds(q0, BLOCK)] = lse[:, :BLOCK]
                lse_ref[0, 2 * p + 1:2 * p + 2, pl.ds(q0, BLOCK)] = lse[:, BLOCK:]
        return 0

    lax.fori_loop(0, length // BLOCK // UNROLL, step, 0)


ATTEND_SCRATCH = lambda length: MASK_SCRATCH(length) + [
    pltpu.VMEM((4 * UNROLL, 1, 2 * BLOCK), F32),
    pltpu.VMEM((4 * UNROLL, 1, 2 * BLOCK), F32), pltpu.VMEM((4 * UNROLL, 128, BLOCK), F32)]


def norm(hidden):
    average = jnp.mean(hidden, axis=-1, keepdims=True)
    centred = hidden - average
    inverse = lax.rsqrt(jnp.mean(centred * centred, axis=-1, keepdims=True) + EPSILON)
    return centred * inverse, inverse


def norm_back(grad, normed, inverse, gain):
    scaled = grad * gain
    return inverse * (scaled - jnp.mean(scaled, axis=-1, keepdims=True)
                      - normed * jnp.mean(scaled * normed, axis=-1, keepdims=True))


def head_sums(grad, mix):
    lane = lax.broadcasted_iota(jnp.int32, (16, 512), 1) // 64
    heads = low(jnp.where(lane == lax.broadcasted_iota(jnp.int32, (16, 512), 0), 1.0, 0.0))
    return mxu(heads, low(wide(grad) * wide(mix)), NT)[:8]


def rows_spec(t, length):
    per = length // t
    return pl.BlockSpec((1, 8, t), lambda i: (i // per, 0, i % per))


def accumulate(ref, where, value):
    ref[where] = jnp.where(pl.program_id(0) == 0, 0.0, ref[where]) + value


def sum_rows(x):
    return jnp.sum(wide(x), axis=0, keepdims=True)


S_BIAS, S_GAIN, S_SHIFT, C_BIAS, C_GAIN, C_SHIFT, I_BIAS, O_BIAS, F_GAIN, F_SHIFT = range(10)


def vec(ref, row, block=0, size=512):
    return ref[row:row + 1, block * size:(block + 1) * size]


def self_kernel(first_ref, extra_ref, x_ref, w_ref, vec_ref, seg_ref, qkv_ref, mix_ref, lse_ref, qone, kout, still, *state):
    r = pl.program_id(0)
    prepare_masks(True, seg_ref, seg_ref, qone, kout, still)
    x = x_ref[...]
    qkv_ref[:, :512] = low(mxu(x, w_ref[:, :512]) + vec(vec_ref, S_BIAS, 0))
    qkv_ref[:, 512:1024] = low(mxu(x, w_ref[:, 512:1024]))
    qkv_ref[:, 1024:] = low(mxu(x, w_ref[:, 1024:]) + vec(vec_ref, S_BIAS, 1))
    attend(True, r, first_ref, extra_ref, (qkv_ref, 0), (qkv_ref, 512), (qkv_ref, 1024), mix_ref, lse_ref,
           (qone, kout, still), *state)


def self_forward(plan, x, w, vectors, seg):
    rows, _, length = seg.shape
    return pl.pallas_call(
        self_kernel, grid=(rows,),
        in_specs=[smem(), smem(), tiled(length, 512), fixed((512, 1536), 0, 0), fixed((16, 2048), 0, 0),
                  pl.BlockSpec((1, 1, length), lambda i: (i, 0, 0))],
        out_specs=[tiled(length, 1536), tiled(length, 512), pl.BlockSpec((1, 8, length), lambda i: (i, 0, 0))],
        out_shape=[pltpu.HBM((rows * length, 1536), BF), pltpu.HBM((rows * length, 512), BF), shape_of((rows, 8, length), F32)],
        scratch_shapes=ATTEND_SCRATCH(length), compiler_params=params(40), cost_estimate=cost(20), name="self_forward",
    )(*plan, x, w, vectors, seg)


def cross_kernel(first_ref, extra_ref, x_ref, mix_ref, mem_ref, wo_ref, wq_ref, wkv_ref, vec_ref, qseg_ref, kseg_ref,
                 hid_ref, q_ref, kv_ref, out_ref, lse_ref, qone, kout, still, *state):
    r = pl.program_id(0)
    prepare_masks(False, qseg_ref, kseg_ref, qone, kout, still)
    hidden = wide(x_ref[...]) + mxu(mix_ref[...], wo_ref[...]) + vec(vec_ref, S_BIAS, 2)
    hid_ref[...] = low(hidden)
    first = low(norm(hidden)[0] * vec(vec_ref, S_GAIN) + vec(vec_ref, S_SHIFT))
    q_ref[...] = low(mxu(first, wq_ref[...]) + vec(vec_ref, C_BIAS, 0))
    mem = mem_ref[...]
    kv_ref[:, :512] = low(mxu(mem, wkv_ref[:, :512]))
    kv_ref[:, 512:] = low(mxu(mem, wkv_ref[:, 512:]) + vec(vec_ref, C_BIAS, 1))
    attend(False, r, first_ref, extra_ref, (q_ref, 0), (kv_ref, 0), (kv_ref, 512), out_ref, lse_ref,
           (qone, kout, still), *state)


def cross_forward(plan, x, mix, mem, weights, vectors, qseg, kseg):
    rows, _, length = qseg.shape
    seg = pl.BlockSpec((1, 1, length), lambda i: (i, 0, 0))
    total = rows * length
    return pl.pallas_call(
        cross_kernel, grid=(rows,),
        in_specs=[smem(), smem(), tiled(length, 512), tiled(length, 512), tiled(length, 512),
                  fixed((512, 512), 0, 0), fixed((512, 512), 0, 1), fixed((512, 1024), 0, 1), fixed((16, 2048), 0, 0), seg, seg],
        out_specs=[tiled(length, 512), tiled(length, 512), tiled(length, 1024), tiled(length, 512),
                   pl.BlockSpec((1, 8, length), lambda i: (i, 0, 0))],
        out_shape=[shape_of((total, 512)), shape_of((total, 512)), shape_of((total, 1024)), shape_of((total, 512)),
                   shape_of((rows, 8, length), F32)],
        scratch_shapes=ATTEND_SCRATCH(length), compiler_params=params(60), cost_estimate=cost(25), name="cross_forward",
    )(*plan, x, mix, mem, weights, weights, weights, vectors, qseg, kseg)


def pair_row(ref, p, q0):
    return jnp.concatenate([ref[0, 2 * p + h:2 * p + h + 1, pl.ds(q0, BLOCK)] for h in range(2)], axis=1)


def back_kernel(causal, first_ref, extra_ref, q_ref, k_ref, v_ref, delta_ref, grad_ref, lse_ref, qseg_ref, kseg_ref, *refs):
    dq_ref, dk_ref, dv_ref, qone, kout, still, dk, dv, dq = refs[-9:]
    r = pl.program_id(0)
    length = q_ref.shape[0]
    joint = 2 if causal else 1
    prepare_masks(causal, qseg_ref, kseg_ref, qone, kout, still)
    dk[...] = jnp.zeros_like(dk)
    dv[...] = jnp.zeros_like(dv)
    masks = lane_masks(0.125)
    ones = lane_masks(1.0)

    def windows(qbs, c):
        places, qs, gs, deltas, lses, keys, biases, scores = [], [], [], [], [], [], [], []
        for qb in qbs:
            q0 = pl.multiple_of(qb * BLOCK, BLOCK)
            start, bound = window(causal, first_ref, r, qb, c, length)
            bias = bias_of(causal, still, qb, c, start, bound)
            queries, outs = qone[pl.ds(q0, BLOCK), :], kout[pl.ds(start, WINDOW), :]
            queries = jnp.concatenate([queries, queries], axis=0)
            for p in range(4):
                lanes = lanes_at(0, p)
                grad = grad_ref[pl.ds(q0, BLOCK), lanes]
                deltas.append(pair_row(delta_ref, p, q0))
                lses.append(pair_row(lse_ref, p, q0))
                qs.append(stacked(q_ref[pl.ds(q0, BLOCK), lanes], masks))
                gs.append(stacked(grad, ones))
                keys.append(k_ref[pl.ds(start, WINDOW), lanes])
                places.append((pl.ds(start, WINDOW), lanes))
                biases.append(bias)
                scores.append(mxu(jnp.concatenate([keys[-1], outs], axis=1), jnp.concatenate([qs[-1], queries], axis=1), NT))
        dprobs = [mxu(v_ref[place], g, NT) for place, g in zip(places, gs)]
        probs = [jnp.exp(masked(x, bias) - lse) for x, bias, lse in zip(scores, biases, lses)]
        dscores = [low(x * (d - delta)) for x, d, delta in zip(probs, dprobs, deltas)]
        new_dv = [mxu(low(x), g) for x, g in zip(probs, gs)]
        new_dk = [mxu(d, x) for d, x in zip(dscores, qs)]
        parts = [pick(mxu(key, d, TN)) for key, d in zip(keys, dscores)]
        for place, more_dv, more_dk in zip(places, new_dv, new_dk):
            dv[place] += more_dv
            dk[place] += more_dk
        return parts

    def step(i, _):
        qbs = [i * UNROLL + u for u in range(UNROLL)]
        for n, part in enumerate(windows(qbs, None)):
            dq[n] = part
        for u in range(0, UNROLL, joint):
            def more(c, _, u=u):
                for p, part in enumerate(windows(qbs[u:u + joint], c + 1)):
                    dq[4 * u + p] += part
                return 0

            lax.fori_loop(0, most(extra_ref, r, qbs[u:u + joint]), more, 0)
        for u, qb in enumerate(qbs):
            q0 = pl.multiple_of(qb * BLOCK, BLOCK)
            for p in range(4):
                dq_ref[pl.ds(q0, BLOCK), lanes_at(0, p)] = low(jnp.transpose(dq[4 * u + p]) * 0.125)
        return 0

    lax.fori_loop(0, length // BLOCK // UNROLL, step, 0)
    dk_ref[...] = low(dk[...])
    dv_ref[...] = low(dv[...])


def attend_back(causal, plan, q, k, v, delta, grad, lse, qseg, kseg, after=()):
    rows, _, length = qseg.shape
    seg = pl.BlockSpec((1, 1, length), lambda i: (i, 0, 0))
    line = pl.BlockSpec((1, 8, length), lambda i: (i, 0, 0))
    return pl.pallas_call(
        functools.partial(back_kernel, causal), grid=(rows,),
        in_specs=[smem(), smem(), tiled(length, 512, q[1]), tiled(length, 512, k[1]), tiled(length, 512, v[1]), line,
                  tiled(length, 512), line, seg, seg] + [pl.BlockSpec(memory_space=pl.ANY)] * len(after),
        out_specs=[tiled(length, 512)] * 3, out_shape=[shape_of((rows * length, 512))] * 3,
        scratch_shapes=MASK_SCRATCH(length) + [pltpu.VMEM((length, 512), F32), pltpu.VMEM((length, 512), F32),
                                               pltpu.VMEM((4 * UNROLL, 128, BLOCK), F32)],
        compiler_params=params(40 if causal else 56), cost_estimate=cost(20), name="self_back" if causal else "cross_back",
    )(*plan, q[0], k[0], v[0], delta, grad, lse, qseg, kseg, *after)


def emit(outs, col, acc, index_ref, acc_col, width):
    half = outs[0].shape[0]
    for r in range(512 // UNIT):
        row = pl.multiple_of(index_ref[r] * UNIT, UNIT)
        outs[r // half][r % half, :, col:col + width] = low(acc[pl.ds(row, UNIT), acc_col:acc_col + width])


def halves(width):
    half = 512 // UNIT // 2
    return [fixed((half, UNIT, width), 0, 0, 0)] * 2, [shape_of((half, UNIT, width))] * 2


MID_TILE = 512
PARTS = 2
CHUNK = 1024


def mid_kernel(index_a, index_b, hid_ref, mix_ref, grad_ref, win_ref, gout_ref, wco_ref, vec_ref,
               out_ref, h2_ref, mg_ref, delta_ref, keep_ref, send_ref, co_ref, small_ref,
               wout, dwin, dwout, dwco, act, slope):
    step = pl.program_id(0)
    hidden_width = win_ref.shape[1]
    tokens = hid_ref.shape[0]

    @pl.when(step == 0)
    def _():
        for d in range(512 // UNIT):
            for b in range(4):
                wout[(4 * d + b) * UNIT:(4 * d + b + 1) * UNIT, :] = gout_ref[d * UNIT:(d + 1) * UNIT, 512 * b:512 * b + 512]
        small_ref[...] = jnp.zeros_like(small_ref)

    chunks = [slice(c, c + CHUNK) for c in range(0, hidden_width, CHUNK)]
    part = tokens // PARTS
    parts = [slice(i * part, i * part + part) for i in range(PARTS)]
    firsts = [norm(wide(hid_ref[t, :]))[0] * vec(vec_ref, S_GAIN) + vec(vec_ref, S_SHIFT) for t in parts]
    norms2 = [norm(first + mxu(mix_ref[t, :], wco_ref[...]) + vec(vec_ref, C_BIAS, 2)) for t, first in zip(parts, firsts)]
    seconds = [normed * vec(vec_ref, C_GAIN) + vec(vec_ref, C_SHIFT) for normed, _ in norms2]
    lows = [low(second) for second in seconds]
    norms3 = []
    for t, second, second_low in zip(parts, seconds, lows):
        hidden3 = second + vec(vec_ref, O_BIAS)
        for c in chunks:
            pre = mxu(second_low, win_ref[:, c]) + vec_ref[I_BIAS:I_BIAS + 1, c]
            sig = 0.5 + 0.5 * jnp.tanh(0.5 * pre)
            active = low(pre * sig)
            act[t, c] = active
            slope[t, c] = sig * (1.0 + pre * (1.0 - sig))
            hidden3 += mxu(active, wout[c, :])
        norms3.append(norm(hidden3))
    backs3 = []
    for t, (normed3, inverse3) in zip(parts, norms3):
        out_ref[t, :] = low(normed3 * vec(vec_ref, F_GAIN) + vec(vec_ref, F_SHIFT))
        grad = wide(grad_ref[t, :])
        backs3.append(norm_back(grad, normed3, inverse3, vec(vec_ref, F_GAIN)))
        small_ref[2:3, :512] += sum_rows(grad * normed3)
        small_ref[3:4, :512] += sum_rows(grad)
    b3s = [low(back3) for back3 in backs3]
    us = [[] for _ in chunks]
    grads2 = []
    for t, back3, b3 in zip(parts, backs3, b3s):
        grad2 = back3
        for n, c in enumerate(chunks):
            u = low(mxu(b3, wout[c, :], NT) * slope[t, c])
            us[n].append(u)
            grad2 += mxu(u, win_ref[:, c], NT)
        grads2.append(grad2)
    b2s = []
    for t, grad2, (normed2, inverse2) in zip(parts, grads2, norms2):
        h2 = norm_back(grad2, normed2, inverse2, vec(vec_ref, C_GAIN))
        b2 = low(h2)
        h2_ref[t, :] = b2
        b2s.append(b2)
        small_ref[4:5, :512] += sum_rows(grad2 * normed2)
        small_ref[5:6, :512] += sum_rows(grad2)
    second_low = jnp.concatenate(lows, axis=0)
    b3 = jnp.concatenate(b3s, axis=0)
    second_t = jnp.transpose(second_low)
    small_ref[1:2, :512] += sum_rows(b3)
    for n, c in enumerate(chunks):
        u = jnp.concatenate(us[n], axis=0)
        accumulate(dwin, (slice(None), c), mxu(second_t, u))
        accumulate(dwout, (c, slice(None)), mxu(act[:, c], b3, TN))
        small_ref[0:1, c] += sum_rows(u)
    b2 = jnp.concatenate(b2s, axis=0)
    small_ref[6:7, :512] += sum_rows(b2)
    accumulate(dwco, ..., mxu(jnp.transpose(mix_ref[...]), b2))
    mix_grad = low(mxu(b2, wco_ref[...], NT))
    mg_ref[...] = mix_grad
    delta_ref[0] = head_sums(mix_grad, mix_ref[...])

    @pl.when(step == pl.num_programs(0) - 1)
    def _():
        outs = keep_ref, send_ref
        emit(outs, 0, dwin, index_a, 0, hidden_width)
        half = keep_ref.shape[0]
        for r in range(512 // UNIT):
            for b in range(4):
                row = pl.multiple_of((index_b[r] * 4 + b) * UNIT, UNIT)
                outs[r // half][r % half, :, 2048 + 512 * b:2560 + 512 * b] = low(dwout[pl.ds(row, UNIT), :])
        co_ref[...] = dwco[...]


def middle(index_a, index_b, hid, mix, grad, rest, vectors, length):
    total = hid.shape[0]
    t = MID_TILE
    specs, shapes = halves(4096)
    return pl.pallas_call(
        mid_kernel, grid=(total // t,),
        in_specs=[smem(), smem(), tiled(t, 512), tiled(t, 512), tiled(t, 512),
                  fixed((512, 2048), 0, 0), fixed((512, 2048), 0, 1), fixed((512, 512), 0, 8), fixed((16, 2048), 0, 0)],
        out_specs=[tiled(t, 512)] * 3 + [rows_spec(t, length)] + specs + [fixed((512, 512), 0, 0), fixed((8, 2048), 0, 0)],
        out_shape=[shape_of((total, 512))] * 3 + [shape_of((total // length, 8, length), F32)] + shapes
        + [shape_of((512, 512), F32), shape_of((8, 2048), F32)],
        scratch_shapes=[pltpu.VMEM((2048, 512), BF), pltpu.VMEM((512, 2048), F32), pltpu.VMEM((2048, 512), F32),
                        pltpu.VMEM((512, 512), F32), pltpu.VMEM((t, 2048), BF), pltpu.VMEM((t, 2048), F32)],
        compiler_params=params(62), cost_estimate=cost(40), name="middle",
    )(index_a, index_b, hid, mix, grad, rest, rest, rest, vectors)


DENSE_TILE = 512
SELF_TILE = 1024


def cross_dense_kernel(index_a, index_b, cq_ref, ck_ref, cv_ref, mem_ref, hid_ref, h2_ref, mix_ref,
                       wq_ref, wo_ref, co_ref, vec_ref,
                       h1_ref, mg_ref, delta_ref, keep_ref, send_ref, small_ref, dq, dkv, do):
    step = pl.program_id(0)

    @pl.when(step == 0)
    def _():
        small_ref[...] = jnp.zeros_like(small_ref)

    cq, ck, cv = cq_ref[...], ck_ref[...], cv_ref[...]
    normed, inverse = norm(wide(hid_ref[...]))
    first = low(normed * vec(vec_ref, S_GAIN) + vec(vec_ref, S_SHIFT))
    grad1 = wide(h2_ref[...]) + mxu(cq, wq_ref[...], NT)
    h1 = norm_back(grad1, normed, inverse, vec(vec_ref, S_GAIN))
    b1 = low(h1)
    h1_ref[...] = b1
    mix_grad = low(mxu(b1, wo_ref[...], NT))
    mg_ref[...] = mix_grad
    delta_ref[0] = head_sums(mix_grad, mix_ref[...])
    accumulate(dq, ..., mxu(jnp.transpose(first), cq))
    mem_t = jnp.transpose(mem_ref[...])
    accumulate(dkv, (slice(None), slice(0, 512)), mxu(mem_t, ck))
    accumulate(dkv, (slice(None), slice(512, 1024)), mxu(mem_t, cv))
    accumulate(do, ..., mxu(jnp.transpose(mix_ref[...]), b1))
    small_ref[0:1, :] += sum_rows(cq)
    small_ref[1:2, :] += sum_rows(cv)
    small_ref[2:3, :] += sum_rows(grad1 * normed)
    small_ref[3:4, :] += sum_rows(grad1)
    small_ref[4:5, :] += sum_rows(b1)

    @pl.when(step == pl.num_programs(0) - 1)
    def _():
        outs = keep_ref, send_ref
        emit(outs, 0, dq, index_a, 0, 512)
        emit(outs, 512, co_ref, index_a, 0, 512)
        emit(outs, 1024, do, index_a, 0, 256)
        emit(outs, 1280, do, index_b, 256, 256)
        emit(outs, 1536, dkv, index_b, 0, 1024)


def cross_dense(index_a, index_b, grads, mem, hid, h2, mix, weights, dco, vectors, length):
    total = hid.shape[0]
    t = DENSE_TILE
    specs, shapes = halves(2560)
    return pl.pallas_call(
        cross_dense_kernel, grid=(total // t,),
        in_specs=[smem(), smem()] + [tiled(t, 512)] * 7
        + [fixed((512, 512), 0, 1), fixed((512, 512), 0, 0), fixed((512, 512), 0, 0), fixed((16, 2048), 0, 0)],
        out_specs=[tiled(t, 512)] * 2 + [rows_spec(t, length)] + specs + [fixed((8, 512), 0, 0)],
        out_shape=[shape_of((total, 512))] * 2 + [shape_of((total // length, 8, length), F32)] + shapes + [shape_of((8, 512), F32)],
        scratch_shapes=[pltpu.VMEM((512, 512), F32), pltpu.VMEM((512, 1024), F32), pltpu.VMEM((512, 512), F32)],
        compiler_params=params(40), cost_estimate=cost(12), name="cross_dense",
    )(index_a, index_b, *grads, mem, hid, h2, mix, weights, weights, dco, vectors)


def memory_kernel(ck_ref, cv_ref, w_ref, *refs):
    refs[-1][...] = low(mxu(ck_ref[...], w_ref[:, :512], NT) + mxu(cv_ref[...], w_ref[:, 512:], NT))


def memory_back(ck, cv, weights, after=()):
    total = ck.shape[0]
    t = 512
    return pl.pallas_call(
        memory_kernel, grid=(total // t,), in_specs=[tiled(t, 512)] * 2 + [fixed((512, 1024), 0, 1)]
        + [pl.BlockSpec(memory_space=pl.ANY)] * len(after),
        out_specs=tiled(t, 512), out_shape=shape_of((total, 512)), compiler_params=params(40), cost_estimate=cost(4), name="memory_grad",
    )(ck, cv, weights, *after)


VECTORS = (1536, 512, 512, 1536, 512, 512, 2048, 512, 512, 512)


def places(n, per, count, axis):
    shape = (1, n)
    at = wide(lax.broadcasted_iota(jnp.int32, shape, 1))
    owner = jnp.floor((at + 0.5) * (1.0 / per))
    return owner, at - owner * per


def one_hot(n, per):
    _, place = places(n, per, n // per, 1)
    return low(jnp.where(wide(lax.broadcasted_iota(jnp.int32, (128, n), 0)) == place, 1.0, 0.0))


def owned(n, per, count):
    owner, _ = places(n, per, count, 1)
    return wide(lax.broadcasted_iota(jnp.int32, (count, n), 0)) == owner


def self_grad_kernel(count, index_a, index_b, dq_ref, dk_ref, dv_ref, x_ref, mid_ref, small_ref, keep_ref, send_ref, lines_ref, dw, table):
    step = pl.program_id(0)

    @pl.when(step == 0)
    def _():
        lines_ref[...] = jnp.zeros_like(lines_ref)

    x_t = jnp.transpose(x_ref[...])
    accumulate(dw, (slice(None), slice(0, 512)), mxu(x_t, dq_ref[...]))
    accumulate(dw, (slice(None), slice(512, 1024)), mxu(x_t, dk_ref[...]))
    accumulate(dw, (slice(None), slice(1024, 1536)), mxu(x_t, dv_ref[...]))
    lines_ref[S_BIAS:S_BIAS + 1, :512] += sum_rows(dq_ref[...])
    lines_ref[S_BIAS:S_BIAS + 1, 512:1024] += sum_rows(dv_ref[...])

    @pl.when(step == pl.num_programs(0) - 1)
    def _():
        outs = keep_ref, send_ref
        emit(outs, 0, dw, index_a, 0, 768)
        emit(outs, 768, dw, index_b, 768, 768)
        for row, col, source, source_row in (
            (S_BIAS, 1024, small_ref, 4), (S_GAIN, 0, small_ref, 2), (S_SHIFT, 0, small_ref, 3),
            (C_BIAS, 0, small_ref, 0), (C_BIAS, 512, small_ref, 1), (C_BIAS, 1024, mid_ref, 6),
            (C_GAIN, 0, mid_ref, 4), (C_SHIFT, 0, mid_ref, 5),
            (O_BIAS, 0, mid_ref, 1), (F_GAIN, 0, mid_ref, 2), (F_SHIFT, 0, mid_ref, 3),
        ):
            lines_ref[row:row + 1, col:col + 512] = source[source_row:source_row + 1, :512]
        lines_ref[I_BIAS:I_BIAS + 1, :] = mid_ref[0:1, :]
        if count:
            table[...] = jnp.zeros_like(table)
            for n in (512, 1536, 2048):
                hot, mine = one_hot(n, n // count), owned(n, n // count, count)
                for j, size in enumerate(VECTORS):
                    if size == n:
                        line = jnp.broadcast_to(lines_ref[j:j + 1, :n], (count, n))
                        table[:, j, :] = mxu(low(jnp.where(mine, line, 0.0)), hot, NT)
            for r in range(count):
                outs[2 * r // count][r % (count // 2), :, 1536:] = low(table[index_b[r]])


def self_grad(count, index_a, index_b, grads, x, mid_small, small):
    total = x.shape[0]
    t = SELF_TILE
    specs, shapes = halves(1664)
    return pl.pallas_call(
        functools.partial(self_grad_kernel, count), grid=(total // t,),
        in_specs=[smem(), smem()] + [tiled(t, 512)] * 4 + [fixed((8, 2048), 0, 0), fixed((8, 512), 0, 0)],
        out_specs=specs + [fixed((16, 2048), 0, 0)],
        out_shape=shapes + [shape_of((16, 2048), F32)],
        scratch_shapes=[pltpu.VMEM((512, 1536), F32), pltpu.VMEM((max(count, 8), 16, 128), F32)],
        compiler_params=params(40), cost_estimate=cost(5), name="self_grad",
    )(index_a, index_b, *grads, x, mid_small, small)


def target_kernel(h1_ref, dq_ref, dk_ref, dv_ref, w_ref, *refs):
    out_ref = refs[-1]
    total = wide(h1_ref[...]) + mxu(dq_ref[...], w_ref[:, :512], NT)
    total += mxu(dk_ref[...], w_ref[:, 512:1024], NT)
    out_ref[...] = low(total + mxu(dv_ref[...], w_ref[:, 1024:], NT))


def target_grad(h1, grads, w, after=()):
    total = h1.shape[0]
    t = 512
    return pl.pallas_call(
        target_kernel, grid=(total // t,), in_specs=[tiled(t, 512)] * 4 + [fixed((512, 1536), 0, 0)]
        + [pl.BlockSpec(memory_space=pl.ANY)] * len(after),
        out_specs=tiled(t, 512), out_shape=shape_of((total, 512)), compiler_params=params(40), cost_estimate=cost(5), name="target_grad",
    )(h1, *grads, w, *after)


class Net:
    def __init__(self):
        self.wide = lax.axis_size("wide")
        self.narrow = lax.axis_size("narrow")
        self.count = self.wide * self.narrow
        self.wide_bits = self.wide.bit_length() - 1
        self.narrow_bits = self.narrow.bit_length() - 1
        self.bits = self.wide_bits + self.narrow_bits
        self.me = lax.axis_index("wide") * self.narrow + lax.axis_index("narrow")
        inner = list(range(self.narrow_bits))
        core, second = [self.narrow_bits], [self.narrow_bits + 1]
        far = list(range(self.narrow_bits + 2, self.bits))
        self.near = self.bits - len(far)
        self.orders = (core + second + inner + far, core + inner + second + far)

    def exchange(self, x, bit):
        if bit < self.narrow_bits:
            return lax.ppermute(x, "narrow", [(i, i ^ (1 << bit)) for i in range(self.narrow)])
        return self.across(x, 1 << bit)

    def across(self, x, mask):
        mask >>= self.narrow_bits
        return lax.ppermute(x, "wide", [(i, i ^ mask) for i in range(self.wide)])

    def far_masks(self, order):
        return [sum(((r >> s) & 1) << bit for s, bit in enumerate(order)) for r in range(1 << len(order))]

    def index(self, chain):
        order, n = self.orders[chain], self.bits
        mask = [sum(((r >> (n - 1 - s)) & 1) << bit for s, bit in enumerate(order)) for r in range(self.count)]
        return jnp.array(mask, jnp.int32) ^ self.me

    def gather_index(self, chain):
        order = self.orders[chain][::-1]
        mask = [sum(((r >> s) & 1) << bit for s, bit in enumerate(order)) for r in range(self.count)]
        return jnp.array(mask, jnp.int32) ^ self.me


def pack_kernel(*refs):
    vectors, (qkv, so, cq, ckv, co, fin, fout, packed_ref, cross_ref, rest_ref) = refs[:10], refs[10:20]
    lines, sem = refs[20:30], refs[30]
    moves = list(zip(vectors, lines))
    moves += [(qkv.at[:, :768], packed_ref.at[0, :, :768]), (qkv.at[:, 768:], packed_ref.at[0, :, 896:]), (fin, rest_ref.at[:, :2048])]
    moves += [(fout.at[UNIT * b:UNIT * b + UNIT, :], rest_ref.at[:, 2048 + 512 * b:2560 + 512 * b]) for b in range(4)]
    moves += [(co, rest_ref.at[:, 4096:]), (so, cross_ref.at[0, :, :512]),
              (cq, cross_ref.at[0, :, 512:1024]), (ckv, cross_ref.at[0, :, 1024:])]
    copies = [pltpu.make_async_copy(src, dst, sem.at[i]) for i, (src, dst) in enumerate(moves)]
    for copy in copies:
        copy.start()
    for copy in copies:
        copy.wait()
    rows = []
    for v in lines:
        line = wide(v[...])
        rows.append(jnp.concatenate([line, jnp.zeros((1, 128 - line.shape[1]), F32)], axis=1))
    rows.append(jnp.zeros((6, 128), F32))
    packed_ref[0, :, 768:896] = low(jnp.concatenate(rows, axis=0))


def unpack_kernel(count, index_a, index_b, *refs):
    n = (len(refs) - 3) // 2
    pieces_a, pieces_b, (w_ref, vec_ref, table) = refs[:n], refs[n:2 * n], refs[2 * n:]
    for pieces, index, col, width in ((pieces_a, index_a, 0, 768), (pieces_b, index_b, 768, 768)):
        r = 0
        for piece in pieces:
            for j in range(piece.shape[0]):
                owner = index[r]
                w_ref[pl.ds(pl.multiple_of(owner * UNIT, UNIT), UNIT), col:col + width] = piece[j, :, :width]
                if col == 0:
                    table[owner] = wide(piece[j, :, 768:896])
                r += 1
    vec_ref[...] = jnp.zeros_like(vec_ref)
    for n in (512, 1536, 2048):
        hot, mine = one_hot(n, n // count), owned(n, n // count, count)
        for j, size in enumerate(VECTORS):
            if size == n:
                spread = mxu(low(table[:, j, :]), hot)
                vec_ref[j:j + 1, :n] = jnp.sum(jnp.where(mine, spread, 0.0), axis=0, keepdims=True)


def place_kernel(index, *refs):
    pieces, w_ref = refs[:-1], refs[-1]
    r = 0
    for piece in pieces:
        for j in range(piece.shape[0]):
            row = pl.multiple_of(index[r] * UNIT, UNIT)
            w_ref[pl.ds(row, UNIT), :] = piece[j]
            r += 1


def gather_weights(net, small, big, early):
    qkv, so, cq, ckv, co, fin, fout = big
    if qkv.shape[0] % UNIT or net.bits < 5:
        small, big = lax.all_gather((small, big), AXES, axis=0, tiled=True) if net.count > 1 else (small, big)
        qkv, so, cq, ckv, co, fin, fout = big
        fout = fout.reshape(-1, 4, UNIT, 512).transpose(0, 2, 1, 3).reshape(512, 2048)
        rows = [jnp.pad(wide(v), (0, 2048 - v.shape[0])) for v in small]
        vectors = jnp.stack(rows + [jnp.zeros((2048,), F32)] * 6)
        return qkv, vectors, jnp.concatenate([fin, fout, co], axis=1), lambda x: (x, jnp.concatenate([so, cq, ckv], axis=1)), early
    packed, cross, rest = pl.pallas_call(
        pack_kernel, in_specs=[pl.BlockSpec(memory_space=pl.ANY)] * 17, out_specs=[vmem()] * 3,
        out_shape=[shape_of((1, UNIT, 1664)), shape_of((1, UNIT, 2048)), shape_of((UNIT, 4608))],
        scratch_shapes=[pltpu.VMEM((1, v.shape[0]), BF) for v in small] + [pltpu.SemaphoreType.DMA((21,))],
        compiler_params=params(60), cost_estimate=cost(2), name="pack",
    )(*[v[None] for v in small], *big)
    rest = lax.all_gather(rest, AXES, axis=0, tiled=True)
    orders = [order[::-1] for order in net.orders]
    far = net.bits - net.near
    masks = net.far_masks(orders[0][:far])[1:]
    everywhere = lambda x: jnp.concatenate([x] + [net.across(x, mask) for mask in masks], axis=0)
    packed = everywhere(packed)
    packed, cross, early = lax.optimization_barrier((packed, cross, early))
    cross = everywhere(cross)
    parts = [packed[:, :, :896], packed[:, :, 896:], cross]
    orders = orders + orders[:1]
    parts = [jnp.concatenate([x, net.exchange(x, order[far])], axis=0) for x, order in zip(parts, orders)]

    def spread(pieces, s):
        got = [[net.exchange(x, order[s]) for x in chain] for chain, order in zip(pieces, orders)]
        return [chain + more for chain, more in zip(pieces, got)]

    pieces = spread(spread([[x] for x in parts[:2]], far + 1), far + 2)
    later = spread([[x] for x in parts[2:]], far + 1)
    gather_index = [net.gather_index(0), net.gather_index(1)]

    def cross_weights(values):
        held, values = lax.optimization_barrier((later, values))
        held = spread(held, far + 2)
        return values, pl.pallas_call(
            place_kernel, in_specs=[smem()] + [vmem()] * len(held[0]), out_specs=vmem(),
            out_shape=pltpu.HBM((512, 2048), BF), compiler_params=params(32), cost_estimate=cost(2), name="place",
        )(gather_index[0], *held[0])

    w, vectors = pl.pallas_call(
        functools.partial(unpack_kernel, net.count), in_specs=[smem(), smem()] + [vmem()] * (len(pieces[0]) * 2), out_specs=[vmem()] * 2,
        out_shape=[shape_of((512, 1536)), shape_of((16, 2048), F32)],
        scratch_shapes=[pltpu.VMEM((net.count, 16, 128), F32)],
        compiler_params=params(40), cost_estimate=cost(2), name="unpack",
    )(*gather_index, *pieces[0], *pieces[1])
    return w, vectors, rest, cross_weights, early


class Reduction:
    def __init__(self, net, keep, send, cut):
        self.net, self.cut = net, cut
        self.keep, self.send = [keep], [send]
        self.stage = 0
        self.sums = None

    def state(self):
        return tuple(self.send) if self.sums is None else ()

    def start(self):
        if self.sums is not None:
            return
        if self.stage < self.net.near:
            self.got = [self.net.exchange(x, order[self.stage]) for x, order in zip(self.send, self.net.orders)]
        else:
            far = self.net.far_masks(self.net.orders[0][:self.net.near - 1:-1])
            self.got = [self.net.across(x, mask) for x, mask in zip(self.send, far[1:])]

    def add(self):
        if self.sums is not None:
            return
        self.stage += 1
        if self.stage > self.net.near:
            self.sums = sum((wide(got[0]) for got in self.got), self.keep[0][0])
            return
        sums = [wide(k) + wide(g) for k, g in zip(self.keep, self.got)]
        if self.stage == 1:
            sums = [sums[0][:, :, :self.cut], sums[0][:, :, self.cut:]]
        elif self.stage == self.net.near:
            total = jnp.concatenate(sums, axis=2)
            self.keep = [total[:1]]
            self.send = [low(total[r:r + 1]) for r in range(1, total.shape[0])]
            return
        half = sums[0].shape[0] // 2
        self.keep = [low(s[:half]) for s in sums]
        self.send = [low(s[half:]) for s in sums]


def hold(groups, values):
    waiting = [group for group in groups if group.sums is None]
    if not waiting:
        return values
    got, values = lax.optimization_barrier(([group.got for group in waiting], values))
    for group, x in zip(waiting, got):
        group.got = x
    return values


def behind(groups, leader):
    for group in groups:
        (group.keep, group.send), _ = lax.optimization_barrier(((group.keep, group.send), leader.send))


def plan_self(seg, positions):
    rows, length = seg.shape
    starts = jnp.arange(0, length, BLOCK, dtype=jnp.int32)
    begin = starts[None, :] - positions[:, ::BLOCK]
    left = jnp.maximum(starts[None, :] + BLOCK - WINDOW - begin, 0)
    return jnp.zeros_like(begin), (left + WINDOW - 1) // WINDOW


def plan_cross(tseg, sseg):
    last = jnp.int32(1 << 20)
    tkey = jnp.where(tseg == 0, last, tseg)
    skey = jnp.where(sseg == 0, last, sseg)
    begin = jnp.sum(skey[:, None, :] < tkey[:, ::BLOCK, None], axis=2, dtype=jnp.int32)
    end = jnp.sum(skey[:, None, :] <= tkey[:, BLOCK - 1::BLOCK, None], axis=2, dtype=jnp.int32)
    first = (begin // 16) * 16
    return first, jnp.maximum((end - first + WINDOW - 1) // WINDOW - 1, 0)


def per_device(
    target, memory, out_grad, target_segments, source_segments, target_positions,
    self_qkv, self_out, cross_query, cross_kv, cross_out, ffn_in, ffn_out, *small,
):
    net = Net()
    rows, length = target_segments.shape
    fast = self_qkv.shape[0] % UNIT == 0 and net.bits >= 5
    self_plan = plan_self(target_segments, target_positions)
    cross_plan = plan_cross(target_segments, source_segments)
    tseg = wide(target_segments)[:, None, :]
    sseg = wide(source_segments)[:, None, :]
    index = (net.index(0), net.index(1)) if fast else (jnp.arange(512 // UNIT, dtype=jnp.int32),) * 2
    w_qkv, vectors, rest, cross_weights, early = gather_weights(
        net, small, (self_qkv, self_out, cross_query, cross_kv, cross_out, ffn_in, ffn_out), (self_plan, cross_plan, tseg, sseg, index))
    self_plan, cross_plan, tseg, sseg, (index_a, index_b) = early
    (qkv, self_mix, self_lse), cross_w = cross_weights(tuple(self_forward(self_plan, target, w_qkv, vectors, tseg)))
    hid, cq, pairs, cross_mix, cross_lse = cross_forward(cross_plan, target, self_mix, memory, cross_w, vectors, tseg, sseg)
    output, h2, cross_mg, cross_delta, ffn_keep, ffn_send, dco, mid_small = middle(index_a, index_b, hid, cross_mix, out_grad, rest, vectors, length)

    groups = [Reduction(net, ffn_keep, ffn_send, 2048)] if fast else []

    def backward(causal, plan, q, k, v, delta, grad, lse, kseg):
        tied = tuple(x for group in groups for x in group.state())
        for group in groups:
            group.start()
        out = hold(groups, attend_back(causal, plan, q, k, v, delta, grad, lse, tseg, kseg, tied))
        for group in groups:
            group.add()
        return out

    cross_grads = backward(False, cross_plan, (cq, 0), (pairs, 0), (pairs, 1), cross_delta, cross_mg, cross_lse, sseg)
    for group in groups:
        group.start()
    h1, self_mg, self_delta, cross_keep, cross_send, small_sums = cross_dense(
        index_a, index_b, cross_grads, memory, hid, h2, self_mix, cross_w, dco, vectors, length)
    h1, self_mg, self_delta, cross_keep, cross_send, small_sums = hold(
        groups, (h1, self_mg, self_delta, cross_keep, cross_send, small_sums))
    for group in groups:
        group.add()
    if fast:
        groups.append(Reduction(net, cross_keep, cross_send, 1280))
    self_grads = backward(True, self_plan, (qkv, 0), (qkv, 1), (qkv, 2), self_delta, self_mg, self_lse, tseg)
    for group in groups:
        group.start()
    self_keep, self_send, lines = self_grad(net.count if fast else 0, index_a, index_b, self_grads, target, mid_small, small_sums)
    self_keep, self_send, lines = hold(groups, (self_keep, self_send, lines))
    for group in groups:
        group.add()

    if not fast:
        target_out = target_grad(h1, self_grads, w_qkv)
        memory_grad = memory_back(*cross_grads[1:], cross_w)
        total = lambda x: lax.psum_scatter(low(x), AXES, scatter_dimension=0, tiled=True).astype(F32) if net.count > 1 else wide(x)
        whole = lambda keep, send: jnp.concatenate([keep, send], axis=0).reshape(512, -1)
        d_self, d_cross, d_ffn = whole(self_keep, self_send), whole(cross_keep, cross_send), whole(ffn_keep, ffn_send)
        d_out = d_ffn[:, 2048:].reshape(-1, UNIT, 4, 512).transpose(0, 2, 1, 3).reshape(2048, 512)
        weights = (d_self[:, :1536], d_cross[:, 1024:1536],
                   d_cross[:, :512], d_cross[:, 1536:], d_cross[:, 512:1024], d_ffn[:, :2048], d_out)
        return (output, target_out, memory_grad, *[total(w) for w in weights], *[total(lines[j, :n]) for j, n in enumerate(VECTORS)])

    groups.append(Reduction(net, self_keep, self_send, 768))
    target_out = None
    while any(group.sums is None for group in groups):
        open_groups = [group for group in groups if group.sums is None]
        tied = tuple(x for group in open_groups for x in group.state())
        for group in open_groups:
            group.start()
        if groups[-1].stage == 1:
            target_out = target_grad(h1, self_grads, w_qkv, tied)
        if groups[-1].stage == 2:
            memory_grad = memory_back(*cross_grads[1:], cross_w, tied)
        for group in open_groups:
            group.add()
        behind([group for group in open_groups[:-1] if group.sums is None], open_groups[-1])
    d_ffn, d_cross, d_self = (group.sums for group in groups)
    vectors_out = [d_self[j, 1536:1536 + n // net.count] for j, n in enumerate(VECTORS)]
    return (
        output, target_out, memory_grad,
        d_self[:, :1536], d_cross[:, 1024:1536],
        d_cross[:, :512], d_cross[:, 1536:], d_cross[:, 512:1024],
        d_ffn[:, :2048], jnp.concatenate([d_ffn[:, 2048 + 512 * b:2560 + 512 * b] for b in range(4)], axis=0),
        *vectors_out,
    )


def solution(mesh):
    both = ("wide", "narrow")
    matrix, vector = P(both, None), P(both)
    return jax.shard_map(
        per_device, mesh=mesh,
        in_specs=(matrix,) * 13 + (vector,) * 10,
        out_specs=(matrix,) * 10 + (vector,) * 10,
        check_vma=False,
    )
```

```python
import functools

import jax
import jax.numpy as jnp
from jax import lax
from jax.experimental import pallas as pl
from jax.experimental.pallas import tpu as pltpu
from jax.sharding import PartitionSpec as P

MASKED = -1e30
EPSILON = 1e-05
BLOCK = 128
WINDOW = 256
UNIT = 16
AXES = ("wide", "narrow")
NT = (((1,), (1,)), ((), ()))
TN = (((0,), (0,)), ((), ()))
NN = (((1,), (0,)), ((), ()))
BF = jnp.bfloat16
F32 = jnp.float32


def mxu(a, b, dims=NN):
    return lax.dot_general(a, b, dims, preferred_element_type=F32)


def low(x):
    return x.astype(BF)


def wide(x):
    return x.astype(F32)


def shape_of(shape, dtype=BF):
    return jax.ShapeDtypeStruct(shape, dtype)


def smem():
    return pl.BlockSpec(memory_space=pltpu.SMEM)


def vmem():
    return pl.BlockSpec(memory_space=pltpu.VMEM)


def fixed(shape, *index):
    return pl.BlockSpec(shape, lambda i, index=index: index, pipeline_mode=pl.Buffered(1))


def tiled(rows, cols, col=0):
    return pl.BlockSpec((rows, cols), lambda i, col=col: (i, col))


def params(mib):
    return pltpu.CompilerParams(vmem_limit_bytes=mib << 20)


def cost(micros):
    return pl.CostEstimate(flops=int(micros * 1e9), bytes_accessed=1 << 20, transcendentals=0)


def lane_masks(scale):
    lane = lax.broadcasted_iota(jnp.int32, (1, 128), 1)
    return low(jnp.where(lane < 64, scale, 0.0)), low(jnp.where(lane < 64, 0.0, scale))


def stacked(pair, masks):
    return jnp.concatenate([pair * masks[0], pair * masks[1]], axis=0)


def pick(both):
    sub = lax.broadcasted_iota(jnp.int32, (128, BLOCK), 0)
    return jnp.where(sub < 64, both[:, :BLOCK], both[:, BLOCK:])


def columns_of(row):
    return jnp.transpose(jnp.broadcast_to(row, (128, row.shape[1])))


def prepare_masks(causal, qseg_ref, kseg_ref, qone, kout, still):
    lane = wide(lax.broadcasted_iota(jnp.int32, (1, 128), 1))
    qone[...] = low(jnp.where(columns_of(qseg_ref[0]) == lane, 1.0, 0.0))
    kout[...] = low(jnp.where(columns_of(kseg_ref[0]) == lane, 0.0, MASKED))
    if causal:
        key = lax.broadcasted_iota(jnp.int32, (WINDOW, BLOCK), 0)
        query = lax.broadcasted_iota(jnp.int32, (WINDOW, BLOCK), 1)
        still[0] = jnp.where(key <= query, 0.0, MASKED)
        still[1] = jnp.where(key <= query + BLOCK, 0.0, MASKED)
        still[2] = jnp.zeros((WINDOW, BLOCK), F32)
        still[3] = jnp.where(key < BLOCK, 0.0, MASKED)


MASK_SCRATCH = lambda length: [pltpu.VMEM((length, 128), BF), pltpu.VMEM((length, 128), BF), pltpu.VMEM((4, WINDOW, BLOCK), F32)]


def bias_of(causal, still, qb, c, start, bound):
    if causal:
        at = jnp.minimum(qb, 1) if c is None else jnp.where(bound < WINDOW, 3, 2)
        return still[at]
    if c is None:
        return None
    key = lax.broadcasted_iota(jnp.int32, (WINDOW, BLOCK), 0) + start
    return jnp.where(key >= bound, 0.0, MASKED)


def masked(scores, bias):
    return scores if bias is None else scores + jnp.concatenate([bias, bias], axis=1)


def window(causal, first_ref, r, qb, c, length):
    c = 0 if c is None else c
    if causal:
        end = (qb + 1) * BLOCK - c * WINDOW
        return pl.multiple_of(jnp.maximum(end - WINDOW, 0), BLOCK), end
    begin = first_ref[r, qb] + c * WINDOW
    return pl.multiple_of(jnp.minimum(begin, length - WINDOW), 16), begin


def lanes_at(offset, p):
    return slice(offset + 128 * p, offset + 128 * p + 128)


UNROLL = 4


def most(extra_ref, r, qbs):
    count = extra_ref[r, qbs[0]]
    for qb in qbs[1:]:
        count = jnp.maximum(count, extra_ref[r, qb])
    return count


def attend(causal, r, first_ref, extra_ref, q, k, v, out_ref, lse_ref, masking, top, total, mix):
    length = q[0].shape[0]
    masks = lane_masks(0.125)
    joint = 2 if causal else 1
    qone, kout, still = masking

    def windows(qbs, c):
        scores, values, biases = [], [], []
        for qb in qbs:
            q0 = pl.multiple_of(qb * BLOCK, BLOCK)
            start, bound = window(causal, first_ref, r, qb, c, length)
            bias = bias_of(causal, still, qb, c, start, bound)
            queries, keys = qone[pl.ds(q0, BLOCK), :], kout[pl.ds(start, WINDOW), :]
            queries = jnp.concatenate([queries, queries], axis=0)
            for p in range(4):
                qs = jnp.concatenate([stacked(q[0][pl.ds(q0, BLOCK), lanes_at(q[1], p)], masks), queries], axis=1)
                ks = jnp.concatenate([k[0][pl.ds(start, WINDOW), lanes_at(k[1], p)], keys], axis=1)
                scores.append(mxu(ks, qs, NT))
                values.append(v[0][pl.ds(start, WINDOW), lanes_at(v[1], p)])
                biases.append(bias)
        return [masked(x, bias) for x, bias in zip(scores, biases)], values

    def step(i, _):
        qbs = [i * UNROLL + u for u in range(UNROLL)]
        scores, values = windows(qbs, None)
        highs = [jnp.max(x, axis=0, keepdims=True) for x in scores]
        weights = [jnp.exp(x - high) for x, high in zip(scores, highs)]
        sums = [jnp.sum(x, axis=0, keepdims=True) for x in weights]
        mixed = [pick(mxu(val, low(x), TN)) for val, x in zip(values, weights)]
        for n in range(4 * UNROLL):
            top[n] = highs[n]
            total[n] = sums[n]
            mix[n] = mixed[n]
        for u in range(0, UNROLL, joint):
            def more(c, _, u=u):
                scores, values = windows(qbs[u:u + joint], c + 1)
                highs = [jnp.maximum(top[4 * u + p], jnp.max(x, axis=0, keepdims=True)) for p, x in enumerate(scores)]
                weights = [jnp.exp(x - high) for x, high in zip(scores, highs)]
                mixed = [pick(mxu(val, low(x), TN)) for val, x in zip(values, weights)]
                for p in range(4 * joint):
                    n = 4 * u + p
                    fade = jnp.exp(top[n] - highs[p])
                    top[n] = highs[p]
                    total[n] = total[n] * fade + jnp.sum(weights[p], axis=0, keepdims=True)
                    mix[n] = mix[n] * pick(jnp.broadcast_to(fade, (128, 2 * BLOCK))) + mixed[p]
                return 0

            lax.fori_loop(0, most(extra_ref, r, qbs[u:u + joint]), more, 0)
        for u, qb in enumerate(qbs):
            q0 = pl.multiple_of(qb * BLOCK, BLOCK)
            for p in range(4):
                sums = total[4 * u + p]
                inverse = pick(jnp.broadcast_to(1.0 / sums, (128, 2 * BLOCK)))
                out_ref[pl.ds(q0, BLOCK), lanes_at(0, p)] = low(jnp.transpose(mix[4 * u + p] * inverse))
                lse = top[4 * u + p] + jnp.log(sums)
                lse_ref[0, 2 * p:2 * p + 1, pl.ds(q0, BLOCK)] = lse[:, :BLOCK]
                lse_ref[0, 2 * p + 1:2 * p + 2, pl.ds(q0, BLOCK)] = lse[:, BLOCK:]
        return 0

    lax.fori_loop(0, length // BLOCK // UNROLL, step, 0)


ATTEND_SCRATCH = lambda length: MASK_SCRATCH(length) + [
    pltpu.VMEM((4 * UNROLL, 1, 2 * BLOCK), F32),
    pltpu.VMEM((4 * UNROLL, 1, 2 * BLOCK), F32), pltpu.VMEM((4 * UNROLL, 128, BLOCK), F32)]


def norm(hidden):
    average = jnp.mean(hidden, axis=-1, keepdims=True)
    centred = hidden - average
    inverse = lax.rsqrt(jnp.mean(centred * centred, axis=-1, keepdims=True) + EPSILON)
    return centred * inverse, inverse


def norm_back(grad, normed, inverse, gain):
    scaled = grad * gain
    return inverse * (scaled - jnp.mean(scaled, axis=-1, keepdims=True)
                      - normed * jnp.mean(scaled * normed, axis=-1, keepdims=True))


def head_sums(grad, mix):
    lane = lax.broadcasted_iota(jnp.int32, (16, 512), 1) // 64
    heads = low(jnp.where(lane == lax.broadcasted_iota(jnp.int32, (16, 512), 0), 1.0, 0.0))
    return mxu(heads, low(wide(grad) * wide(mix)), NT)[:8]


def rows_spec(t, length):
    per = length // t
    return pl.BlockSpec((1, 8, t), lambda i: (i // per, 0, i % per))


def accumulate(ref, where, value):
    ref[where] = jnp.where(pl.program_id(0) == 0, 0.0, ref[where]) + value


def sum_rows(x):
    return jnp.sum(wide(x), axis=0, keepdims=True)


S_BIAS, S_GAIN, S_SHIFT, C_BIAS, C_GAIN, C_SHIFT, I_BIAS, O_BIAS, F_GAIN, F_SHIFT = range(10)


def vec(ref, row, block=0, size=512):
    return ref[row:row + 1, block * size:(block + 1) * size]


def self_kernel(first_ref, extra_ref, x_ref, w_ref, vec_ref, seg_ref, qkv_ref, mix_ref, lse_ref, qone, kout, still, *state):
    r = pl.program_id(0)
    prepare_masks(True, seg_ref, seg_ref, qone, kout, still)
    x = x_ref[...]
    qkv_ref[:, :512] = low(mxu(x, w_ref[:, :512]) + vec(vec_ref, S_BIAS, 0))
    qkv_ref[:, 512:1024] = low(mxu(x, w_ref[:, 512:1024]))
    qkv_ref[:, 1024:] = low(mxu(x, w_ref[:, 1024:]) + vec(vec_ref, S_BIAS, 1))
    attend(True, r, first_ref, extra_ref, (qkv_ref, 0), (qkv_ref, 512), (qkv_ref, 1024), mix_ref, lse_ref,
           (qone, kout, still), *state)


def self_forward(plan, x, w, vectors, seg):
    rows, _, length = seg.shape
    return pl.pallas_call(
        self_kernel, grid=(rows,),
        in_specs=[smem(), smem(), tiled(length, 512), fixed((512, 1536), 0, 0), fixed((16, 2048), 0, 0),
                  pl.BlockSpec((1, 1, length), lambda i: (i, 0, 0))],
        out_specs=[tiled(length, 1536), tiled(length, 512), pl.BlockSpec((1, 8, length), lambda i: (i, 0, 0))],
        out_shape=[pltpu.HBM((rows * length, 1536), BF), pltpu.HBM((rows * length, 512), BF), shape_of((rows, 8, length), F32)],
        scratch_shapes=ATTEND_SCRATCH(length), compiler_params=params(40), cost_estimate=cost(20), name="self_forward",
    )(*plan, x, w, vectors, seg)


def cross_kernel(first_ref, extra_ref, x_ref, mix_ref, mem_ref, wo_ref, wq_ref, wkv_ref, vec_ref, qseg_ref, kseg_ref,
                 hid_ref, q_ref, kv_ref, out_ref, lse_ref, qone, kout, still, *state):
    r = pl.program_id(0)
    prepare_masks(False, qseg_ref, kseg_ref, qone, kout, still)
    hidden = wide(x_ref[...]) + mxu(mix_ref[...], wo_ref[...]) + vec(vec_ref, S_BIAS, 2)
    hid_ref[...] = low(hidden)
    first = low(norm(hidden)[0] * vec(vec_ref, S_GAIN) + vec(vec_ref, S_SHIFT))
    q_ref[...] = low(mxu(first, wq_ref[...]) + vec(vec_ref, C_BIAS, 0))
    mem = mem_ref[...]
    kv_ref[:, :512] = low(mxu(mem, wkv_ref[:, :512]))
    kv_ref[:, 512:] = low(mxu(mem, wkv_ref[:, 512:]) + vec(vec_ref, C_BIAS, 1))
    attend(False, r, first_ref, extra_ref, (q_ref, 0), (kv_ref, 0), (kv_ref, 512), out_ref, lse_ref,
           (qone, kout, still), *state)


def cross_forward(plan, x, mix, mem, weights, vectors, qseg, kseg):
    rows, _, length = qseg.shape
    seg = pl.BlockSpec((1, 1, length), lambda i: (i, 0, 0))
    total = rows * length
    return pl.pallas_call(
        cross_kernel, grid=(rows,),
        in_specs=[smem(), smem(), tiled(length, 512), tiled(length, 512), tiled(length, 512),
                  fixed((512, 512), 0, 0), fixed((512, 512), 0, 1), fixed((512, 1024), 0, 1), fixed((16, 2048), 0, 0), seg, seg],
        out_specs=[tiled(length, 512), tiled(length, 512), tiled(length, 1024), tiled(length, 512),
                   pl.BlockSpec((1, 8, length), lambda i: (i, 0, 0))],
        out_shape=[shape_of((total, 512)), shape_of((total, 512)), shape_of((total, 1024)), shape_of((total, 512)),
                   shape_of((rows, 8, length), F32)],
        scratch_shapes=ATTEND_SCRATCH(length), compiler_params=params(60), cost_estimate=cost(25), name="cross_forward",
    )(*plan, x, mix, mem, weights, weights, weights, vectors, qseg, kseg)


def pair_row(ref, p, q0):
    return jnp.concatenate([ref[0, 2 * p + h:2 * p + h + 1, pl.ds(q0, BLOCK)] for h in range(2)], axis=1)


def back_kernel(causal, first_ref, extra_ref, q_ref, k_ref, v_ref, delta_ref, grad_ref, lse_ref, qseg_ref, kseg_ref, *refs):
    dq_ref, dk_ref, dv_ref, qone, kout, still, dk, dv, dq = refs[-9:]
    r = pl.program_id(0)
    length = q_ref.shape[0]
    joint = 2 if causal else 1
    prepare_masks(causal, qseg_ref, kseg_ref, qone, kout, still)
    dk[...] = jnp.zeros_like(dk)
    dv[...] = jnp.zeros_like(dv)
    masks = lane_masks(0.125)
    ones = lane_masks(1.0)

    def windows(qbs, c):
        places, qs, gs, deltas, lses, keys, biases, scores = [], [], [], [], [], [], [], []
        for qb in qbs:
            q0 = pl.multiple_of(qb * BLOCK, BLOCK)
            start, bound = window(causal, first_ref, r, qb, c, length)
            bias = bias_of(causal, still, qb, c, start, bound)
            queries, outs = qone[pl.ds(q0, BLOCK), :], kout[pl.ds(start, WINDOW), :]
            queries = jnp.concatenate([queries, queries], axis=0)
            for p in range(4):
                lanes = lanes_at(0, p)
                grad = grad_ref[pl.ds(q0, BLOCK), lanes]
                deltas.append(pair_row(delta_ref, p, q0))
                lses.append(pair_row(lse_ref, p, q0))
                qs.append(stacked(q_ref[pl.ds(q0, BLOCK), lanes], masks))
                gs.append(stacked(grad, ones))
                keys.append(k_ref[pl.ds(start, WINDOW), lanes])
                places.append((pl.ds(start, WINDOW), lanes))
                biases.append(bias)
                scores.append(mxu(jnp.concatenate([keys[-1], outs], axis=1), jnp.concatenate([qs[-1], queries], axis=1), NT))
        dprobs = [mxu(v_ref[place], g, NT) for place, g in zip(places, gs)]
        probs = [jnp.exp(masked(x, bias) - lse) for x, bias, lse in zip(scores, biases, lses)]
        dscores = [low(x * (d - delta)) for x, d, delta in zip(probs, dprobs, deltas)]
        new_dv = [mxu(low(x), g) for x, g in zip(probs, gs)]
        new_dk = [mxu(d, x) for d, x in zip(dscores, qs)]
        parts = [pick(mxu(key, d, TN)) for key, d in zip(keys, dscores)]
        for place, more_dv, more_dk in zip(places, new_dv, new_dk):
            dv[place] += more_dv
            dk[place] += more_dk
        return parts

    def step(i, _):
        qbs = [i * UNROLL + u for u in range(UNROLL)]
        for n, part in enumerate(windows(qbs, None)):
            dq[n] = part
        for u in range(0, UNROLL, joint):
            def more(c, _, u=u):
                for p, part in enumerate(windows(qbs[u:u + joint], c + 1)):
                    dq[4 * u + p] += part
                return 0

            lax.fori_loop(0, most(extra_ref, r, qbs[u:u + joint]), more, 0)
        for u, qb in enumerate(qbs):
            q0 = pl.multiple_of(qb * BLOCK, BLOCK)
            for p in range(4):
                dq_ref[pl.ds(q0, BLOCK), lanes_at(0, p)] = low(jnp.transpose(dq[4 * u + p]) * 0.125)
        return 0

    lax.fori_loop(0, length // BLOCK // UNROLL, step, 0)
    dk_ref[...] = low(dk[...])
    dv_ref[...] = low(dv[...])


def attend_back(causal, plan, q, k, v, delta, grad, lse, qseg, kseg, after=()):
    rows, _, length = qseg.shape
    seg = pl.BlockSpec((1, 1, length), lambda i: (i, 0, 0))
    line = pl.BlockSpec((1, 8, length), lambda i: (i, 0, 0))
    return pl.pallas_call(
        functools.partial(back_kernel, causal), grid=(rows,),
        in_specs=[smem(), smem(), tiled(length, 512, q[1]), tiled(length, 512, k[1]), tiled(length, 512, v[1]), line,
                  tiled(length, 512), line, seg, seg] + [pl.BlockSpec(memory_space=pl.ANY)] * len(after),
        out_specs=[tiled(length, 512)] * 3, out_shape=[shape_of((rows * length, 512))] * 3,
        scratch_shapes=MASK_SCRATCH(length) + [pltpu.VMEM((length, 512), F32), pltpu.VMEM((length, 512), F32),
                                               pltpu.VMEM((4 * UNROLL, 128, BLOCK), F32)],
        compiler_params=params(40 if causal else 56), cost_estimate=cost(20), name="self_back" if causal else "cross_back",
    )(*plan, q[0], k[0], v[0], delta, grad, lse, qseg, kseg, *after)


def emit(outs, col, acc, index_ref, acc_col, width):
    half = outs[0].shape[0]
    for r in range(512 // UNIT):
        row = pl.multiple_of(index_ref[r] * UNIT, UNIT)
        outs[r // half][r % half, :, col:col + width] = low(acc[pl.ds(row, UNIT), acc_col:acc_col + width])


def halves(width):
    half = 512 // UNIT // 2
    return [fixed((half, UNIT, width), 0, 0, 0)] * 2, [shape_of((half, UNIT, width))] * 2


MID_TILE = 512
PARTS = 2
CHUNK = 1024


def mid_kernel(index_a, index_b, hid_ref, mix_ref, grad_ref, win_ref, gout_ref, wco_ref, vec_ref,
               out_ref, h2_ref, mg_ref, delta_ref, keep_ref, send_ref, co_ref, small_ref,
               wout, dwin, dwout, dwco, act, slope):
    step = pl.program_id(0)
    hidden_width = win_ref.shape[1]
    tokens = hid_ref.shape[0]

    @pl.when(step == 0)
    def _():
        for d in range(512 // UNIT):
            for b in range(4):
                wout[(4 * d + b) * UNIT:(4 * d + b + 1) * UNIT, :] = gout_ref[d * UNIT:(d + 1) * UNIT, 512 * b:512 * b + 512]
        small_ref[...] = jnp.zeros_like(small_ref)

    chunks = [slice(c, c + CHUNK) for c in range(0, hidden_width, CHUNK)]
    part = tokens // PARTS
    parts = [slice(i * part, i * part + part) for i in range(PARTS)]
    firsts = [norm(wide(hid_ref[t, :]))[0] * vec(vec_ref, S_GAIN) + vec(vec_ref, S_SHIFT) for t in parts]
    norms2 = [norm(first + mxu(mix_ref[t, :], wco_ref[...]) + vec(vec_ref, C_BIAS, 2)) for t, first in zip(parts, firsts)]
    seconds = [normed * vec(vec_ref, C_GAIN) + vec(vec_ref, C_SHIFT) for normed, _ in norms2]
    lows = [low(second) for second in seconds]
    norms3 = []
    for t, second, second_low in zip(parts, seconds, lows):
        hidden3 = second + vec(vec_ref, O_BIAS)
        for c in chunks:
            pre = mxu(second_low, win_ref[:, c]) + vec_ref[I_BIAS:I_BIAS + 1, c]
            sig = 0.5 + 0.5 * jnp.tanh(0.5 * pre)
            active = low(pre * sig)
            act[t, c] = active
            slope[t, c] = sig * (1.0 + pre * (1.0 - sig))
            hidden3 += mxu(active, wout[c, :])
        norms3.append(norm(hidden3))
    backs3 = []
    for t, (normed3, inverse3) in zip(parts, norms3):
        out_ref[t, :] = low(normed3 * vec(vec_ref, F_GAIN) + vec(vec_ref, F_SHIFT))
        grad = wide(grad_ref[t, :])
        backs3.append(norm_back(grad, normed3, inverse3, vec(vec_ref, F_GAIN)))
        small_ref[2:3, :512] += sum_rows(grad * normed3)
        small_ref[3:4, :512] += sum_rows(grad)
    b3s = [low(back3) for back3 in backs3]
    us = [[] for _ in chunks]
    grads2 = []
    for t, back3, b3 in zip(parts, backs3, b3s):
        grad2 = back3
        for n, c in enumerate(chunks):
            u = low(mxu(b3, wout[c, :], NT) * slope[t, c])
            us[n].append(u)
            grad2 += mxu(u, win_ref[:, c], NT)
        grads2.append(grad2)
    b2s = []
    for t, grad2, (normed2, inverse2) in zip(parts, grads2, norms2):
        h2 = norm_back(grad2, normed2, inverse2, vec(vec_ref, C_GAIN))
        b2 = low(h2)
        h2_ref[t, :] = b2
        b2s.append(b2)
        small_ref[4:5, :512] += sum_rows(grad2 * normed2)
        small_ref[5:6, :512] += sum_rows(grad2)
    second_low = jnp.concatenate(lows, axis=0)
    b3 = jnp.concatenate(b3s, axis=0)
    second_t = jnp.transpose(second_low)
    small_ref[1:2, :512] += sum_rows(b3)
    for n, c in enumerate(chunks):
        u = jnp.concatenate(us[n], axis=0)
        accumulate(dwin, (slice(None), c), mxu(second_t, u))
        accumulate(dwout, (c, slice(None)), mxu(act[:, c], b3, TN))
        small_ref[0:1, c] += sum_rows(u)
    b2 = jnp.concatenate(b2s, axis=0)
    small_ref[6:7, :512] += sum_rows(b2)
    accumulate(dwco, ..., mxu(jnp.transpose(mix_ref[...]), b2))
    mix_grad = low(mxu(b2, wco_ref[...], NT))
    mg_ref[...] = mix_grad
    delta_ref[0] = head_sums(mix_grad, mix_ref[...])

    @pl.when(step == pl.num_programs(0) - 1)
    def _():
        outs = keep_ref, send_ref
        emit(outs, 0, dwin, index_a, 0, hidden_width)
        half = keep_ref.shape[0]
        for r in range(512 // UNIT):
            for b in range(4):
                row = pl.multiple_of((index_b[r] * 4 + b) * UNIT, UNIT)
                outs[r // half][r % half, :, 2048 + 512 * b:2560 + 512 * b] = low(dwout[pl.ds(row, UNIT), :])
        co_ref[...] = dwco[...]


def middle(index_a, index_b, hid, mix, grad, rest, vectors, length):
    total = hid.shape[0]
    t = MID_TILE
    specs, shapes = halves(4096)
    return pl.pallas_call(
        mid_kernel, grid=(total // t,),
        in_specs=[smem(), smem(), tiled(t, 512), tiled(t, 512), tiled(t, 512),
                  fixed((512, 2048), 0, 0), fixed((512, 2048), 0, 1), fixed((512, 512), 0, 8), fixed((16, 2048), 0, 0)],
        out_specs=[tiled(t, 512)] * 3 + [rows_spec(t, length)] + specs + [fixed((512, 512), 0, 0), fixed((8, 2048), 0, 0)],
        out_shape=[shape_of((total, 512))] * 3 + [shape_of((total // length, 8, length), F32)] + shapes
        + [shape_of((512, 512), F32), shape_of((8, 2048), F32)],
        scratch_shapes=[pltpu.VMEM((2048, 512), BF), pltpu.VMEM((512, 2048), F32), pltpu.VMEM((2048, 512), F32),
                        pltpu.VMEM((512, 512), F32), pltpu.VMEM((t, 2048), BF), pltpu.VMEM((t, 2048), F32)],
        compiler_params=params(62), cost_estimate=cost(40), name="middle",
    )(index_a, index_b, hid, mix, grad, rest, rest, rest, vectors)


DENSE_TILE = 512
SELF_TILE = 1024


def cross_dense_kernel(index_a, index_b, cq_ref, ck_ref, cv_ref, mem_ref, hid_ref, h2_ref, mix_ref,
                       wq_ref, wo_ref, co_ref, vec_ref,
                       h1_ref, mg_ref, delta_ref, keep_ref, send_ref, small_ref, dq, dkv, do):
    step = pl.program_id(0)

    @pl.when(step == 0)
    def _():
        small_ref[...] = jnp.zeros_like(small_ref)

    cq, ck, cv = cq_ref[...], ck_ref[...], cv_ref[...]
    normed, inverse = norm(wide(hid_ref[...]))
    first = low(normed * vec(vec_ref, S_GAIN) + vec(vec_ref, S_SHIFT))
    grad1 = wide(h2_ref[...]) + mxu(cq, wq_ref[...], NT)
    h1 = norm_back(grad1, normed, inverse, vec(vec_ref, S_GAIN))
    b1 = low(h1)
    h1_ref[...] = b1
    mix_grad = low(mxu(b1, wo_ref[...], NT))
    mg_ref[...] = mix_grad
    delta_ref[0] = head_sums(mix_grad, mix_ref[...])
    accumulate(dq, ..., mxu(jnp.transpose(first), cq))
    mem_t = jnp.transpose(mem_ref[...])
    accumulate(dkv, (slice(None), slice(0, 512)), mxu(mem_t, ck))
    accumulate(dkv, (slice(None), slice(512, 1024)), mxu(mem_t, cv))
    accumulate(do, ..., mxu(jnp.transpose(mix_ref[...]), b1))
    small_ref[0:1, :] += sum_rows(cq)
    small_ref[1:2, :] += sum_rows(cv)
    small_ref[2:3, :] += sum_rows(grad1 * normed)
    small_ref[3:4, :] += sum_rows(grad1)
    small_ref[4:5, :] += sum_rows(b1)

    @pl.when(step == pl.num_programs(0) - 1)
    def _():
        outs = keep_ref, send_ref
        emit(outs, 0, dq, index_a, 0, 512)
        emit(outs, 512, co_ref, index_a, 0, 512)
        emit(outs, 1024, do, index_a, 0, 256)
        emit(outs, 1280, do, index_b, 256, 256)
        emit(outs, 1536, dkv, index_b, 0, 1024)


def cross_dense(index_a, index_b, grads, mem, hid, h2, mix, weights, dco, vectors, length):
    total = hid.shape[0]
    t = DENSE_TILE
    specs, shapes = halves(2560)
    return pl.pallas_call(
        cross_dense_kernel, grid=(total // t,),
        in_specs=[smem(), smem()] + [tiled(t, 512)] * 7
        + [fixed((512, 512), 0, 1), fixed((512, 512), 0, 0), fixed((512, 512), 0, 0), fixed((16, 2048), 0, 0)],
        out_specs=[tiled(t, 512)] * 2 + [rows_spec(t, length)] + specs + [fixed((8, 512), 0, 0)],
        out_shape=[shape_of((total, 512))] * 2 + [shape_of((total // length, 8, length), F32)] + shapes + [shape_of((8, 512), F32)],
        scratch_shapes=[pltpu.VMEM((512, 512), F32), pltpu.VMEM((512, 1024), F32), pltpu.VMEM((512, 512), F32)],
        compiler_params=params(40), cost_estimate=cost(12), name="cross_dense",
    )(index_a, index_b, *grads, mem, hid, h2, mix, weights, weights, dco, vectors)


def memory_kernel(ck_ref, cv_ref, w_ref, *refs):
    refs[-1][...] = low(mxu(ck_ref[...], w_ref[:, :512], NT) + mxu(cv_ref[...], w_ref[:, 512:], NT))


def memory_back(ck, cv, weights, after=()):
    total = ck.shape[0]
    t = 512
    return pl.pallas_call(
        memory_kernel, grid=(total // t,), in_specs=[tiled(t, 512)] * 2 + [fixed((512, 1024), 0, 1)]
        + [pl.BlockSpec(memory_space=pl.ANY)] * len(after),
        out_specs=tiled(t, 512), out_shape=shape_of((total, 512)), compiler_params=params(40), cost_estimate=cost(4), name="memory_grad",
    )(ck, cv, weights, *after)


VECTORS = (1536, 512, 512, 1536, 512, 512, 2048, 512, 512, 512)


def places(n, per, count, axis):
    shape = (1, n)
    at = wide(lax.broadcasted_iota(jnp.int32, shape, 1))
    owner = jnp.floor((at + 0.5) * (1.0 / per))
    return owner, at - owner * per


def one_hot(n, per):
    _, place = places(n, per, n // per, 1)
    return low(jnp.where(wide(lax.broadcasted_iota(jnp.int32, (128, n), 0)) == place, 1.0, 0.0))


def owned(n, per, count):
    owner, _ = places(n, per, count, 1)
    return wide(lax.broadcasted_iota(jnp.int32, (count, n), 0)) == owner


def self_grad_kernel(count, index_a, index_b, dq_ref, dk_ref, dv_ref, x_ref, mid_ref, small_ref, keep_ref, send_ref, lines_ref, dw, table):
    step = pl.program_id(0)

    @pl.when(step == 0)
    def _():
        lines_ref[...] = jnp.zeros_like(lines_ref)

    x_t = jnp.transpose(x_ref[...])
    accumulate(dw, (slice(None), slice(0, 512)), mxu(x_t, dq_ref[...]))
    accumulate(dw, (slice(None), slice(512, 1024)), mxu(x_t, dk_ref[...]))
    accumulate(dw, (slice(None), slice(1024, 1536)), mxu(x_t, dv_ref[...]))
    lines_ref[S_BIAS:S_BIAS + 1, :512] += sum_rows(dq_ref[...])
    lines_ref[S_BIAS:S_BIAS + 1, 512:1024] += sum_rows(dv_ref[...])

    @pl.when(step == pl.num_programs(0) - 1)
    def _():
        outs = keep_ref, send_ref
        emit(outs, 0, dw, index_a, 0, 768)
        emit(outs, 768, dw, index_b, 768, 768)
        for row, col, source, source_row in (
            (S_BIAS, 1024, small_ref, 4), (S_GAIN, 0, small_ref, 2), (S_SHIFT, 0, small_ref, 3),
            (C_BIAS, 0, small_ref, 0), (C_BIAS, 512, small_ref, 1), (C_BIAS, 1024, mid_ref, 6),
            (C_GAIN, 0, mid_ref, 4), (C_SHIFT, 0, mid_ref, 5),
            (O_BIAS, 0, mid_ref, 1), (F_GAIN, 0, mid_ref, 2), (F_SHIFT, 0, mid_ref, 3),
        ):
            lines_ref[row:row + 1, col:col + 512] = source[source_row:source_row + 1, :512]
        lines_ref[I_BIAS:I_BIAS + 1, :] = mid_ref[0:1, :]
        if count:
            table[...] = jnp.zeros_like(table)
            for n in (512, 1536, 2048):
                hot, mine = one_hot(n, n // count), owned(n, n // count, count)
                for j, size in enumerate(VECTORS):
                    if size == n:
                        line = jnp.broadcast_to(lines_ref[j:j + 1, :n], (count, n))
                        table[:, j, :] = mxu(low(jnp.where(mine, line, 0.0)), hot, NT)
            for r in range(count):
                outs[2 * r // count][r % (count // 2), :, 1536:] = low(table[index_b[r]])


def self_grad(count, index_a, index_b, grads, x, mid_small, small):
    total = x.shape[0]
    t = SELF_TILE
    specs, shapes = halves(1664)
    return pl.pallas_call(
        functools.partial(self_grad_kernel, count), grid=(total // t,),
        in_specs=[smem(), smem()] + [tiled(t, 512)] * 4 + [fixed((8, 2048), 0, 0), fixed((8, 512), 0, 0)],
        out_specs=specs + [fixed((16, 2048), 0, 0)],
        out_shape=shapes + [shape_of((16, 2048), F32)],
        scratch_shapes=[pltpu.VMEM((512, 1536), F32), pltpu.VMEM((max(count, 8), 16, 128), F32)],
        compiler_params=params(40), cost_estimate=cost(5), name="self_grad",
    )(index_a, index_b, *grads, x, mid_small, small)


def target_kernel(h1_ref, dq_ref, dk_ref, dv_ref, w_ref, *refs):
    out_ref = refs[-1]
    total = wide(h1_ref[...]) + mxu(dq_ref[...], w_ref[:, :512], NT)
    total += mxu(dk_ref[...], w_ref[:, 512:1024], NT)
    out_ref[...] = low(total + mxu(dv_ref[...], w_ref[:, 1024:], NT))


def target_grad(h1, grads, w, after=()):
    total = h1.shape[0]
    t = 512
    return pl.pallas_call(
        target_kernel, grid=(total // t,), in_specs=[tiled(t, 512)] * 4 + [fixed((512, 1536), 0, 0)]
        + [pl.BlockSpec(memory_space=pl.ANY)] * len(after),
        out_specs=tiled(t, 512), out_shape=shape_of((total, 512)), compiler_params=params(40), cost_estimate=cost(5), name="target_grad",
    )(h1, *grads, w, *after)


class Net:
    def __init__(self):
        self.wide = lax.axis_size("wide")
        self.narrow = lax.axis_size("narrow")
        self.count = self.wide * self.narrow
        self.wide_bits = self.wide.bit_length() - 1
        self.narrow_bits = self.narrow.bit_length() - 1
        self.bits = self.wide_bits + self.narrow_bits
        self.me = lax.axis_index("wide") * self.narrow + lax.axis_index("narrow")
        inner = list(range(self.narrow_bits))
        core, second = [self.narrow_bits], [self.narrow_bits + 1]
        far = list(range(self.narrow_bits + 2, self.bits))
        self.near = self.bits - len(far)
        self.orders = (core + second + inner + far, core + inner + second + far)

    def exchange(self, x, bit):
        if bit < self.narrow_bits:
            return lax.ppermute(x, "narrow", [(i, i ^ (1 << bit)) for i in range(self.narrow)])
        return self.across(x, 1 << bit)

    def across(self, x, mask):
        mask >>= self.narrow_bits
        return lax.ppermute(x, "wide", [(i, i ^ mask) for i in range(self.wide)])

    def far_masks(self, order):
        return [sum(((r >> s) & 1) << bit for s, bit in enumerate(order)) for r in range(1 << len(order))]

    def index(self, chain):
        order, n = self.orders[chain], self.bits
        mask = [sum(((r >> (n - 1 - s)) & 1) << bit for s, bit in enumerate(order)) for r in range(self.count)]
        return jnp.array(mask, jnp.int32) ^ self.me

    def gather_index(self, chain):
        order = self.orders[chain][::-1]
        mask = [sum(((r >> s) & 1) << bit for s, bit in enumerate(order)) for r in range(self.count)]
        return jnp.array(mask, jnp.int32) ^ self.me


def pack_kernel(*refs):
    vectors, (qkv, so, cq, ckv, co, fin, fout, packed_ref, cross_ref, rest_ref) = refs[:10], refs[10:20]
    lines, sem = refs[20:30], refs[30]
    moves = list(zip(vectors, lines))
    moves += [(qkv.at[:, :768], packed_ref.at[0, :, :768]), (qkv.at[:, 768:], packed_ref.at[0, :, 896:]), (fin, rest_ref.at[:, :2048])]
    moves += [(fout.at[UNIT * b:UNIT * b + UNIT, :], rest_ref.at[:, 2048 + 512 * b:2560 + 512 * b]) for b in range(4)]
    moves += [(co, rest_ref.at[:, 4096:]), (so, cross_ref.at[0, :, :512]),
              (cq, cross_ref.at[0, :, 512:1024]), (ckv, cross_ref.at[0, :, 1024:])]
    copies = [pltpu.make_async_copy(src, dst, sem.at[i]) for i, (src, dst) in enumerate(moves)]
    for copy in copies:
        copy.start()
    for copy in copies:
        copy.wait()
    rows = []
    for v in lines:
        line = wide(v[...])
        rows.append(jnp.concatenate([line, jnp.zeros((1, 128 - line.shape[1]), F32)], axis=1))
    rows.append(jnp.zeros((6, 128), F32))
    packed_ref[0, :, 768:896] = low(jnp.concatenate(rows, axis=0))


def unpack_kernel(count, index_a, index_b, *refs):
    n = (len(refs) - 3) // 2
    pieces_a, pieces_b, (w_ref, vec_ref, table) = refs[:n], refs[n:2 * n], refs[2 * n:]
    for pieces, index, col, width in ((pieces_a, index_a, 0, 768), (pieces_b, index_b, 768, 768)):
        r = 0
        for piece in pieces:
            for j in range(piece.shape[0]):
                owner = index[r]
                w_ref[pl.ds(pl.multiple_of(owner * UNIT, UNIT), UNIT), col:col + width] = piece[j, :, :width]
                if col == 0:
                    table[owner] = wide(piece[j, :, 768:896])
                r += 1
    vec_ref[...] = jnp.zeros_like(vec_ref)
    for n in (512, 1536, 2048):
        hot, mine = one_hot(n, n // count), owned(n, n // count, count)
        for j, size in enumerate(VECTORS):
            if size == n:
                spread = mxu(low(table[:, j, :]), hot)
                vec_ref[j:j + 1, :n] = jnp.sum(jnp.where(mine, spread, 0.0), axis=0, keepdims=True)


def place_kernel(index, *refs):
    pieces, w_ref = refs[:-1], refs[-1]
    r = 0
    for piece in pieces:
        for j in range(piece.shape[0]):
            row = pl.multiple_of(index[r] * UNIT, UNIT)
            w_ref[pl.ds(row, UNIT), :] = piece[j]
            r += 1


def gather_weights(net, small, big, early):
    qkv, so, cq, ckv, co, fin, fout = big
    if qkv.shape[0] % UNIT or net.bits < 5:
        small, big = lax.all_gather((small, big), AXES, axis=0, tiled=True) if net.count > 1 else (small, big)
        qkv, so, cq, ckv, co, fin, fout = big
        fout = fout.reshape(-1, 4, UNIT, 512).transpose(0, 2, 1, 3).reshape(512, 2048)
        rows = [jnp.pad(wide(v), (0, 2048 - v.shape[0])) for v in small]
        vectors = jnp.stack(rows + [jnp.zeros((2048,), F32)] * 6)
        return qkv, vectors, jnp.concatenate([fin, fout, co], axis=1), lambda x: (x, jnp.concatenate([so, cq, ckv], axis=1)), early
    packed, cross, rest = pl.pallas_call(
        pack_kernel, in_specs=[pl.BlockSpec(memory_space=pl.ANY)] * 17, out_specs=[vmem()] * 3,
        out_shape=[shape_of((1, UNIT, 1664)), shape_of((1, UNIT, 2048)), shape_of((UNIT, 4608))],
        scratch_shapes=[pltpu.VMEM((1, v.shape[0]), BF) for v in small] + [pltpu.SemaphoreType.DMA((21,))],
        compiler_params=params(60), cost_estimate=cost(2), name="pack",
    )(*[v[None] for v in small], *big)
    rest = lax.all_gather(rest, AXES, axis=0, tiled=True)
    orders = [order[::-1] for order in net.orders]
    far = net.bits - net.near
    masks = net.far_masks(orders[0][:far])[1:]
    everywhere = lambda x: jnp.concatenate([x] + [net.across(x, mask) for mask in masks], axis=0)
    packed = everywhere(packed)
    packed, cross, early = lax.optimization_barrier((packed, cross, early))
    cross = everywhere(cross)
    parts = [packed[:, :, :896], packed[:, :, 896:], cross]
    orders = orders + orders[:1]
    parts = [jnp.concatenate([x, net.exchange(x, order[far])], axis=0) for x, order in zip(parts, orders)]

    def spread(pieces, s):
        got = [[net.exchange(x, order[s]) for x in chain] for chain, order in zip(pieces, orders)]
        return [chain + more for chain, more in zip(pieces, got)]

    pieces = spread(spread([[x] for x in parts[:2]], far + 1), far + 2)
    later = spread([[x] for x in parts[2:]], far + 1)
    gather_index = [net.gather_index(0), net.gather_index(1)]

    def cross_weights(values):
        held, values = lax.optimization_barrier((later, values))
        held = spread(held, far + 2)
        return values, pl.pallas_call(
            place_kernel, in_specs=[smem()] + [vmem()] * len(held[0]), out_specs=vmem(),
            out_shape=pltpu.HBM((512, 2048), BF), compiler_params=params(32), cost_estimate=cost(2), name="place",
        )(gather_index[0], *held[0])

    w, vectors = pl.pallas_call(
        functools.partial(unpack_kernel, net.count), in_specs=[smem(), smem()] + [vmem()] * (len(pieces[0]) * 2), out_specs=[vmem()] * 2,
        out_shape=[shape_of((512, 1536)), shape_of((16, 2048), F32)],
        scratch_shapes=[pltpu.VMEM((net.count, 16, 128), F32)],
        compiler_params=params(40), cost_estimate=cost(2), name="unpack",
    )(*gather_index, *pieces[0], *pieces[1])
    return w, vectors, rest, cross_weights, early


class Reduction:
    def __init__(self, net, keep, send, cut, direct=True):
        self.net, self.cut, self.direct = net, cut, direct
        self.keep, self.send = [keep], [send]
        self.stage = 0
        self.sums = None

    def state(self):
        return tuple(self.send) if self.sums is None else ()

    def start(self):
        if self.sums is not None:
            return
        if self.stage < self.net.near or not self.direct:
            self.got = [self.net.exchange(x, order[self.stage]) for x, order in zip(self.send, self.net.orders)]
        else:
            far = self.net.far_masks(self.net.orders[0][:self.net.near - 1:-1])
            self.got = [self.net.across(x, mask) for x, mask in zip(self.send, far[1:])]

    def add(self):
        if self.sums is not None:
            return
        self.stage += 1
        if self.direct and self.stage > self.net.near:
            self.sums = sum((wide(got[0]) for got in self.got), self.keep[0][0])
            return
        sums = [wide(k) + wide(g) for k, g in zip(self.keep, self.got)]
        if self.stage == self.net.bits:
            self.sums = sums[0][0]
            return
        if self.stage == 1:
            sums = [sums[0][:, :, :self.cut], sums[0][:, :, self.cut:]]
        elif self.stage == self.net.near and not self.direct:
            sums = [jnp.concatenate(sums, axis=2)]
        elif self.stage == self.net.near:
            total = jnp.concatenate(sums, axis=2)
            self.keep = [total[:1]]
            self.send = [low(total[r:r + 1]) for r in range(1, total.shape[0])]
            return
        half = sums[0].shape[0] // 2
        self.keep = [low(s[:half]) for s in sums]
        self.send = [low(s[half:]) for s in sums]


def hold(groups, values):
    waiting = [group for group in groups if group.sums is None]
    if not waiting:
        return values
    got, values = lax.optimization_barrier(([group.got for group in waiting], values))
    for group, x in zip(waiting, got):
        group.got = x
    return values


def behind(groups, leader):
    for group in groups:
        (group.keep, group.send), _ = lax.optimization_barrier(((group.keep, group.send), leader.send))


def plan_self(seg, positions):
    rows, length = seg.shape
    starts = jnp.arange(0, length, BLOCK, dtype=jnp.int32)
    begin = starts[None, :] - positions[:, ::BLOCK]
    left = jnp.maximum(starts[None, :] + BLOCK - WINDOW - begin, 0)
    return jnp.zeros_like(begin), (left + WINDOW - 1) // WINDOW


def plan_cross(tseg, sseg):
    last = jnp.int32(1 << 20)
    tkey = jnp.where(tseg == 0, last, tseg)
    skey = jnp.where(sseg == 0, last, sseg)
    begin = jnp.sum(skey[:, None, :] < tkey[:, ::BLOCK, None], axis=2, dtype=jnp.int32)
    end = jnp.sum(skey[:, None, :] <= tkey[:, BLOCK - 1::BLOCK, None], axis=2, dtype=jnp.int32)
    first = (begin // 16) * 16
    return first, jnp.maximum((end - first + WINDOW - 1) // WINDOW - 1, 0)


def per_device(
    target, memory, out_grad, target_segments, source_segments, target_positions,
    self_qkv, self_out, cross_query, cross_kv, cross_out, ffn_in, ffn_out, *small,
):
    net = Net()
    rows, length = target_segments.shape
    fast = self_qkv.shape[0] % UNIT == 0 and net.bits >= 5
    self_plan = plan_self(target_segments, target_positions)
    cross_plan = plan_cross(target_segments, source_segments)
    tseg = wide(target_segments)[:, None, :]
    sseg = wide(source_segments)[:, None, :]
    index = (net.index(0), net.index(1)) if fast else (jnp.arange(512 // UNIT, dtype=jnp.int32),) * 2
    w_qkv, vectors, rest, cross_weights, early = gather_weights(
        net, small, (self_qkv, self_out, cross_query, cross_kv, cross_out, ffn_in, ffn_out), (self_plan, cross_plan, tseg, sseg, index))
    self_plan, cross_plan, tseg, sseg, (index_a, index_b) = early
    (qkv, self_mix, self_lse), cross_w = cross_weights(tuple(self_forward(self_plan, target, w_qkv, vectors, tseg)))
    hid, cq, pairs, cross_mix, cross_lse = cross_forward(cross_plan, target, self_mix, memory, cross_w, vectors, tseg, sseg)
    output, h2, cross_mg, cross_delta, ffn_keep, ffn_send, dco, mid_small = middle(index_a, index_b, hid, cross_mix, out_grad, rest, vectors, length)

    groups = [Reduction(net, ffn_keep, ffn_send, 2048)] if fast else []

    def backward(causal, plan, q, k, v, delta, grad, lse, kseg):
        tied = tuple(x for group in groups for x in group.state())
        for group in groups:
            group.start()
        out = hold(groups, attend_back(causal, plan, q, k, v, delta, grad, lse, tseg, kseg, tied))
        for group in groups:
            group.add()
        return out

    cross_grads = backward(False, cross_plan, (cq, 0), (pairs, 0), (pairs, 1), cross_delta, cross_mg, cross_lse, sseg)
    for group in groups:
        group.start()
    h1, self_mg, self_delta, cross_keep, cross_send, small_sums = cross_dense(
        index_a, index_b, cross_grads, memory, hid, h2, self_mix, cross_w, dco, vectors, length)
    h1, self_mg, self_delta, cross_keep, cross_send, small_sums = hold(
        groups, (h1, self_mg, self_delta, cross_keep, cross_send, small_sums))
    for group in groups:
        group.add()
    if fast:
        groups.append(Reduction(net, cross_keep, cross_send, 1280, direct=False))
    self_grads = backward(True, self_plan, (qkv, 0), (qkv, 1), (qkv, 2), self_delta, self_mg, self_lse, tseg)
    for group in groups:
        group.start()
    self_keep, self_send, lines = self_grad(net.count if fast else 0, index_a, index_b, self_grads, target, mid_small, small_sums)
    self_keep, self_send, lines = hold(groups, (self_keep, self_send, lines))
    for group in groups:
        group.add()

    if not fast:
        target_out = target_grad(h1, self_grads, w_qkv)
        memory_grad = memory_back(*cross_grads[1:], cross_w)
        total = lambda x: lax.psum_scatter(low(x), AXES, scatter_dimension=0, tiled=True).astype(F32) if net.count > 1 else wide(x)
        whole = lambda keep, send: jnp.concatenate([keep, send], axis=0).reshape(512, -1)
        d_self, d_cross, d_ffn = whole(self_keep, self_send), whole(cross_keep, cross_send), whole(ffn_keep, ffn_send)
        d_out = d_ffn[:, 2048:].reshape(-1, UNIT, 4, 512).transpose(0, 2, 1, 3).reshape(2048, 512)
        weights = (d_self[:, :1536], d_cross[:, 1024:1536],
                   d_cross[:, :512], d_cross[:, 1536:], d_cross[:, 512:1024], d_ffn[:, :2048], d_out)
        return (output, target_out, memory_grad, *[total(w) for w in weights], *[total(lines[j, :n]) for j, n in enumerate(VECTORS)])

    groups.append(Reduction(net, self_keep, self_send, 768))
    target_out = None
    while any(group.sums is None for group in groups):
        open_groups = [group for group in groups if group.sums is None]
        tied = tuple(x for group in open_groups for x in group.state())
        for group in open_groups:
            group.start()
        if groups[-1].stage == 1:
            target_out = target_grad(h1, self_grads, w_qkv, tied)
        if groups[-1].stage == 2:
            memory_grad = memory_back(*cross_grads[1:], cross_w, tied)
        for group in open_groups:
            group.add()
        behind([group for group in open_groups[:-1] if group.sums is None], open_groups[-1])
    d_ffn, d_cross, d_self = (group.sums for group in groups)
    vectors_out = [d_self[j, 1536:1536 + n // net.count] for j, n in enumerate(VECTORS)]
    return (
        output, target_out, memory_grad,
        d_self[:, :1536], d_cross[:, 1024:1536],
        d_cross[:, :512], d_cross[:, 1536:], d_cross[:, 512:1024],
        d_ffn[:, :2048], jnp.concatenate([d_ffn[:, 2048 + 512 * b:2560 + 512 * b] for b in range(4)], axis=0),
        *vectors_out,
    )


def solution(mesh):
    both = ("wide", "narrow")
    matrix, vector = P(both, None), P(both)
    return jax.shard_map(
        per_device, mesh=mesh,
        in_specs=(matrix,) * 13 + (vector,) * 10,
        out_specs=(matrix,) * 10 + (vector,) * 10,
        check_vma=False,
    )
```
